32 devices in a mesh: section: 4 (over x, core), dp: 8 (over z, y).
Axes of the slice: x: 2, y: 2, z: 4, core: 2. Of those that a mesh axis runs over, the one named last changes fastest.
Arguments:
- section_data: bfloat16 [4, 16, 768, 768], P('section', 'dp'), may hold values from -6 to 6
- text_len: int32 [2, 16], P(None, 'dp'), may hold values from 1 to 191, as said below
- patches: int32 [2, 16], P(None, 'dp'), may hold values from 196 to 576, as said below
- box_x: int32 [2, 16, 768], P(None, 'dp'), may hold values from 0 to 1000
- box_y: int32 [2, 16, 768], P(None, 'dp'), may hold values from 0 to 1000
- w_qkv: bfloat16 [4, 384, 2304], P('section'), may hold values from -0.21875 to 0.21875
- b_qv: bfloat16 [4, 768], P('section'), may hold values from -1.75 to 1.75
- w_out: bfloat16 [4, 384, 768], P('section'), may hold values from -0.875 to 0.875
- b_out: bfloat16 [4, 384], P('section'), may hold values from -1.75 to 1.75
- norm1_gain: bfloat16 [4, 384], P('section'), may hold values from 0.5 to 1.5
- norm1_bias: bfloat16 [4, 384], P('section'), may hold values from -1.75 to 1.75
- w_in: bfloat16 [4, 384, 3072], P('section'), may hold values from -0.21875 to 0.21875
- b_in: bfloat16 [4, 1536], P('section'), may hold values from -1.75 to 1.75
- w_back: bfloat16 [4, 1536, 768], P('section'), may hold values from -0.109375 to 0.109375
- b_back: bfloat16 [4, 384], P('section'), may hold values from -1.75 to 1.75
- norm2_gain: bfloat16 [4, 384], P('section'), may hold values from 0.5 to 1.5
- norm2_bias: bfloat16 [4, 384], P('section'), may hold values from -1.75 to 1.75
- rel_line: bfloat16 [4, 16, 12], P('section'), may hold values from -3 to 3
- rel_x: bfloat16 [4, 32, 12], P('section'), may hold values from -3 to 3
- rel_y: bfloat16 [4, 32, 12], P('section'), may hold values from -3 to 3
Outputs:
- section_result: bfloat16 [4, 16, 768, 768], P('section', 'dp')
- grad_w_qkv: float32 [4, 384, 2304], P('section')
- grad_b_qv: float32 [4, 768], P('section')
- grad_w_out: float32 [4, 384, 768], P('section')
- grad_b_out: float32 [4, 384], P('section')
- grad_norm1_gain: float32 [4, 384], P('section')
- grad_norm1_bias: float32 [4, 384], P('section')
- grad_w_in: float32 [4, 384, 3072], P('section')
- grad_b_in: float32 [4, 1536], P('section')
- grad_w_back: float32 [4, 1536, 768], P('section')
- grad_b_back: float32 [4, 384], P('section')
- grad_norm2_gain: float32 [4, 384], P('section')
- grad_norm2_bias: float32 [4, 384], P('section')
- grad_rel_line: float32 [4, 16, 12], P('section')
- grad_rel_x: float32 [4, 32, 12], P('section')
- grad_rel_y: float32 [4, 32, 12], P('section')
The draws below stay inside these ranges and needn't reach their ends.
Inputs may be any that keep to these rules, and one draw needn't show every extreme that they name: `text_len`: text tokens of a document; some document has exactly 191. `patches`: each value is 196 or 576; both occur.
All inputs are finite; a program needn't handle non-finite values.
Results may differ from the reference program's by a relative error of at most 0.028.
Values may be sent and summed in bfloat16 or wider, within the bound.
No kernel may reach another device: no remote copies, remote signals or barrier semaphores. Data moves between devices by JAX's collectives and lax.ppermute only.
A program may use at most 640 MiB of HBM per device.

```python
import math
import jax
import jax.numpy as jnp
from jax import lax

D = 768
HEADS = 12
FF = 3072
REL1 = 32
REL2 = 64
REACH1 = 128
REACH2 = 256
HEAD_DIM = 64
TEXT_MAX = 191
PATCH_SMALL = 196
PATCH_LARGE = 576
BOX_BINS = 1001
QBLOCKS = 1
ROWS = 768
NDOC = 16
N_SECTION = 4


def draw_text_len(key, part):
    key = jax.random.fold_in(key, 7)
    count_key, place_key = jax.random.split(key)
    counts = jax.random.randint(count_key, (2 * NDOC,), 1, TEXT_MAX + 1)
    placed = jax.random.randint(place_key, (), 0, 2 * NDOC)
    return counts.at[placed].set(TEXT_MAX).reshape(2, NDOC).astype(jnp.int32)


def draw_patches(key, part):
    key = jax.random.fold_in(key, 19)
    key_list = jax.random.split(key, 3)
    picked = jax.random.randint(key_list[0], (2 * NDOC,), 0, 2)
    counts = PATCH_SMALL + picked * (PATCH_LARGE - PATCH_SMALL)
    large_spot = jax.random.randint(key_list[1], (), 0, 2 * NDOC)
    small_spot = (large_spot + 1 + jax.random.randint(key_list[2], (), 0, 2 * NDOC - 1)) % (2 * NDOC)
    counts = counts.at[large_spot].set(PATCH_LARGE).at[small_spot].set(PATCH_SMALL)
    return counts.reshape(2, NDOC).astype(jnp.int32)


def place_ends(drawn, stream_key, low, top_value):
    index_at = [jax.random.randint(jax.random.fold_in(stream_key, axis), (), 0, length) for axis, length in enumerate(drawn.shape)]
    longest = drawn.shape.index(max(drawn.shape))
    beside = index_at[:longest] + [(index_at[longest] + 1) % drawn.shape[longest]] + index_at[longest + 1:]
    return drawn.at[tuple(index_at)].set(low).at[tuple(beside)].set(top_value)


def levels(own_key, extent, shards, smallest, high):
    loudness = 1.0
    for position, shards_of in shards:
        draws = jax.random.uniform(jax.random.fold_in(jax.random.fold_in(own_key, 6), position), (shards_of,), jnp.float32, smallest / len(shards), high / len(shards))
        loudness = loudness * jnp.repeat(jnp.exp(draws), extent[position] // shards_of).reshape((-1,) + (1,) * (len(extent) - 1 - position))
    return loudness


def bell_draw(stream_key, dims, deviation, most, cuts=(), kind=jnp.bfloat16):
    values = jax.random.normal(stream_key, dims, jnp.float32) * deviation
    if len(cuts) > 0:
        values = levels(stream_key, dims, cuts, -0.22, 0.18) * values
    return jnp.clip(values, min=-most, max=most).astype(kind)


def setup_inputs(seed: int = 0) -> dict:
    streams_of = jax.random.split(jax.random.key(seed), 21)
    section_data = bell_draw(streams_of[0], (N_SECTION, NDOC, ROWS, D), 1.0, 6.0, ((0, 4), (1, 8)))
    text_len = draw_text_len(jax.random.fold_in(streams_of[20], 71), 0)
    patches = draw_patches(jax.random.fold_in(streams_of[20], 71), 0)
    box_x = place_ends(jax.random.randint(streams_of[3], (2, NDOC, ROWS), 0, BOX_BINS), jax.random.fold_in(streams_of[3], 1), 0, BOX_BINS - 1).astype(jnp.int32)
    box_y = place_ends(jax.random.randint(streams_of[4], (2, NDOC, ROWS), 0, BOX_BINS), jax.random.fold_in(streams_of[4], 1), 0, BOX_BINS - 1).astype(jnp.int32)
    w_qkv = bell_draw(streams_of[5], (N_SECTION, D // 2, 3 * D), D ** -0.5, 0.21875, ((0, 4),))
    b_qv = bell_draw(streams_of[6], (N_SECTION, D), 0.3, 1.75, ((0, 4),))
    w_out = bell_draw(streams_of[7], (N_SECTION, D // 2, D), (D // 16) ** -0.5, 0.875, ((0, 4),))
    b_out = bell_draw(streams_of[8], (N_SECTION, D // 2), 0.3, 1.75, ((0, 4),))
    norm1_gain = jnp.clip(1.0 + 0.1 * jax.random.normal(streams_of[9], (N_SECTION, D // 2), jnp.float32), 0.5, 1.5).astype(jnp.bfloat16)
    norm1_bias = bell_draw(streams_of[10], (N_SECTION, D // 2), 0.3, 1.75, ((0, 4),))
    w_in = bell_draw(streams_of[11], (N_SECTION, D // 2, FF), D ** -0.5, 0.21875, ((0, 4),))
    b_in = bell_draw(streams_of[12], (N_SECTION, FF // 2), 0.3, 1.75, ((0, 4),))
    w_back = bell_draw(streams_of[13], (N_SECTION, FF // 2, D), FF ** -0.5, 0.109375, ((0, 4),))
    b_back = bell_draw(streams_of[14], (N_SECTION, D // 2), 0.3, 1.75, ((0, 4),))
    norm2_gain = jnp.clip(1.0 + 0.1 * jax.random.normal(streams_of[15], (N_SECTION, D // 2), jnp.float32), 0.5, 1.5).astype(jnp.bfloat16)
    norm2_bias = bell_draw(streams_of[16], (N_SECTION, D // 2), 0.3, 1.75, ((0, 4),))
    rel_line = bell_draw(streams_of[17], (N_SECTION, REL1 // 2, HEADS), 0.5, 3.0, ((0, 4),))
    rel_x = bell_draw(streams_of[18], (N_SECTION, REL2 // 2, HEADS), 0.5, 3.0, ((0, 4),))
    rel_y = bell_draw(streams_of[19], (N_SECTION, REL2 // 2, HEADS), 0.5, 3.0, ((0, 4),))
    return {"section_data": section_data, "text_len": text_len, "patches": patches, "box_x": box_x, "box_y": box_y, "w_qkv": w_qkv, "b_qv": b_qv, "w_out": w_out, "b_out": b_out, "norm1_gain": norm1_gain, "norm1_bias": norm1_bias, "w_in": w_in, "b_in": b_in, "w_back": w_back, "b_back": b_back, "norm2_gain": norm2_gain, "norm2_bias": norm2_bias, "rel_line": rel_line, "rel_x": rel_x, "rel_y": rel_y}


EPS = 1e-05
NEG = -1000000000.0
HIGH = lax.Precision.HIGHEST

@jax.custom_vjp
def low(v):
    return lax.optimization_barrier(v.astype(jnp.bfloat16)).astype(jnp.float32)

@jax.custom_vjp
def low_back(v):
    return v

def low_keep(v):
    return (low(v), None)

def low_pass(kept, grad):
    return (grad,)

def back_keep(v):
    return (v, None)

def back_low(kept, grad):
    return (low(grad),)
low.defvjp(low_keep, low_pass)
low_back.defvjp(back_keep, back_low)

def normalize(values):
    centered = values - lax.optimization_barrier(jnp.mean(values, axis=-1, keepdims=True))
    return centered * lax.rsqrt(lax.optimization_barrier(jnp.mean(centered * centered, axis=-1, keepdims=True)) + EPS)

def rel_bucket(delta, total, reach):
    half = total // 2
    exact = half // 2
    limits = [int(math.ceil(exact * (reach / exact) ** (step / (half - exact)) - 1e-09)) for step in range(1, half - exact)]
    dist = jnp.abs(delta)
    far = exact + jnp.zeros_like(dist)
    for limit in limits:
        far = far + (dist >= limit).astype(jnp.int32)
    return jnp.where(delta > 0, half, 0).astype(jnp.int32) + jnp.where(dist < exact, dist, far).astype(jnp.int32)

def buckets(start, block, box_x, box_y):
    query = start + jnp.arange(block, dtype=jnp.int32)
    keyrow = jnp.arange(ROWS, dtype=jnp.int32)
    line = rel_bucket(keyrow[None, :] - query[:, None], REL1, REACH1)
    near_x = lax.dynamic_slice_in_dim(box_x, start, block)
    near_y = lax.dynamic_slice_in_dim(box_y, start, block)
    across = rel_bucket(box_x[None, :] - near_x[:, None], REL2, REACH2)
    upward = rel_bucket(box_y[None, :] - near_y[:, None], REL2, REACH2)
    return (line, across, upward)

def attend_block(start, queries, keys_all, values, live, box_x, box_y, t_line, t_x, t_y):
    block = ROWS // QBLOCKS
    q_block = lax.dynamic_slice_in_dim(queries, start, block, 0)
    line, across, upward = buckets(start, block, box_x, box_y)
    bias = jnp.take(t_line.T, line, axis=1) + jnp.take(t_x.T, across, axis=1) + jnp.take(t_y.T, upward, axis=1)
    raw = jnp.einsum('ihd,jhd->hij', q_block, keys_all, precision=HIGH) * HEAD_DIM ** (-0.5) + bias
    masked = jnp.where(live[None, None, :], low_back(raw), NEG)
    peak = lax.optimization_barrier(jnp.max(masked, axis=-1, keepdims=True))
    expo = jnp.exp(masked - peak)
    weights = low(expo / lax.optimization_barrier(jnp.sum(expo, axis=-1, keepdims=True)))
    return jnp.einsum('hij,jhd->ihd', weights, values, precision=HIGH).reshape(block, D)

def layer_apply(inputs, params, live, box_x, box_y):
    w_qkv, b_qv, w_out, b_out, gain_one, shift_one, w_in, b_in, w_back, b_back, gain_two, shift_two, t_line, t_x, t_y = params
    bias_qkv = jnp.concatenate([b_qv[:D], jnp.zeros((D,), b_qv.dtype), b_qv[D:]])
    qkv = low(low_back(jnp.dot(inputs, w_qkv, precision=HIGH) + bias_qkv))
    queries = qkv[:, :D].reshape(ROWS, HEADS, HEAD_DIM)
    keys_all = qkv[:, D:2 * D].reshape(ROWS, HEADS, HEAD_DIM)
    values = qkv[:, 2 * D:].reshape(ROWS, HEADS, HEAD_DIM)
    starts = jnp.arange(QBLOCKS, dtype=jnp.int32) * (ROWS // QBLOCKS)
    checked = jax.checkpoint(attend_block)
    contexts = lax.map(lambda start: checked(start, queries, keys_all, values, live, box_x, box_y, t_line, t_x, t_y), starts)
    context = low(low_back(contexts.reshape(ROWS, D)))
    attended = low_back(jnp.dot(context, w_out, precision=HIGH) + b_out)
    hidden = normalize(inputs + attended) * gain_one + shift_one
    pre_gelu = low_back(jnp.dot(low(hidden), w_in, precision=HIGH) + b_in)
    activated = low(jax.nn.gelu(pre_gelu, approximate=False))
    ffn = low_back(jnp.dot(activated, w_back, precision=HIGH) + b_back)
    result = normalize(hidden + ffn) * gain_two + shift_two
    return jnp.where(live[:, None], result, 0.0)

def reference(section_data, text_len, patches, box_x, box_y, w_qkv, b_qv, w_out, b_out, norm1_gain, norm1_bias, w_in, b_in, w_back, b_back, norm2_gain, norm2_bias, rel_line, rel_x, rel_y):
    allparams = (w_qkv, b_qv, w_out, b_out, norm1_gain, norm1_bias, w_in, b_in, w_back, b_back, norm2_gain, norm2_bias, rel_line, rel_x, rel_y)
    first = tuple((jnp.concatenate([param[0], param[1]], 0).astype(jnp.float32) for param in allparams))
    second = tuple((jnp.concatenate([param[2], param[3]], 0).astype(jnp.float32) for param in allparams))
    sources = section_data[:2].reshape(-1, ROWS, D).astype(jnp.float32)
    cotangents = section_data[2:].reshape(-1, ROWS, D).astype(jnp.float32)
    rowindex = jnp.arange(ROWS, dtype=jnp.int32)

    def per_doc(totals, item):
        source, cotangent, text_count, patch_count, across, upward = item
        live = (rowindex < text_count) | (rowindex >= TEXT_MAX) & (rowindex < TEXT_MAX + 1 + patch_count)

        def whole(source, first, second):
            middle = low(low_back(layer_apply(source, first, live, across, upward)))
            return layer_apply(middle, second, live, across, upward)
        result, pull = jax.vjp(whole, source, first, second)
        grad_source, grad_first, grad_second = pull(cotangent)
        totals = jax.tree.map(jnp.add, totals, (grad_first, grad_second))
        return (totals, (result, grad_source))
    zero = jax.tree.map(jnp.zeros_like, (first, second))
    (grad_first, grad_second), (results, grad_sources) = lax.scan(per_doc, zero, (sources, cotangents, text_len.reshape(-1), patches.reshape(-1), box_x.reshape(-1, ROWS), box_y.reshape(-1, ROWS)))
    section_result = jnp.concatenate([grad_sources.reshape(2, -1, ROWS, D), results.reshape(2, -1, ROWS, D)], 0).astype(jnp.bfloat16)
    grads = []
    for one, two in zip(grad_first, grad_second):
        middle = one.shape[0] // 2
        grads.append(jnp.stack([one[:middle], one[middle:], two[:middle], two[middle:]], 0))
    return (section_result, grads[0], grads[1], grads[2], grads[3], grads[4], grads[5], grads[6], grads[7], grads[8], grads[9], grads[10], grads[11], grads[12], grads[13], grads[14])
```

```python
import functools
import math

import jax
import jax.numpy as jnp
import numpy as np
from jax import lax
from jax.experimental import pallas as pl
from jax.experimental.pallas import tpu as pltpu
from jax.sharding import PartitionSpec as P

REL1 = 32
REL2 = 64
REACH1 = 128
REACH2 = 256
HEAD_DIM = 64
TEXT_MAX = 191
EPS = 1e-05
NEG = -1000000000.0
ROOT_HALF = 0.7071067811865476
INV_ROOT_TAU = 0.3989422804014327

UNIT = 4096.0
LOG2E = 1.4426950408889634
TILE = 128
VMEM = 60 * 2**20

BF = jnp.bfloat16
F32 = jnp.float32
NT = (((1,), (1,)), ((), ()))
TN = (((0,), (0,)), ((), ()))


def dot(a, b):
    return jnp.dot(a, b, preferred_element_type=F32)


def dot_nt(a, b):
    return lax.dot_general(a, b, NT, preferred_element_type=F32)


def dot_tn(a, b):
    return lax.dot_general(a, b, TN, preferred_element_type=F32)


def bucket_limits(total, reach):
    half = total // 2
    exact = half // 2
    return [
        int(math.ceil(exact * (reach / exact) ** (step / (half - exact)) - 1e-09))
        for step in range(1, half - exact)
    ]


def rel_bucket(delta, total, reach):
    half = total // 2
    exact = half // 2
    dist = jnp.abs(delta)
    far = exact + jnp.zeros_like(dist)
    for limit in bucket_limits(total, reach):
        far = far + (dist >= limit).astype(jnp.int32)
    return jnp.where(delta > 0, half, 0).astype(jnp.int32) + jnp.where(dist < exact, dist, far)


def line_bucket_np(delta):
    half = REL1 // 2
    exact = half // 2
    dist = np.abs(delta)
    far = np.full(dist.shape, exact)
    for limit in bucket_limits(REL1, REACH1):
        far = far + (dist >= limit)
    return np.where(delta > 0, half, 0) + np.where(dist < exact, dist, far)


def line_rows():
    k = np.arange(2 * TILE)
    shift = np.where(k < TILE, k, k - 2 * TILE)
    return line_bucket_np(np.stack([TILE * (s - 2) - shift for s in range(5)]))


def line_tiles():
    r = np.arange(TILE)
    return line_bucket_np(np.stack([TILE * (s - 2) + r[:, None] - r[None, :] for s in range(5)]))


def lane_pick(table, index):
    dims = lax.GatherDimensionNumbers(
        offset_dims=(),
        collapsed_slice_dims=(1,),
        start_index_map=(1,),
        operand_batching_dims=(0,),
        start_indices_batching_dims=(0,),
    )
    return lax.gather(
        table,
        index[..., None],
        dims,
        slice_sizes=(1, 1),
        mode=lax.GatherScatterMode.PROMISE_IN_BOUNDS,
    )


def attend_kernel(
    k_ref,
    qt_ref,
    vt_ref,
    mask_ref,
    x_ref,
    y_ref,
    tab_ref,
    line_ref,
    p_ref,
    c_ref,
    exact_ref,
    inv_ref,
    kaug,
    qaug,
    strip,
    sa,
    sb,
):
    rows = k_ref.shape[0]
    chunk = 2 * TILE
    step = 32
    lane = lax.broadcasted_iota(jnp.int32, (rows, TILE), 1)
    keys = k_ref[...].astype(F32) * (UNIT / 8.0)
    kaug[0, :, :TILE] = jnp.where(lane < HEAD_DIM, keys, 0.0).astype(BF)
    kaug[1, :, :TILE] = jnp.where(lane < HEAD_DIM, 0.0, keys).astype(BF)
    kaug[0, :, TILE:] = mask_ref[...]
    kaug[1, :, TILE:] = mask_ref[...]
    qaug[:TILE, :] = qt_ref[...]
    qaug[TILE:, :] = jnp.ones((TILE, rows), BF)
    for head in range(2):
        for s in range(5):
            wide = jnp.broadcast_to(line_ref[head, s : s + 1, :], (TILE, 2 * TILE))
            strip[head, s] = pltpu.roll(wide, 0, axis=1, stride=1, stride_axis=0)[:, :TILE]
    table = jnp.concatenate([tab_ref[0]] * (step // 8), axis=0)
    ones = jnp.ones((16, rows), BF)
    for t in range(rows // chunk):
        cols = slice(t * chunk, (t + 1) * chunk)
        sa[...] = dot(kaug[0], qaug[:, cols])
        sb[...] = dot(kaug[1], qaug[:, cols])

        def score(n, peaks):
            peak_a, peak_b = peaks
            at = pl.ds(pl.multiple_of(n * step, step), step)
            sub = pl.ds(pl.multiple_of((n % (TILE // step)) * step, step), step)
            out_a, out_b = [], []
            for part in range(2):
                lanes = slice(part * TILE, (part + 1) * TILE)
                wide = slice(t * chunk + part * TILE, t * chunk + (part + 1) * TILE)
                both = lane_pick(table, x_ref[at, wide]) + lane_pick(table, y_ref[at, wide])
                off = jnp.clip(n // (TILE // step) - (2 * t + part), -2, 2) + 2
                one = sa[at, lanes] + strip[0, off, sub, :] + (both >> 16).astype(F32)
                two = sb[at, lanes] + strip[1, off, sub, :] + (both & 0xFFFF).astype(F32)
                sa[at, lanes] = one
                sb[at, lanes] = two
                out_a.append(one)
                out_b.append(two)
            return (
                jnp.maximum(peak_a, jnp.concatenate(out_a, axis=1)),
                jnp.maximum(peak_b, jnp.concatenate(out_b, axis=1)),
            )

        low = jnp.full((step, chunk), -3e38, F32)
        peak_a, peak_b = lax.fori_loop(0, rows // step, score, (low, low))
        peak_a = jnp.max(peak_a, axis=0, keepdims=True)
        peak_b = jnp.max(peak_b, axis=0, keepdims=True)

        def weigh(n, carry):
            at = pl.ds(pl.multiple_of(n * step, step), step)
            p_ref[0, at, cols] = jnp.exp2((sa[at, :] - peak_a) * (LOG2E / UNIT)).astype(BF)
            p_ref[1, at, cols] = jnp.exp2((sb[at, :] - peak_b) * (LOG2E / UNIT)).astype(BF)
            return carry

        lax.fori_loop(0, rows // step, weigh, 0)
        for head in range(2):
            vals = jnp.concatenate([vt_ref[head * HEAD_DIM : (head + 1) * HEAD_DIM, :], ones], axis=0)
            mixed = dot(vals, p_ref[head, :, cols])
            inv = 1.0 / mixed[HEAD_DIM : HEAD_DIM + 1, :]
            mixed = mixed[:HEAD_DIM, :] * inv
            exact_ref[head * HEAD_DIM : (head + 1) * HEAD_DIM, cols] = mixed
            c_ref[head * HEAD_DIM : (head + 1) * HEAD_DIM, cols] = mixed.astype(BF)
            inv_ref[0, head : head + 1, cols] = inv


def attend(qkv, qkv_t, mask, across, upward, tabs, lines):
    rows = qkv.shape[0]
    width = qkv.shape[1] // 3
    pairs = width // TILE
    whole = lambda p: (0, 0)
    return pl.pallas_call(
        attend_kernel,
        grid=(pairs,),
        in_specs=[
            pl.BlockSpec((rows, TILE), lambda p: (0, pairs + p)),
            pl.BlockSpec((TILE, rows), lambda p: (p, 0)),
            pl.BlockSpec((TILE, rows), lambda p: (2 * pairs + p, 0)),
            pl.BlockSpec((rows, TILE), whole),
            pl.BlockSpec((rows, rows), whole),
            pl.BlockSpec((rows, rows), whole),
            pl.BlockSpec((1, 8, TILE), lambda p: (p, 0, 0)),
            pl.BlockSpec((2, 8, 2 * TILE), lambda p: (p, 0, 0)),
        ],
        out_specs=[
            pl.BlockSpec((2, rows, rows), lambda p: (p, 0, 0)),
            pl.BlockSpec((TILE, rows), lambda p: (p, 0)),
            pl.BlockSpec((TILE, rows), lambda p: (p, 0)),
            pl.BlockSpec((1, 8, rows), lambda p: (p, 0, 0)),
        ],
        out_shape=[
            jax.ShapeDtypeStruct((2 * pairs, rows, rows), BF),
            jax.ShapeDtypeStruct((width, rows), BF),
            jax.ShapeDtypeStruct((width, rows), F32),
            jax.ShapeDtypeStruct((pairs, 8, rows), F32),
        ],
        scratch_shapes=[
            pltpu.VMEM((2, rows, 2 * TILE), BF),
            pltpu.VMEM((2 * TILE, rows), BF),
            pltpu.VMEM((2, 5, TILE, TILE), F32),
            pltpu.VMEM((rows, 2 * TILE), F32),
            pltpu.VMEM((rows, 2 * TILE), F32),
        ],
        compiler_params=pltpu.CompilerParams(vmem_limit_bytes=VMEM),
        name="attend",
    )(qkv, qkv_t, qkv_t, mask, across, upward, tabs, lines)


def attend_back_kernel(
    p_ref,
    q_ref,
    kt_ref,
    v_ref,
    dc_ref,
    dct_ref,
    ct_ref,
    ds_ref,
    d_ref,
    line_ref,
    dp,
    dqt,
):
    rows = q_ref.shape[0]
    block = 2 * TILE
    step = 32
    line_ref[...] = jnp.zeros_like(line_ref)
    product = dct_ref[...].astype(F32) * ct_ref[...]
    lane = lax.broadcasted_iota(jnp.int32, (block, TILE), 1)
    for n in range(rows // block):
        at = slice(n * block, (n + 1) * block)
        vals = v_ref[at, :]
        out_k, out_v = [], []
        for head in range(2):
            mine = slice(head * HEAD_DIM, (head + 1) * HEAD_DIM)
            delta = jnp.sum(product[mine, :], axis=0, keepdims=True)
            own = (lane < HEAD_DIM) if head == 0 else (lane >= HEAD_DIM)
            dp[head] = dot(jnp.where(own, vals, jnp.zeros_like(vals)), dct_ref[...])

            def score(m, carry):
                inner = pl.ds(pl.multiple_of(m * step, step), step)
                outer = pl.ds(pl.multiple_of(n * block + m * step, step), step)
                sub = pl.ds(pl.multiple_of((m % (TILE // step)) * step, step), step)
                for part in range(rows // TILE):
                    lanes = slice(part * TILE, (part + 1) * TILE)
                    weights = p_ref[head, outer, lanes].astype(F32)
                    grad = weights * (dp[head, inner, lanes] - delta[:, lanes])
                    ds_ref[head, outer, lanes] = grad.astype(BF)
                    off = jnp.clip(2 * n + m // (TILE // step) - part, -2, 2) + 2
                    line_ref[head, off, sub, :] += grad
                return carry

            lax.fori_loop(0, block // step, score, 0)
            grad_low = ds_ref[head, at, :]
            out_k.append(dot(grad_low, q_ref[...]))
            out_v.append(dot(p_ref[head, at, :], dc_ref[...]))
            part_q = dot(kt_ref[mine, at], grad_low)
            if n == 0:
                dqt[mine, :] = part_q
            else:
                dqt[mine, :] += part_q
        d_ref[1, at, :] = (jnp.where(lane < HEAD_DIM, out_k[0], out_k[1]) * 0.125).astype(BF)
        d_ref[2, at, :] = jnp.where(lane < HEAD_DIM, out_v[0], out_v[1]).astype(BF)
    d_ref[0] = (jnp.transpose(dqt[...]) * 0.125).astype(BF)


def attend_back(weights, qkv, qkv_t, dc, dct, ct):
    rows = qkv.shape[0]
    width = qkv.shape[1] // 3
    pairs = width // TILE
    return pl.pallas_call(
        attend_back_kernel,
        grid=(pairs,),
        in_specs=[
            pl.BlockSpec((2, rows, rows), lambda p: (p, 0, 0)),
            pl.BlockSpec((rows, TILE), lambda p: (0, p)),
            pl.BlockSpec((TILE, rows), lambda p: (pairs + p, 0)),
            pl.BlockSpec((rows, TILE), lambda p: (0, 2 * pairs + p)),
            pl.BlockSpec((rows, TILE), lambda p: (0, p)),
            pl.BlockSpec((TILE, rows), lambda p: (p, 0)),
            pl.BlockSpec((TILE, rows), lambda p: (p, 0)),
        ],
        out_specs=[
            pl.BlockSpec((2, rows, rows), lambda p: (p, 0, 0)),
            pl.BlockSpec((3, rows, TILE), lambda p: (0, 0, p)),
            pl.BlockSpec((2, 5, TILE, TILE), lambda p: (p, 0, 0, 0)),
        ],
        out_shape=[
            jax.ShapeDtypeStruct((2 * pairs, rows, rows), BF),
            jax.ShapeDtypeStruct((3, rows, width), BF),
            jax.ShapeDtypeStruct((2 * pairs, 5, TILE, TILE), F32),
        ],
        scratch_shapes=[
            pltpu.VMEM((2, 2 * TILE, rows), F32),
            pltpu.VMEM((TILE, rows), F32),
        ],
        compiler_params=pltpu.CompilerParams(vmem_limit_bytes=VMEM),
        name="attend_back",
    )(weights, qkv, qkv_t, qkv, dc, dct, ct)


def table_kernel(ds_ref, x_ref, y_ref, o_ref, scr):
    heads, block, rows = ds_ref.shape
    parts = rows // TILE

    @pl.when(pl.program_id(0) == 0)
    def start():
        o_ref[...] = jnp.zeros_like(o_ref)
        scr[...] = jnp.zeros_like(scr)

    for head in range(heads):
        wide = ds_ref[head].astype(F32)
        for c in range(parts):
            scr[c, head * block : (head + 1) * block, :] = wide[:, c * TILE : (c + 1) * TILE]
    index = lax.broadcasted_iota(jnp.int32, (REL2, rows), 0)
    total = o_ref[...]
    for j in range(block):
        grads = jnp.concatenate(
            [scr[c, pl.ds(j, 16, stride=block), :] for c in range(parts)], axis=1
        ).astype(BF)
        row_x = jnp.broadcast_to(x_ref[j : j + 1, :], (REL2, rows))
        row_y = jnp.broadcast_to(y_ref[j : j + 1, :], (REL2, rows))
        hot = jnp.concatenate(
            [
                jnp.where(row_x == index, 1.0, 0.0).astype(BF),
                jnp.where(row_y == index + REL2, 1.0, 0.0).astype(BF),
            ],
            axis=0,
        )
        total = total + dot_nt(grads, hot)
    o_ref[...] = total


def table_sums(ds, across, upward):
    heads, rows, _ = ds.shape
    block = 16
    return pl.pallas_call(
        table_kernel,
        grid=(rows // block,),
        in_specs=[
            pl.BlockSpec((heads, block, rows), lambda g: (0, g, 0)),
            pl.BlockSpec((block, rows), lambda g: (g, 0)),
            pl.BlockSpec((block, rows), lambda g: (g, 0)),
        ],
        out_specs=pl.BlockSpec((16, 2 * REL2), lambda g: (0, 0)),
        out_shape=jax.ShapeDtypeStruct((16, 2 * REL2), F32),
        scratch_shapes=[pltpu.VMEM((rows // TILE, 16 * block, TILE), F32)],
        compiler_params=pltpu.CompilerParams(vmem_limit_bytes=VMEM),
        name="table_sums",
    )(ds, across, upward)


def nothing_kernel(*refs):
    pass


def unset(like):
    return jax.tree.map(
        lambda a: pl.pallas_call(
            nothing_kernel,
            out_specs=pl.BlockSpec(memory_space=pl.ANY),
            out_shape=jax.ShapeDtypeStruct(a.shape, a.dtype),
            name="unset",
        )(),
        like,
    )


def passed_along(array, axis, by):
    peers = lax.axis_size(axis)
    pairs = [(i, i + by) for i in range(peers) if 0 <= i + by < peers]
    return lax.ppermute(array, axis, pairs)


def partner(value):
    pairs = [(source, source ^ 1) for source in range(lax.axis_size("section"))]
    return lax.ppermute(value, "section", pairs)


def normalize(values):
    centered = values - jnp.mean(values, axis=-1, keepdims=True)
    scale = lax.rsqrt(jnp.mean(centered * centered, axis=-1, keepdims=True) + EPS)
    return (centered * scale, scale)


def norm_back(grad_norm, normed, scale):
    return scale * (
        grad_norm
        - jnp.mean(grad_norm, axis=-1, keepdims=True)
        - normed * jnp.mean(grad_norm * normed, axis=-1, keepdims=True)
    )


def doc_tables(text_len, patches, box_x, box_y):
    rows = box_x.shape[0]
    index = jnp.arange(rows, dtype=jnp.int32)
    live = (index < text_len) | ((index >= TEXT_MAX) & (index < TEXT_MAX + 1 + patches))
    across = rel_bucket(box_x[:, None] - box_x[None, :], REL2, REACH2)
    upward = rel_bucket(box_y[:, None] - box_y[None, :], REL2, REACH2) + REL2
    first = jnp.arange(TILE) == 0
    mask = jnp.where(first[None, :] & ~live[:, None], NEG * UNIT, 0.0).astype(BF)
    return (live, across, upward, mask)


def score_tables(t_line, t_x, t_y):
    heads = t_line.shape[1]
    both = jnp.concatenate([t_x, t_y], axis=0).astype(F32)
    fixed = jnp.round(both * UNIT).astype(jnp.int32).T.reshape(heads // 2, 2, 2 * REL2)
    packed = fixed[:, 0] * 65536 + fixed[:, 1] + 16384
    tabs = jnp.broadcast_to(packed[:, None, :], (heads // 2, 8, 2 * REL2))
    chosen = line_rows().reshape(-1)
    hot = jnp.asarray(chosen[None, :] == np.arange(REL1)[:, None], BF)
    lines = dot_tn(t_line, hot).reshape(heads, 5, 2 * TILE) * UNIT
    odd = (jnp.arange(heads) % 2)[:, None, None].astype(F32)
    lines = jnp.pad(lines - odd * 32768.0, ((0, 0), (0, 3), (0, 0)))
    return (tabs, lines)


def forward_doc(x, meta, params, tables):
    live, across, upward, mask = meta
    w_qkv, b_qv, w_out, b_out, gain1, shift1, w_in, b_in, w_back, b_back, gain2, shift2 = params
    width = x.shape[1]
    bias = jnp.concatenate([b_qv[:width], jnp.zeros((width,), F32), b_qv[width:]])
    qkv = (dot(x, w_qkv) + bias).astype(BF)
    qkv_t = (lax.dot_general(w_qkv, x, (((0,), (1,)), ((), ())), preferred_element_type=F32) + bias[:, None]).astype(BF)
    weights, ct, exact, inv = attend(qkv, qkv_t, mask, across, upward, *tables)
    attended = dot_tn(ct, w_out) + b_out
    n1, rstd1 = normalize(x.astype(F32) + attended)
    hidden = n1 * gain1 + shift1
    hidden_low = hidden.astype(BF)
    u = dot(hidden_low, w_in) + b_in
    phi = 0.5 * (1.0 + lax.erf(u * ROOT_HALF))
    tg = (u * phi).astype(BF)
    slope = (phi + u * jnp.exp(-0.5 * u * u) * INV_ROOT_TAU).astype(BF)
    n2, rstd2 = normalize(hidden + dot(tg, w_back) + b_back)
    y = jnp.where(live[:, None], n2 * gain2 + shift2, 0.0).astype(BF)
    return dict(
        x=x, qkv=qkv, qkv_t=qkv_t, weights=weights, ct=ct, exact=exact, inv=inv, n1=n1, rstd1=rstd1,
        hidden=hidden_low, tg=tg, slope=slope, n2=n2, rstd2=rstd2, y=y,
    )


def backward_doc(dy, meta, params, kept):
    live = meta[0]
    w_qkv, b_qv, w_out, b_out, gain1, shift1, w_in, b_in, w_back, b_back, gain2, shift2 = params
    width = dy.shape[1]
    dym = jnp.where(live[:, None], dy.astype(F32), 0.0)
    g_gain2 = jnp.sum(dym * kept["n2"], axis=0)
    g_shift2 = jnp.sum(dym, axis=0)
    dr2 = norm_back(dym * gain2, kept["n2"], kept["rstd2"])
    df = dr2.astype(BF)
    g_b_back = jnp.sum(df.astype(F32), axis=0)
    du = (dot_nt(df, w_back) * kept["slope"].astype(F32)).astype(BF)
    g_b_in = jnp.sum(du.astype(F32), axis=0)
    dh1 = dr2 + dot_nt(du, w_in)
    g_gain1 = jnp.sum(dh1 * kept["n1"], axis=0)
    g_shift1 = jnp.sum(dh1, axis=0)
    dr1 = norm_back(dh1 * gain1, kept["n1"], kept["rstd1"])
    da = dr1.astype(BF)
    g_b_out = jnp.sum(da.astype(F32), axis=0)
    inv = kept["inv"][:, :2, :].reshape(-1, dy.shape[0])
    inv = jnp.repeat(inv, HEAD_DIM, axis=0)
    dct = (dot_nt(w_out, da).astype(BF).astype(F32) * inv).astype(BF)
    dc = (dot_nt(da, w_out).astype(BF).astype(F32) * inv.T).astype(BF)
    ds, dqkv, line = attend_back(kept["weights"], kept["qkv"], kept["qkv_t"], dc, dct, kept["exact"])
    g_b_qv = jnp.sum(dqkv[::2].astype(F32), axis=1).reshape(-1)
    dx = dr1
    for part in range(3):
        dx = dx + dot_nt(dqkv[part], w_qkv[:, part * width : (part + 1) * width])
    return dict(
        dx=dx.astype(BF), ds=ds, dqkv=dqkv, df=df, du=du, da=da, line=line,
        small=(g_b_qv, g_b_out, g_gain1, g_shift1, g_b_in, g_b_back, g_gain2, g_shift2),
    )


def weight_grads(docs):
    def total(pick):
        return sum(pick(kept, back) for kept, back in docs)

    g_back = total(lambda k, b: dot_tn(k["tg"], b["df"]))
    g_in = total(lambda k, b: dot_tn(k["hidden"], b["du"]))
    g_out = total(lambda k, b: dot(k["ct"], b["da"]))
    g_qkv = total(
        lambda k, b: lax.dot_general(
            k["x"], b["dqkv"], (((0,), (1,)), ((), ())), preferred_element_type=F32
        )
    )
    return (g_qkv.reshape(g_qkv.shape[0], -1), g_out, g_in, g_back)


def small_grads(docs):
    return jax.tree.map(lambda *parts: sum(parts), *[(b["small"], b["line"]) for _, b in docs])


def local(
    section_data,
    text_len,
    patches,
    box_x,
    box_y,
    w_qkv,
    b_qv,
    w_out,
    b_out,
    norm1_gain,
    norm1_bias,
    w_in,
    b_in,
    w_back,
    b_back,
    norm2_gain,
    norm2_bias,
    rel_line,
    rel_x,
    rel_y,
):
    index = lax.axis_index("section")
    half = index % 2
    later = index >= 2
    heads = rel_line.shape[2]

    def whole(mine):
        theirs = partner(mine)
        return jnp.where(
            half == 0,
            jnp.concatenate([mine, theirs], 0),
            jnp.concatenate([theirs, mine], 0),
        )

    small_params = (b_qv, b_out, norm1_gain, norm1_bias, b_in, b_back, norm2_gain, norm2_bias)
    sizes = [a.shape[1] for a in small_params]
    packed = jnp.concatenate([a[0] for a in small_params] + [a[0].reshape(-1) for a in (rel_line, rel_x, rel_y)])
    pair = whole(packed[None])
    fulls = []
    start = 0
    for size in sizes:
        fulls.append(pair[:, start : start + size].reshape(-1).astype(F32))
        start += size
    tabs = []
    for table in (rel_line, rel_x, rel_y):
        size = table.shape[1] * heads
        tabs.append(pair[:, start : start + size].reshape(-1, heads))
        start += size
    wide_qkv = whole(w_qkv[0])
    wide_out = whole(w_out[0])
    wide_in = whole(w_in[0])
    wide_back = whole(w_back[0])
    params = (
        wide_qkv, fulls[0], wide_out, fulls[1], fulls[2], fulls[3],
        wide_in, fulls[4], wide_back, fulls[5], fulls[6], fulls[7],
    )
    tables = score_tables(*tabs)

    def pick(table):
        return jnp.where(half == 0, table[0], table[1])

    mine = [pick(t) for t in (text_len, patches, box_x, box_y)]
    metas = [doc_tables(*[t[n] for t in mine]) for n in range(2)]
    entries = section_data[0]

    def choose(when_later, else_first):
        return jax.tree.map(lambda a, b: jnp.where(later, a, b), when_later, else_first)

    def forward(x, meta):
        return forward_doc(x, meta, params, tables)

    def backward(dy, meta, kept):
        return backward_doc(dy, meta, params, kept)

    f0 = forward(entries[0], metas[0])
    y0 = passed_along(f0["y"], "section", 2)
    f1 = forward(jnp.where(later, y0, entries[1]), choose(metas[0], metas[1]))
    y1 = passed_along(f1["y"], "section", 2)
    b2 = backward(entries[0], choose(metas[0], metas[1]), f1)
    dx0 = passed_along(b2["dx"], "section", -2)
    f_like = jax.eval_shape(lambda: f1)
    b_like = jax.eval_shape(lambda: b2)
    f3, b3 = lax.cond(
        later,
        lambda: (forward(y1, metas[1]), unset(b_like)),
        lambda: (unset(f_like), backward(dx0, metas[0], f0)),
    )
    table_like = jax.ShapeDtypeStruct((16, 2 * REL2), F32)
    b4, t4 = lax.cond(
        later,
        lambda: (backward(entries[1], metas[1], f3), unset(table_like)),
        lambda: (unset(b_like), table_sums(b3["ds"], *metas[0][1:3])),
    )
    dx1 = passed_along(b4["dx"], "section", -2)
    b5, t5 = lax.cond(
        later,
        lambda: (unset(b_like), table_sums(b2["ds"], *metas[0][1:3])),
        lambda: (backward(dx1, metas[1], f1), unset(table_like)),
    )
    first_docs = [(f0, b3), (f1, b5)]
    later_docs = [(f1, b2), (f3, b4)]
    big = lax.cond(later, lambda: weight_grads(later_docs), lambda: weight_grads(first_docs))
    small, line = choose(small_grads(later_docs), small_grads(first_docs))
    t6 = lax.cond(
        later,
        lambda: table_sums(b4["ds"], *metas[1][1:3]),
        lambda: table_sums(b5["ds"], *metas[1][1:3]),
    )
    table = jnp.where(later, t5, t4) + t6
    tiles = line_tiles().reshape(-1)
    hot = jnp.asarray(tiles[:, None] == np.arange(REL1)[None, :], BF)
    g_line = lax.dot_general(
        line.reshape(heads, -1).astype(BF), hot, (((1,), (0,)), ((), ())), preferred_element_type=F32
    ).T
    g_x = table[:heads, :REL2].T
    g_y = table[:heads, REL2:].T

    def keep_half(full):
        rows = full.shape[0] // 2
        own = lax.dynamic_slice_in_dim(full, half * rows, rows, 0)
        other = lax.dynamic_slice_in_dim(full, (1 - half) * rows, rows, 0)
        return own + partner(other.astype(BF)).astype(F32)

    wide = [keep_half(g) for g in big]
    vectors = list(small)
    pieces = [v.reshape(2, -1) for v in vectors]
    pieces += [g.reshape(2, -1) for g in (g_line, g_x, g_y)]
    slim = keep_half(jnp.concatenate(pieces, axis=1))[0]
    slim, wide = lax.psum((slim, tuple(wide)), "dp")
    outs = []
    start = 0
    for size in sizes:
        outs.append(slim[start : start + size][None])
        start += size
    for table_arg in (rel_line, rel_x, rel_y):
        size = table_arg.shape[1] * heads
        outs.append(slim[start : start + size].reshape(table_arg.shape))
        start += size
    result = jnp.where(
        later,
        jnp.stack([f1["y"], f3["y"]]),
        jnp.stack([b3["dx"], b5["dx"]]),
    )[None]
    g_b_qv, g_b_out, g_g1, g_s1, g_b_in, g_b_back, g_g2, g_s2, g_l, g_rx, g_ry = outs
    return (
        result, wide[0][None], g_b_qv, wide[1][None], g_b_out, g_g1, g_s1,
        wide[2][None], g_b_in, wide[3][None], g_b_back, g_g2, g_s2, g_l, g_rx, g_ry,
    )


def solution(mesh):
    matrix = P("section", None, None)
    vector = P("section", None)
    weights = (
        matrix, vector, matrix, vector, vector, vector, matrix, vector, matrix,
        vector, vector, vector, matrix, matrix, matrix,
    )
    data = P("section", "dp", None, None)
    return jax.shard_map(
        local,
        mesh=mesh,
        in_specs=(data, P(None, "dp"), P(None, "dp"), P(None, "dp", None), P(None, "dp", None))
        + weights,
        out_specs=(data,) + weights,
        check_vma=False,
    )
```

```python
import functools
import math

import jax
import jax.numpy as jnp
import numpy as np
from jax import lax
from jax.experimental import pallas as pl
from jax.experimental.pallas import tpu as pltpu
from jax.sharding import PartitionSpec as P

REL1 = 32
REL2 = 64
REACH1 = 128
REACH2 = 256
HEAD_DIM = 64
TEXT_MAX = 191
EPS = 1e-05
NEG = -1000000000.0
ROOT_HALF = 0.7071067811865476
INV_ROOT_TAU = 0.3989422804014327

UNIT = 4096.0
LOG2E = 1.4426950408889634
TILE = 128
VMEM = 60 * 2**20

BF = jnp.bfloat16
F32 = jnp.float32
NT = (((1,), (1,)), ((), ()))
TN = (((0,), (0,)), ((), ()))


def dot(a, b):
    return jnp.dot(a, b, preferred_element_type=F32)


def dot_nt(a, b):
    return lax.dot_general(a, b, NT, preferred_element_type=F32)


def dot_tn(a, b):
    return lax.dot_general(a, b, TN, preferred_element_type=F32)


def bucket_limits(total, reach):
    half = total // 2
    exact = half // 2
    return [
        int(math.ceil(exact * (reach / exact) ** (step / (half - exact)) - 1e-09))
        for step in range(1, half - exact)
    ]


def rel_bucket(delta, total, reach):
    half = total // 2
    exact = half // 2
    dist = jnp.abs(delta)
    far = exact + jnp.zeros_like(dist)
    for limit in bucket_limits(total, reach):
        far = far + (dist >= limit).astype(jnp.int32)
    return jnp.where(delta > 0, half, 0).astype(jnp.int32) + jnp.where(dist < exact, dist, far)


def line_bucket_np(delta):
    half = REL1 // 2
    exact = half // 2
    dist = np.abs(delta)
    far = np.full(dist.shape, exact)
    for limit in bucket_limits(REL1, REACH1):
        far = far + (dist >= limit)
    return np.where(delta > 0, half, 0) + np.where(dist < exact, dist, far)


def line_rows():
    k = np.arange(2 * TILE)
    shift = np.where(k < TILE, k, k - 2 * TILE)
    return line_bucket_np(np.stack([TILE * (s - 2) - shift for s in range(5)]))


def line_tiles():
    r = np.arange(TILE)
    return line_bucket_np(np.stack([TILE * (s - 2) + r[:, None] - r[None, :] for s in range(5)]))


def lane_pick(table, index):
    dims = lax.GatherDimensionNumbers(
        offset_dims=(),
        collapsed_slice_dims=(1,),
        start_index_map=(1,),
        operand_batching_dims=(0,),
        start_indices_batching_dims=(0,),
    )
    return lax.gather(
        table,
        index[..., None],
        dims,
        slice_sizes=(1, 1),
        mode=lax.GatherScatterMode.PROMISE_IN_BOUNDS,
    )


def attend_kernel(
    k_ref,
    qt_ref,
    vt_ref,
    mask_ref,
    x_ref,
    y_ref,
    tab_ref,
    line_ref,
    p_ref,
    c_ref,
    exact_ref,
    inv_ref,
    kaug,
    qaug,
    strip,
    scores,
):
    rows = k_ref.shape[0]
    chunk = 2 * TILE
    step = 32
    lane = lax.broadcasted_iota(jnp.int32, (rows, TILE), 1)
    keys = k_ref[...].astype(F32) * (UNIT / 8.0)
    kaug[0, :, :TILE] = jnp.where(lane < HEAD_DIM, keys, 0.0).astype(BF)
    kaug[1, :, :TILE] = jnp.where(lane < HEAD_DIM, 0.0, keys).astype(BF)
    kaug[0, :, TILE:] = mask_ref[...]
    kaug[1, :, TILE:] = mask_ref[...]
    qaug[:TILE, :] = qt_ref[...]
    qaug[TILE:, :] = jnp.ones((TILE, rows), BF)
    for head in range(2):
        for s in range(5):
            wide = jnp.broadcast_to(line_ref[head, s : s + 1, :], (TILE, 2 * TILE))
            if s in (1, 2, 3):
                wide = pltpu.roll(wide, 0, axis=1, stride=1, stride_axis=0)
            strip[head, s] = wide[:, :TILE]
    table = jnp.broadcast_to(tab_ref[0], (step, TILE))
    chunks = rows // chunk
    low = jnp.full((8, chunk), -3e38, F32)

    def score(t, n, peaks):
        cols = slice(t * chunk, (t + 1) * chunk)
        tile = pl.ds(pl.multiple_of(n * TILE, TILE), TILE)
        raw = [dot(kaug[head, tile, :], qaug[:, cols]) for head in range(2)]
        peaks = list(peaks)
        for m in range(TILE // step):
            at = pl.ds(pl.multiple_of(n * TILE + m * step, step), step)
            sub = slice(m * step, (m + 1) * step)
            parts = ([], [])
            for part in range(2):
                lanes = slice(part * TILE, (part + 1) * TILE)
                wide = slice(t * chunk + part * TILE, t * chunk + (part + 1) * TILE)
                both = lane_pick(table, x_ref[at, wide]) + lane_pick(table, y_ref[at, wide])
                off = jnp.clip(n - (2 * t + part), -2, 2) + 2
                for head, bits in ((0, both >> 16), (1, both & 0xFFFF)):
                    value = raw[head][sub, lanes] + strip[head, off, sub, :] + bits.astype(F32)
                    scores[t % 2, head, at, lanes] = value
                    parts[head].append(value)
            for head in range(2):
                wide = jnp.concatenate(parts[head], axis=1)
                for r in range(step // 8):
                    peaks[head] = jnp.maximum(peaks[head], wide[8 * r : 8 * r + 8, :])
        return tuple(peaks)

    def weigh(t, n, peaks):
        cols = slice(t * chunk, (t + 1) * chunk)
        for m in range(TILE // step):
            at = pl.ds(pl.multiple_of(n * TILE + m * step, step), step)
            for head in range(2):
                power = (scores[t % 2, head, at, :] - peaks[head]) * (LOG2E / UNIT)
                p_ref[head, at, cols] = jnp.exp2(power).astype(BF)

    ones = jnp.ones((16, rows), BF)

    def mix(t):
        cols = slice(t * chunk, (t + 1) * chunk)
        for head in range(2):
            mine = slice(head * HEAD_DIM, (head + 1) * HEAD_DIM)
            vals = jnp.concatenate([vt_ref[mine, :], ones], axis=0)
            mixed = dot(vals, p_ref[head, :, cols])
            inv = 1.0 / mixed[HEAD_DIM : HEAD_DIM + 1, :]
            exact = mixed[:HEAD_DIM, :] * inv
            exact_ref[mine, cols] = exact
            c_ref[mine, cols] = exact.astype(BF)
            inv_ref[0, head : head + 1, cols] = inv

    peaks = None
    for t in range(chunks + 1):
        old = peaks

        def both_steps(n, tops):
            if t < chunks:
                tops = score(t, n, tops)
            if t > 0:
                weigh(t - 1, n, old)
            return tops

        tops = lax.fori_loop(0, rows // TILE, both_steps, (low, low), unroll=6)
        peaks = [jnp.max(top, axis=0, keepdims=True) for top in tops]
        if t > 0:
            mix(t - 1)

def attend(qkv, qkv_t, mask, across, upward, tabs, lines, calls=1, part=0, before=()):
    rows = qkv.shape[0]
    width = qkv.shape[1] // 3
    pairs = width // TILE
    count = pairs // calls
    at = part * count
    whole = lambda p: (0, 0)
    kernel = attend_kernel
    if before:
        kernel = lambda *refs: attend_kernel(*refs[:8], *refs[12:])
    return pl.pallas_call(
        kernel,
        grid=(count,),
        in_specs=[
            pl.BlockSpec((rows, TILE), lambda p: (0, pairs + at + p)),
            pl.BlockSpec((TILE, rows), lambda p: (at + p, 0)),
            pl.BlockSpec((TILE, rows), lambda p: (2 * pairs + at + p, 0)),
            pl.BlockSpec((rows, TILE), whole),
            pl.BlockSpec((rows, rows), whole),
            pl.BlockSpec((rows, rows), whole),
            pl.BlockSpec((1, 1, TILE), lambda p: (at + p, 0, 0)),
            pl.BlockSpec((2, 8, 2 * TILE), lambda p: (at + p, 0, 0)),
        ]
        + [pl.BlockSpec(memory_space=pl.ANY) for _ in before],
        out_specs=[
            pl.BlockSpec((2, rows, rows), lambda p: (at + p, 0, 0)),
            pl.BlockSpec((TILE, rows), lambda p: (at + p, 0)),
            pl.BlockSpec((TILE, rows), lambda p: (at + p, 0)),
            pl.BlockSpec((1, 8, rows), lambda p: (at + p, 0, 0)),
        ],
        out_shape=[
            jax.ShapeDtypeStruct((2 * pairs, rows, rows), BF),
            jax.ShapeDtypeStruct((width, rows), BF),
            jax.ShapeDtypeStruct((width, rows), F32),
            jax.ShapeDtypeStruct((pairs, 8, rows), F32),
        ],
        scratch_shapes=[
            pltpu.VMEM((2, rows, 2 * TILE), BF),
            pltpu.VMEM((2 * TILE, rows), BF),
            pltpu.VMEM((2, 5, TILE, TILE), F32),
            pltpu.VMEM((2, 2, rows, 2 * TILE), F32),
        ],
        input_output_aliases={8 + n: n for n in range(len(before))},
        compiler_params=pltpu.CompilerParams(vmem_limit_bytes=VMEM),
        cost_estimate=pl.CostEstimate(
            flops=33 * 10**9 // calls, bytes_accessed=33 * 10**6 // calls, transcendentals=0
        ),
        name="attend",
    )(qkv, qkv_t, qkv_t, mask, across, upward, tabs, lines, *before)


def attend_back_kernel(
    p_ref,
    q_ref,
    kt_ref,
    v_ref,
    dc_ref,
    dct_ref,
    ct_ref,
    ds_ref,
    d_ref,
    line_ref,
    dqt,
):
    rows = q_ref.shape[0]
    line_ref[...] = jnp.zeros_like(line_ref)
    product = dct_ref[...].astype(F32) * ct_ref[...]
    lane = lax.broadcasted_iota(jnp.int32, (rows, TILE), 1)
    vals = v_ref[...]
    out_k, out_v = [], []
    for head in range(2):
        mine = slice(head * HEAD_DIM, (head + 1) * HEAD_DIM)
        delta = jnp.sum(product[mine, :], axis=0, keepdims=True)
        own = (lane < HEAD_DIM) if head == 0 else (lane >= HEAD_DIM)
        picked = jnp.where(own, vals, jnp.zeros_like(vals))
        for n in range(rows // TILE):
            at = slice(n * TILE, (n + 1) * TILE)
            dp = dot(picked[at, :], dct_ref[...])
            sums = {}
            for part in range(rows // TILE):
                lanes = slice(part * TILE, (part + 1) * TILE)
                weights = p_ref[head, at, lanes].astype(F32)
                grad = weights * (dp[:, lanes] - delta[:, lanes])
                ds_ref[head, at, lanes] = grad.astype(BF)
                off = min(max(n - part, -2), 2) + 2
                sums[off] = grad if off not in sums else sums[off] + grad
            for off, value in sums.items():
                line_ref[head, off] += value
        out_k.append(dot(ds_ref[head], q_ref[...]))
        out_v.append(dot(p_ref[head], dc_ref[...]))
        dqt[mine, :] = dot(kt_ref[mine, :], ds_ref[head])
    d_ref[1] = (jnp.where(lane < HEAD_DIM, out_k[0], out_k[1]) * 0.125).astype(BF)
    d_ref[2] = jnp.where(lane < HEAD_DIM, out_v[0], out_v[1]).astype(BF)
    d_ref[0] = (jnp.transpose(dqt[...]) * 0.125).astype(BF)


def attend_back(weights, qkv, qkv_t, dc, dct, ct):
    rows = qkv.shape[0]
    width = qkv.shape[1] // 3
    pairs = width // TILE
    return pl.pallas_call(
        attend_back_kernel,
        grid=(pairs,),
        in_specs=[
            pl.BlockSpec((2, rows, rows), lambda p: (p, 0, 0)),
            pl.BlockSpec((rows, TILE), lambda p: (0, p)),
            pl.BlockSpec((TILE, rows), lambda p: (pairs + p, 0)),
            pl.BlockSpec((rows, TILE), lambda p: (0, 2 * pairs + p)),
            pl.BlockSpec((rows, TILE), lambda p: (0, p)),
            pl.BlockSpec((TILE, rows), lambda p: (p, 0)),
            pl.BlockSpec((TILE, rows), lambda p: (p, 0)),
        ],
        out_specs=[
            pl.BlockSpec((2, rows, rows), lambda p: (p, 0, 0)),
            pl.BlockSpec((3, rows, TILE), lambda p: (0, 0, p)),
            pl.BlockSpec((2, 5, TILE, TILE), lambda p: (p, 0, 0, 0)),
        ],
        out_shape=[
            jax.ShapeDtypeStruct((2 * pairs, rows, rows), BF),
            jax.ShapeDtypeStruct((3, rows, width), BF),
            jax.ShapeDtypeStruct((2 * pairs, 5, TILE, TILE), F32),
        ],
        scratch_shapes=[
            pltpu.VMEM((TILE, rows), F32),
        ],
        compiler_params=pltpu.CompilerParams(vmem_limit_bytes=VMEM),
        cost_estimate=pl.CostEstimate(flops=20 * 10**9, bytes_accessed=20 * 10**6, transcendentals=0),
        name="attend_back",
    )(weights, qkv, qkv_t, qkv, dc, dct, ct)


def table_kernel(first_ref, second_ref, x_ref, y_ref, o_ref, scr):
    heads, block, rows = first_ref.shape
    parts = rows // TILE

    @pl.when(pl.program_id(0) == 0)
    def start():
        o_ref[...] = jnp.zeros_like(o_ref)
        scr[...] = jnp.zeros_like(scr)

    for layer, ref in enumerate((first_ref, second_ref)):
        for head in range(heads):
            wide = ref[head].astype(F32)
            at = (layer * heads + head) * block
            for c in range(parts):
                scr[c, at : at + block, :] = wide[:, c * TILE : (c + 1) * TILE]
    index = lax.broadcasted_iota(jnp.int32, (REL2, rows), 0)
    total = o_ref[...]
    for j in range(block):
        grads = jnp.concatenate(
            [scr[c, pl.ds(j, 32, stride=block), :] for c in range(parts)], axis=1
        ).astype(BF)
        row_x = jnp.broadcast_to(x_ref[j : j + 1, :], (REL2, rows))
        row_y = jnp.broadcast_to(y_ref[j : j + 1, :], (REL2, rows))
        hot = jnp.concatenate(
            [
                jnp.where(row_x == index, 1.0, 0.0).astype(BF),
                jnp.where(row_y == index + REL2, 1.0, 0.0).astype(BF),
            ],
            axis=0,
        )
        total = total + dot_nt(grads, hot)
    o_ref[...] = total


def table_sums(first, second, across, upward, part, parts):
    heads, rows, _ = first.shape
    block = 32
    count = rows // block // parts
    at = part * count
    return pl.pallas_call(
        table_kernel,
        grid=(count,),
        in_specs=[
            pl.BlockSpec((heads, block, rows), lambda g: (0, at + g, 0)),
            pl.BlockSpec((heads, block, rows), lambda g: (0, at + g, 0)),
            pl.BlockSpec((block, rows), lambda g: (at + g, 0)),
            pl.BlockSpec((block, rows), lambda g: (at + g, 0)),
        ],
        out_specs=pl.BlockSpec((32, 2 * REL2), lambda g: (0, 0)),
        out_shape=jax.ShapeDtypeStruct((32, 2 * REL2), F32),
        scratch_shapes=[pltpu.VMEM((rows // TILE, 32 * block, TILE), F32)],
        compiler_params=pltpu.CompilerParams(vmem_limit_bytes=VMEM),
        cost_estimate=pl.CostEstimate(flops=13 * 10**9, bytes_accessed=13 * 10**6, transcendentals=0),
        name="table_sums",
    )(first, second, across, upward)


def nothing_kernel(*refs):
    pass


def unset(shape, dtype):
    return pl.pallas_call(
        nothing_kernel,
        out_specs=pl.BlockSpec(memory_space=pl.ANY),
        out_shape=jax.ShapeDtypeStruct(shape, dtype),
        name="unset",
    )()


class Place:
    def __init__(self):
        index = lax.axis_index("section")
        self.peers = lax.axis_size("section")
        self.docs = lax.axis_size("dp")
        self.half = index % 2
        self.layer = index // 2
        where = lax.axis_index("dp")
        bits = range(self.docs.bit_length() - 1)
        self.orders = [list(bits), [1, 0] + list(bits)[2:]]
        self.sides = [
            jnp.where(self.half == 0, (where >> one) & 1, (where >> two) & 1)
            for one, two in zip(*self.orders)
        ]

    def across(self, value, mask):
        return lax.ppermute(value, "section", [(i, i ^ mask) for i in range(self.peers)])

    def to_layer(self, value, layer):
        other = 1 - layer
        pairs = [(2 * other + h, 2 * layer + h) for h in range(2)]
        return lax.ppermute(value, "section", pairs)

    def facing(self, value, step):
        pairs = []
        for s in range(self.peers):
            for d in range(self.docs):
                pairs.append((s * self.docs + d, s * self.docs + (d ^ (1 << self.orders[s % 2][step]))))
        return lax.ppermute(value, ("section", "dp"), pairs)

    def joined(self, mine, theirs, side):
        return jnp.where(
            side == 0, jnp.concatenate([mine, theirs], 0), jnp.concatenate([theirs, mine], 0)
        )

    def parted(self, value, side):
        rows = value.shape[0] // 2
        return (
            lax.dynamic_slice_in_dim(value, side * rows, rows, 0),
            lax.dynamic_slice_in_dim(value, (1 - side) * rows, rows, 0),
        )


    def weight_flow(self, mine):
        rows, cols = mine.shape
        part = rows // 4
        spot = 2 * self.sides[1] + self.sides[0]
        mate = self.across(mine, 1)
        got = yield self.across(lax.dynamic_slice_in_dim(mine, spot * part, part, 0), 2)
        for step in range(2):
            got = self.joined(got, (yield self.facing(got, step)), self.sides[step])
        full = unset((4 * rows, cols), mine.dtype)
        arrived = yield self.across(got, 1)
        for value, layer, half in (
            (mine, self.layer, self.half),
            (mate, self.layer, 1 - self.half),
            (got, 1 - self.layer, self.half),
            (arrived, 1 - self.layer, 1 - self.half),
        ):
            full = lax.dynamic_update_slice_in_dim(full, value, (2 * layer + half) * rows, 0)
        return full.reshape(2, 2 * rows, cols)

    def scatter_flow(self, full):
        keep, send = self.parted(full.astype(BF), self.half)
        total = (keep.astype(F32) + (yield self.across(send, 1)).astype(F32)).astype(BF)
        for step, side in enumerate(self.sides):
            keep, send = self.parted(total, side)
            total = (keep.astype(F32) + (yield self.facing(send, step)).astype(F32)).astype(BF)
        return total

    def gather_flow(self, second, first):
        mine = jnp.where(self.layer == 1, second, first)
        sent = yield self.across(jnp.where(self.layer == 1, first, second), 2)
        total = (mine.astype(F32) + sent.astype(F32)).astype(BF)
        for step, side in reversed(list(enumerate(self.sides))):
            total = self.joined(total, (yield self.facing(total, step)), side)
        return total.astype(F32)

    def all_flow(self, value):
        for mask in (1, 2):
            value = value + (yield self.across(value, mask))
        for step in range(len(self.sides)):
            value = value + (yield self.facing(value, step))
        return value


class Flow:
    def __init__(self, steps):
        self.steps = steps
        self.result = None
        self.air = next(steps)

    def land(self, arrived):
        try:
            self.air = self.steps.send(arrived)
        except StopIteration as end:
            self.air = None
            self.result = end.value


def pace(value, *flows):
    flows = [flow for flow in flows if flow.air is not None]
    value, air = lax.optimization_barrier((value, [flow.air for flow in flows]))
    for flow, arrived in zip(flows, air):
        flow.land(arrived)
    return value


def finished(flow):
    while flow.air is not None:
        flow.land(flow.air)
    return flow.result


def normalize(values):
    centered = values - jnp.mean(values, axis=-1, keepdims=True)
    scale = lax.rsqrt(jnp.mean(centered * centered, axis=-1, keepdims=True) + EPS)
    return (centered * scale, scale)


def norm_back(grad_norm, normed, scale):
    return scale * (
        grad_norm
        - jnp.mean(grad_norm, axis=-1, keepdims=True)
        - normed * jnp.mean(grad_norm * normed, axis=-1, keepdims=True)
    )


def doc_tables(text_len, patches, box_x, box_y):
    rows = box_x.shape[0]
    index = jnp.arange(rows, dtype=jnp.int32)
    live = (index < text_len) | ((index >= TEXT_MAX) & (index < TEXT_MAX + 1 + patches))
    across = rel_bucket(box_x[:, None] - box_x[None, :], REL2, REACH2)
    upward = rel_bucket(box_y[:, None] - box_y[None, :], REL2, REACH2) + REL2
    first = jnp.arange(TILE) == 0
    mask = jnp.where(first[None, :] & ~live[:, None], NEG * UNIT, 0.0).astype(BF)
    return (live, across, upward, mask)


def score_tables(quarters):
    count, _, _, heads = quarters.shape
    cut = REL1 // 2
    box = quarters[:, :, cut:, :].astype(F32).reshape(count, 2, 2, REL2 // 2, heads)
    box = jnp.transpose(box, (0, 4, 2, 1, 3)).reshape(count, heads // 2, 2, 2 * REL2)
    fixed = jnp.round(box * UNIT).astype(jnp.int32)
    tabs = fixed[:, :, :1] * 65536 + fixed[:, :, 1:] + 16384
    chosen = np.concatenate([line_rows(), np.zeros((3, 2 * TILE), int)]).reshape(-1)
    hot = jnp.asarray(chosen[None, :] == np.arange(REL1)[:, None], BF)
    line = quarters[:, :, :cut, :].reshape(count, REL1, heads)
    lines = lax.dot_general(line, hot, (((1,), (0,)), ((), ())), preferred_element_type=F32)
    odd = (jnp.arange(heads) % 2).astype(F32)[:, None]
    lines = (lines * UNIT - odd * 32768.0).reshape(count, heads, 8, 2 * TILE)
    return (tabs, lines)


def packed_vectors(vectors):
    wide = vectors[1].shape[-1]
    rows = [v.reshape(-1, wide) for v in vectors]
    rows.append(jnp.zeros((4, wide), rows[0].dtype))
    return jnp.concatenate(rows, axis=0)


def layer_vectors(quarters):
    wide = quarters.shape[-1]
    quarters = quarters.astype(F32)
    rows = jnp.transpose(quarters, (0, 2, 1, 3)).reshape(2, -1, 2 * wide)
    layers = []
    for n in range(2):
        b_qv = quarters[n, :, :2].reshape(2, 2 * wide)
        b_in = quarters[n, :, 5:9].reshape(8 * wide)
        b_out, gain1, shift1 = rows[n, 2], rows[n, 3], rows[n, 4]
        b_back, gain2, shift2 = rows[n, 9], rows[n, 10], rows[n, 11]
        layers.append((b_qv, b_out, gain1, shift1, b_in, b_back, gain2, shift2))
    return layers


def norm_grads(dy, gain, normed, scale):
    return (
        norm_back(dy * gain, normed, scale),
        (jnp.sum(dy * normed, axis=0), jnp.sum(dy, axis=0)),
    )


def local(
    section_data,
    text_len,
    patches,
    box_x,
    box_y,
    w_qkv,
    b_qv,
    w_out,
    b_out,
    norm1_gain,
    norm1_bias,
    w_in,
    b_in,
    w_back,
    b_back,
    norm2_gain,
    norm2_bias,
    rel_line,
    rel_x,
    rel_y,
):
    place = Place()
    heads = rel_line.shape[2]
    rows, width = section_data.shape[2:]
    first = place.layer == 0

    entries = section_data[0]
    wf_qkv = Flow(place.weight_flow(w_qkv[0]))
    got = place.across(jnp.where(first, entries[1], entries[0]), 2)

    def mine(table):
        table = jnp.where(place.half == 0, table[0], table[1])
        return jnp.where(first, table[0], table[1])

    vectors = packed_vectors(
        [v[0] for v in (b_qv, b_out, norm1_gain, norm1_bias, b_in, b_back, norm2_gain, norm2_bias)]
    )
    tables = jnp.concatenate([rel_line[0], rel_x[0], rel_y[0]], axis=0)
    index = 2 * place.layer + place.half

    def quarters(own):
        shifts = jnp.stack([own] + [place.across(own, mask) for mask in (1, 2, 3)])
        every = jnp.stack(
            [lax.dynamic_index_in_dim(shifts, index ^ q, 0, keepdims=False) for q in range(4)]
        )
        return every.reshape(2, 2, *own.shape)

    vectors = quarters(vectors)
    tables = quarters(tables)
    boxes = pace([mine(t) for t in (text_len, patches, box_x, box_y)], wf_qkv)
    w_rest = lax.optimization_barrier((w_out[0], w_in[0], w_back[0], wf_qkv.air))[:3]
    wf_out, wf_in, wf_back = [Flow(place.weight_flow(w)) for w in w_rest]
    meta = pace(doc_tables(*boxes), wf_qkv)
    live = meta[0]
    scores = pace(score_tables(tables), wf_qkv)
    params = layer_vectors(vectors)
    source = jnp.where(first, entries[0], got)
    cotangent = jnp.where(first, got, entries[1])
    source = pace(source, wf_qkv, wf_out)
    w_qkv = finished(wf_qkv)

    def no_pace(value, *flows):
        return value

    def forward(x, n, paced, calls):
        b_qv, b_out, gain1, shift1, b_in, b_back, gain2, shift2 = params[n]
        bias = jnp.concatenate([b_qv[0], jnp.zeros((width,), F32), b_qv[1]])
        qkv = (dot(x, w_qkv[n]) + bias).astype(BF)
        qkv = paced(qkv, wf_out, wf_in)
        qkv_t = lax.dot_general(w_qkv[n], x, (((0,), (1,)), ((), ())), preferred_element_type=F32)
        qkv_t = (qkv_t + bias[:, None]).astype(BF)
        mixed = ()
        for part in range(calls):
            mixed = attend(
                qkv, qkv_t, meta[3], *meta[1:3], scores[0][n], scores[1][n], calls, part, mixed
            )
            mixed = paced(mixed, wf_out, wf_in, wf_back)
        weights, ct, exact, inv = mixed
        w_out = finished(wf_out)
        attended = dot_tn(ct, w_out[n]) + b_out
        n1, rstd1 = normalize(x.astype(F32) + attended)
        n1, rstd1 = paced((n1, rstd1), wf_in)
        w_in = finished(wf_in)
        hidden = n1 * gain1 + shift1
        hidden_low = hidden.astype(BF)
        u = dot(hidden_low, w_in[n]) + b_in
        phi = 0.5 * (1.0 + lax.erf(u * ROOT_HALF))
        tg = (u * phi).astype(BF)
        slope = (phi + u * jnp.exp(-0.5 * u * u) * INV_ROOT_TAU).astype(BF)
        tg, slope = paced((tg, slope), wf_back)
        tg, slope = paced((tg, slope), wf_back)
        w_back = finished(wf_back)
        n2, rstd2 = normalize(hidden + dot(tg, w_back[n]) + b_back)
        y = jnp.where(live[:, None], n2 * gain2 + shift2, 0.0).astype(BF)
        return dict(
            x=x, qkv=qkv, qkv_t=qkv_t, weights=weights, ct=ct, exact=exact, inv=inv, n1=n1, rstd1=rstd1,
            hidden=hidden_low, tg=tg, slope=slope, n2=n2, rstd2=rstd2, y=y,
        )

    kept = [forward(source, 0, pace, 2)]
    kept.append(forward(kept[0]["y"], 1, no_pace, 1))
    w_out, w_in, w_back = finished(wf_out), finished(wf_in), finished(wf_back)

    def feed_back(dy, n):
        keep = kept[n]
        gain2 = params[n][6]
        dym = jnp.where(live[:, None], dy.astype(F32), 0.0)
        dr2, g_norm2 = norm_grads(dym, gain2, keep["n2"], keep["rstd2"])
        df = dr2.astype(BF)
        du = (dot_nt(df, w_back[n]) * keep["slope"].astype(F32)).astype(BF)
        g_b_back = jnp.sum(df.astype(F32), axis=0)
        g_b_in = jnp.sum(du.astype(F32), axis=0)
        return (dr2, df, du, (g_norm2, g_b_back, g_b_in))

    def norm1_back(dr2, du, n):
        keep = kept[n]
        dh1 = dr2 + dot_nt(du, w_in[n])
        return norm_grads(dh1, params[n][2], keep["n1"], keep["rstd1"])

    def context_back(dr1, n):
        da = dr1.astype(BF)
        inv = kept[n]["inv"][:, :2, :].reshape(-1, rows)
        inv = jnp.repeat(inv, HEAD_DIM, axis=0)
        dct = (dot_nt(w_out[n], da).astype(BF).astype(F32) * inv).astype(BF)
        dc = (dot_nt(da, w_out[n]).astype(BF).astype(F32) * inv.T).astype(BF)
        return (da, dc, dct, jnp.sum(da.astype(F32), axis=0))

    def scores_back(dc, dct, n):
        keep = kept[n]
        return attend_back(keep["weights"], keep["qkv"], keep["qkv_t"], dc, dct, keep["exact"])

    def input_back(dr1, dqkv, n):
        dx = dr1
        for part in range(3):
            dx = dx + dot_nt(dqkv[part], w_qkv[n][:, part * width : (part + 1) * width])
        return (dx.astype(BF), jnp.sum(dqkv[::2].astype(F32), axis=1))

    def back_grad(df, n):
        return Flow(place.scatter_flow(dot_tn(kept[n]["tg"], df)))

    def in_grad(du, n):
        return Flow(place.scatter_flow(dot_tn(kept[n]["hidden"], du)))

    def mixing_grad(dqkv, da, n):
        g_qkv = lax.dot_general(
            kept[n]["x"], dqkv, (((0,), (1,)), ((), ())), preferred_element_type=F32
        ).reshape(width, -1)
        g_out = dot(kept[n]["ct"], da)
        return Flow(place.scatter_flow(jnp.concatenate([g_qkv, g_out], axis=1)))

    def vector_rows(g_norm1, g_norm2, g_b_back, g_b_in, g_b_out, g_b_qv):
        rows = [*g_b_qv, g_b_out, *g_norm1, *g_b_in.reshape(-1, width), g_b_back, *g_norm2]
        return jnp.stack(rows)

    dr2, df, du, s_feed = feed_back(cotangent, 1)
    f_back = back_grad(df, 1)
    dr1, g_norm1 = norm1_back(dr2, du, 1)
    f_in = in_grad(du, 1)
    da, dc, dct, s_out = context_back(dr1, 1)
    dc, dct = pace((dc, dct), f_back, f_in)
    ds1, dqkv, line1 = pace(scores_back(dc, dct, 1), f_back, f_in)
    dx, s_qv = input_back(dr1, dqkv, 1)
    dx = pace(dx, f_back, f_in)
    f_mix = mixing_grad(dqkv, da, 1)
    vectors1 = vector_rows(g_norm1, *s_feed, s_out, s_qv)

    dr2, df, du, s_feed = feed_back(dx, 0)
    du = pace(du, f_back, f_in, f_mix)
    dr1, g_norm1 = norm1_back(dr2, du, 0)
    e_back, e_in = back_grad(df, 0), in_grad(du, 0)
    dr1 = pace(dr1, f_mix)
    da, dc, dct, s_out = context_back(dr1, 0)
    dc, dct = pace((dc, dct), f_mix, e_back, e_in)
    ds0, dqkv, line0 = pace(scores_back(dc, dct, 0), f_mix, e_back, e_in)
    dx, s_qv = input_back(dr1, dqkv, 0)
    dx = pace(dx, e_back, e_in)
    e_mix = mixing_grad(dqkv, da, 0)
    vectors0 = vector_rows(g_norm1, *s_feed, s_out, s_qv)
    sent = place.across(jnp.where(first, kept[1]["y"], dx), 2)
    a_vectors = Flow(place.all_flow(jnp.stack([vectors0, vectors1])))

    flows = [e_back, e_in, e_mix, a_vectors]
    stores = (ds0, ds1)
    table = 0.0
    for part in range(4):
        table = table + table_sums(*stores, *meta[1:3], part, 4)
        table, stores = pace((table, stores), *flows)
        if part == 0:
            s_back = Flow(place.gather_flow(finished(f_back), finished(e_back)))
            s_in = Flow(place.gather_flow(finished(f_in), finished(e_in)))
            flows = [e_mix, s_back, s_in, a_vectors]
    s_mix = Flow(place.gather_flow(finished(f_mix), finished(e_mix)))
    hot = jnp.asarray(line_tiles().reshape(-1)[:, None] == np.arange(REL1)[None, :], BF)
    lines = jnp.concatenate([line0, line1], axis=0).reshape(2 * heads, -1).astype(BF)
    lines = jnp.pad(dot(lines, hot), ((0, 32 - 2 * heads), (0, 0)))
    a_tables = Flow(place.all_flow(jnp.concatenate([table, lines], axis=1)))
    flows = [s_back, s_in, s_mix, a_vectors, a_tables]
    token = dx
    while any(flow.air is not None for flow in flows):
        token = pace(token, *flows)
    g_back, g_in, g_mix = s_back.result, s_in.result, s_mix.result
    g_qkv, g_out = g_mix[:, : 3 * width], g_mix[:, 3 * width :]

    def own(array):
        return lax.dynamic_index_in_dim(array, place.layer, 0, keepdims=False)

    v = own(a_vectors.result)
    half_width = width // 2
    v_half = lax.dynamic_slice_in_dim(v, place.half * half_width, half_width, 1)
    v_qv = lax.dynamic_index_in_dim(v, place.half, 0)
    v_in = lax.dynamic_slice_in_dim(v, 5 + 2 * place.half, 2, 0).reshape(1, -1)
    t = a_tables.result[: 2 * heads].reshape(2, heads, -1)
    t = own(t).T

    def table_half(at, size):
        return lax.dynamic_slice_in_dim(t, at + place.half * size, size, 0)[None]

    t_x, t_y = table_half(0, REL2 // 2), table_half(REL2, REL2 // 2)
    t_line = table_half(2 * REL2, REL1 // 2)
    result = jnp.where(first, jnp.stack([dx, sent]), jnp.stack([sent, kept[1]["y"]]))[None]
    return (
        result, g_qkv[None], v_qv, g_out[None], v_half[2:3], v_half[3:4], v_half[4:5],
        g_in[None], v_in, g_back[None], v_half[9:10], v_half[10:11], v_half[11:12],
        t_line, t_x, t_y,
    )


def solution(mesh):
    matrix = P("section", None, None)
    vector = P("section", None)
    weights = (
        matrix, vector, matrix, vector, vector, vector, matrix, vector, matrix,
        vector, vector, vector, matrix, matrix, matrix,
    )
    data = P("section", "dp", None, None)
    return jax.shard_map(
        local,
        mesh=mesh,
        in_specs=(data, P(None, "dp"), P(None, "dp"), P(None, "dp", None), P(None, "dp", None))
        + weights,
        out_specs=(data,) + weights,
        check_vma=False,
    )
```

```python
import functools
import math

import jax
import jax.numpy as jnp
import numpy as np
from jax import lax
from jax.experimental import pallas as pl
from jax.experimental.pallas import tpu as pltpu
from jax.sharding import PartitionSpec as P

REL1 = 32
REL2 = 64
REACH1 = 128
REACH2 = 256
HEAD_DIM = 64
TEXT_MAX = 191
EPS = 1e-05
NEG = -1000000000.0
ROOT_HALF = 0.7071067811865476
INV_ROOT_TAU = 0.3989422804014327

UNIT = 4096.0
LOG2E = 1.4426950408889634
TILE = 128
VMEM = 60 * 2**20
FREE = pl.CostEstimate(flops=1, bytes_accessed=1, transcendentals=0)

BF = jnp.bfloat16
F32 = jnp.float32
NT = (((1,), (1,)), ((), ()))
TN = (((0,), (0,)), ((), ()))


def dot(a, b):
    return jnp.dot(a, b, preferred_element_type=F32)


def dot_nt(a, b):
    return lax.dot_general(a, b, NT, preferred_element_type=F32)


def dot_tn(a, b):
    return lax.dot_general(a, b, TN, preferred_element_type=F32)


def bucket_limits(total, reach):
    half = total // 2
    exact = half // 2
    return [
        int(math.ceil(exact * (reach / exact) ** (step / (half - exact)) - 1e-09))
        for step in range(1, half - exact)
    ]


def line_bucket_np(delta):
    half = REL1 // 2
    exact = half // 2
    dist = np.abs(delta)
    far = np.full(dist.shape, exact)
    for limit in bucket_limits(REL1, REACH1):
        far = far + (dist >= limit)
    return np.where(delta > 0, half, 0) + np.where(dist < exact, dist, far)


def line_rows():
    k = np.arange(2 * TILE)
    shift = np.where(k < TILE, k, k - 2 * TILE)
    return line_bucket_np(np.stack([TILE * (s - 2) - shift for s in range(5)]))


def line_tiles():
    r = np.arange(TILE)
    return line_bucket_np(np.stack([TILE * (s - 2) + r[:, None] - r[None, :] for s in range(5)]))


def lane_pick(table, index):
    dims = lax.GatherDimensionNumbers(
        offset_dims=(),
        collapsed_slice_dims=(1,),
        start_index_map=(1,),
        operand_batching_dims=(0,),
        start_indices_batching_dims=(0,),
    )
    return lax.gather(
        table,
        index[..., None],
        dims,
        slice_sizes=(1, 1),
        mode=lax.GatherScatterMode.PROMISE_IN_BOUNDS,
    )


def attend_kernel(
    k_ref,
    qt_ref,
    vt_ref,
    mask_ref,
    x_ref,
    y_ref,
    tab_ref,
    line_ref,
    p_ref,
    c_ref,
    exact_ref,
    inv_ref,
    kaug,
    qaug,
    strip,
    scores,
):
    rows = k_ref.shape[0]
    chunk = 2 * TILE
    step = 32
    lane = lax.broadcasted_iota(jnp.int32, (rows, TILE), 1)
    keys = k_ref[...].astype(F32) * (UNIT / 8.0)
    kaug[0, :, :TILE] = jnp.where(lane < HEAD_DIM, keys, 0.0).astype(BF)
    kaug[1, :, :TILE] = jnp.where(lane < HEAD_DIM, 0.0, keys).astype(BF)
    kaug[0, :, TILE:] = mask_ref[...]
    kaug[1, :, TILE:] = mask_ref[...]
    qaug[:TILE, :] = qt_ref[...]
    qaug[TILE:, :] = jnp.ones((TILE, rows), BF)
    for head in range(2):
        for s in range(5):
            wide = jnp.broadcast_to(line_ref[head, s : s + 1, :], (TILE, 2 * TILE))
            if s in (1, 2, 3):
                wide = pltpu.roll(wide, 0, axis=1, stride=1, stride_axis=0)
            strip[head, s] = wide[:, :TILE]
    table = jnp.broadcast_to(tab_ref[0], (step, TILE))
    chunks = rows // chunk
    low = jnp.full((8, chunk), -3e38, F32)

    def score(t, n, peaks):
        cols = slice(t * chunk, (t + 1) * chunk)
        tile = pl.ds(pl.multiple_of(n * TILE, TILE), TILE)
        raw = [dot(kaug[head, tile, :], qaug[:, cols]) for head in range(2)]
        peaks = list(peaks)
        for m in range(TILE // step):
            at = pl.ds(pl.multiple_of(n * TILE + m * step, step), step)
            sub = slice(m * step, (m + 1) * step)
            parts = ([], [])
            for part in range(2):
                lanes = slice(part * TILE, (part + 1) * TILE)
                wide = slice(t * chunk + part * TILE, t * chunk + (part + 1) * TILE)
                both = lane_pick(table, x_ref[at, wide]) + lane_pick(table, y_ref[at, wide])
                off = jnp.clip(n - (2 * t + part), -2, 2) + 2
                for head, bits in ((0, both >> 16), (1, both & 0xFFFF)):
                    value = raw[head][sub, lanes] + strip[head, off, sub, :] + bits.astype(F32)
                    scores[t % 2, head, at, lanes] = value
                    parts[head].append(value)
            for head in range(2):
                wide = jnp.concatenate(parts[head], axis=1)
                for r in range(step // 8):
                    peaks[head] = jnp.maximum(peaks[head], wide[8 * r : 8 * r + 8, :])
        return tuple(peaks)

    def weigh(t, n, peaks):
        cols = slice(t * chunk, (t + 1) * chunk)
        for m in range(TILE // step):
            at = pl.ds(pl.multiple_of(n * TILE + m * step, step), step)
            for head in range(2):
                power = (scores[t % 2, head, at, :] - peaks[head]) * (LOG2E / UNIT)
                p_ref[head, at, cols] = jnp.exp2(power).astype(BF)

    ones = jnp.ones((16, rows), BF)

    def mix(t):
        cols = slice(t * chunk, (t + 1) * chunk)
        for head in range(2):
            mine = slice(head * HEAD_DIM, (head + 1) * HEAD_DIM)
            vals = jnp.concatenate([vt_ref[mine, :], ones], axis=0)
            mixed = dot(vals, p_ref[head, :, cols])
            inv = 1.0 / mixed[HEAD_DIM : HEAD_DIM + 1, :]
            exact = mixed[:HEAD_DIM, :] * inv
            exact_ref[mine, cols] = exact
            c_ref[mine, cols] = exact.astype(BF)
            inv_ref[0, head : head + 1, cols] = inv

    peaks = None
    for t in range(chunks + 1):
        old = peaks

        def both_steps(n, tops):
            if t < chunks:
                tops = score(t, n, tops)
            if t > 0:
                weigh(t - 1, n, old)
            return tops

        tops = lax.fori_loop(0, rows // TILE, both_steps, (low, low), unroll=6)
        peaks = [jnp.max(top, axis=0, keepdims=True) for top in tops]
        if t > 0:
            mix(t - 1)

def attend(qkv, qkv_t, mask, across, upward, tabs, lines, calls=1, part=0, before=()):
    rows = qkv.shape[0]
    width = qkv.shape[1] // 3
    pairs = width // TILE
    count = pairs // calls
    at = part * count
    whole = lambda p: (0, 0)
    kernel = attend_kernel
    if before:
        kernel = lambda *refs: attend_kernel(*refs[:8], *refs[12:])
    return pl.pallas_call(
        kernel,
        grid=(count,),
        in_specs=[
            pl.BlockSpec((rows, TILE), lambda p: (0, pairs + at + p)),
            pl.BlockSpec((TILE, rows), lambda p: (at + p, 0)),
            pl.BlockSpec((TILE, rows), lambda p: (2 * pairs + at + p, 0)),
            pl.BlockSpec((rows, TILE), whole),
            pl.BlockSpec((rows, rows), whole),
            pl.BlockSpec((rows, rows), whole),
            pl.BlockSpec((1, 1, TILE), lambda p: (at + p, 0, 0)),
            pl.BlockSpec((2, 8, 2 * TILE), lambda p: (at + p, 0, 0)),
        ]
        + [pl.BlockSpec(memory_space=pl.ANY) for _ in before],
        out_specs=[
            pl.BlockSpec((2, rows, rows), lambda p: (at + p, 0, 0)),
            pl.BlockSpec((TILE, rows), lambda p: (at + p, 0)),
            pl.BlockSpec((TILE, rows), lambda p: (at + p, 0)),
            pl.BlockSpec((1, 8, rows), lambda p: (at + p, 0, 0)),
        ],
        out_shape=[
            jax.ShapeDtypeStruct((2 * pairs, rows, rows), BF),
            jax.ShapeDtypeStruct((width, rows), BF),
            jax.ShapeDtypeStruct((width, rows), F32),
            jax.ShapeDtypeStruct((pairs, 8, rows), F32),
        ],
        scratch_shapes=[
            pltpu.VMEM((2, rows, 2 * TILE), BF),
            pltpu.VMEM((2 * TILE, rows), BF),
            pltpu.VMEM((2, 5, TILE, TILE), F32),
            pltpu.VMEM((2, 2, rows, 2 * TILE), F32),
        ],
        input_output_aliases={8 + n: n for n in range(len(before))},
        compiler_params=pltpu.CompilerParams(vmem_limit_bytes=VMEM),
        cost_estimate=FREE,
        name="attend",
    )(qkv, qkv_t, qkv_t, mask, across, upward, tabs, lines, *before)


def attend_back_kernel(
    p_ref,
    q_ref,
    kt_ref,
    v_ref,
    dc_ref,
    dct_ref,
    ct_ref,
    ds_ref,
    d_ref,
    line_ref,
    dqt,
):
    rows = q_ref.shape[0]
    line_ref[...] = jnp.zeros_like(line_ref)
    product = dct_ref[...].astype(F32) * ct_ref[...]
    lane = lax.broadcasted_iota(jnp.int32, (rows, TILE), 1)
    vals = v_ref[...]
    out_k, out_v = [], []
    for head in range(2):
        mine = slice(head * HEAD_DIM, (head + 1) * HEAD_DIM)
        delta = jnp.sum(product[mine, :], axis=0, keepdims=True)
        own = (lane < HEAD_DIM) if head == 0 else (lane >= HEAD_DIM)
        picked = jnp.where(own, vals, jnp.zeros_like(vals))
        for n in range(rows // TILE):
            at = slice(n * TILE, (n + 1) * TILE)
            dp = dot(picked[at, :], dct_ref[...])
            sums = {}
            for part in range(rows // TILE):
                lanes = slice(part * TILE, (part + 1) * TILE)
                weights = p_ref[head, at, lanes].astype(F32)
                grad = weights * (dp[:, lanes] - delta[:, lanes])
                ds_ref[head, at, lanes] = grad.astype(BF)
                off = min(max(n - part, -2), 2) + 2
                sums[off] = grad if off not in sums else sums[off] + grad
            for off, value in sums.items():
                line_ref[head, off] += value
        out_k.append(dot(ds_ref[head], q_ref[...]))
        out_v.append(dot(p_ref[head], dc_ref[...]))
        dqt[mine, :] = dot(kt_ref[mine, :], ds_ref[head])
    width = d_ref.shape[1] // 3
    base = pl.multiple_of(pl.program_id(0) * TILE, TILE)
    d_ref[:, pl.ds(width + base, TILE)] = (
        jnp.where(lane < HEAD_DIM, out_k[0], out_k[1]) * 0.125
    ).astype(BF)
    d_ref[:, pl.ds(2 * width + base, TILE)] = jnp.where(lane < HEAD_DIM, out_v[0], out_v[1]).astype(BF)
    d_ref[:, pl.ds(base, TILE)] = (jnp.transpose(dqt[...]) * 0.125).astype(BF)


def attend_back(weights, qkv, qkv_t, dc, dct, ct):
    rows = qkv.shape[0]
    width = qkv.shape[1] // 3
    pairs = width // TILE
    return pl.pallas_call(
        attend_back_kernel,
        grid=(pairs,),
        in_specs=[
            pl.BlockSpec((2, rows, rows), lambda p: (p, 0, 0)),
            pl.BlockSpec((rows, TILE), lambda p: (0, p)),
            pl.BlockSpec((TILE, rows), lambda p: (pairs + p, 0)),
            pl.BlockSpec((rows, TILE), lambda p: (0, 2 * pairs + p)),
            pl.BlockSpec((rows, TILE), lambda p: (0, p)),
            pl.BlockSpec((TILE, rows), lambda p: (p, 0)),
            pl.BlockSpec((TILE, rows), lambda p: (p, 0)),
        ],
        out_specs=[
            pl.BlockSpec((2, rows, rows), lambda p: (p, 0, 0)),
            pl.BlockSpec((rows, 3 * width), lambda p: (0, 0)),
            pl.BlockSpec((2, 5, TILE, TILE), lambda p: (p, 0, 0, 0)),
        ],
        out_shape=[
            jax.ShapeDtypeStruct((2 * pairs, rows, rows), BF),
            jax.ShapeDtypeStruct((rows, 3 * width), BF),
            jax.ShapeDtypeStruct((2 * pairs, 5, TILE, TILE), F32),
        ],
        scratch_shapes=[
            pltpu.VMEM((TILE, rows), F32),
        ],
        compiler_params=pltpu.CompilerParams(vmem_limit_bytes=VMEM),
        cost_estimate=FREE,
        name="attend_back",
    )(weights, qkv, qkv_t, qkv, dc, dct, ct)


def halves(pieces, whole, sems):
    rows = pieces[0].shape[0]
    return [(whole.at[pl.ds(half * rows, rows), :], sems.at[half]) for half in range(2)]


def load_whole(pieces, layer, where_ref, whole, sems):
    for half, (slot, sem) in enumerate(halves(pieces, whole, sems)):
        own_layer = where_ref[0] == layer
        own_half = where_ref[1] == half
        cases = (
            own_layer & own_half,
            own_layer & jnp.logical_not(own_half),
            jnp.logical_not(own_layer) & own_half,
            jnp.logical_not(own_layer) & jnp.logical_not(own_half),
        )
        for piece, case in zip(pieces, cases):

            @pl.when(case)
            def begin(piece=piece, slot=slot, sem=sem):
                pltpu.make_async_copy(piece, slot, sem).start()


def await_whole(pieces, whole, sems):
    for slot, sem in halves(pieces, whole, sems):
        pltpu.make_async_copy(pieces[0], slot, sem).wait()


def any_specs(count):
    return [pl.BlockSpec(memory_space=pl.ANY)] * count


SMEM_SPEC = pl.BlockSpec(memory_space=pltpu.SMEM)


def project_kernel(layer, where_ref, x_ref, bias_ref, m0, m1, m2, m3, o_ref, t_ref, whole, sems):
    step = pl.program_id(0)

    @pl.when(step == 0)
    def fetch():
        load_whole((m0, m1, m2, m3), layer, where_ref, whole, sems)
        await_whole((m0, m1, m2, m3), whole, sems)

    cols = o_ref.shape[1]
    at = pl.ds(pl.multiple_of(step * cols, cols), cols)
    value = (dot(x_ref[...], whole[:, at]) + bias_ref[0]).astype(BF)
    o_ref[...] = value
    t_ref[...] = jnp.transpose(value)


def project(where, x, bias, pieces, layer):
    rows = x.shape[0]
    half_rows, width = pieces[0].shape
    cols = 2 * TILE
    return pl.pallas_call(
        functools.partial(project_kernel, layer),
        grid=(width // cols,),
        in_specs=[
            SMEM_SPEC,
            pl.BlockSpec(x.shape, lambda g: (0, 0)),
            pl.BlockSpec((1, 1, cols), lambda g: (layer, 0, g)),
        ]
        + any_specs(4),
        out_specs=[
            pl.BlockSpec((rows, cols), lambda g: (0, g)),
            pl.BlockSpec((cols, rows), lambda g: (g, 0)),
        ],
        out_shape=[
            jax.ShapeDtypeStruct((rows, width), BF),
            jax.ShapeDtypeStruct((width, rows), BF),
        ],
        scratch_shapes=[pltpu.VMEM((2 * half_rows, width), BF), pltpu.SemaphoreType.DMA((2,))],
        compiler_params=pltpu.CompilerParams(vmem_limit_bytes=VMEM),
        cost_estimate=FREE,
        name="project",
    )(where, x, bias, *pieces)


def centre(values):
    width = values.shape[1]
    centered = values - jnp.sum(values, axis=1, keepdims=True) * (1.0 / width)
    square = jnp.sum(centered * centered, axis=1, keepdims=True) * (1.0 / width)
    scale = lax.rsqrt(square + EPS)
    return (centered * scale, scale)


def centre_back(grad, normed, scale):
    width = grad.shape[1]
    mean = jnp.sum(grad, axis=1, keepdims=True) * (1.0 / width)
    along = jnp.sum(grad * normed, axis=1, keepdims=True) * (1.0 / width)
    return scale * (grad - mean - normed * along)


def feed_kernel(layer, where_ref, ct_ref, x_ref, live_ref, vec_ref, wide_ref, *rest):
    pieces, rest = rest[:12], rest[12:]
    (n1_ref, s1_ref, hid_ref, tg_ref, slope_ref, n2_ref, s2_ref, y_ref), rest = rest[:8], rest[8:]
    w_out, w_in, w_back, sems = rest
    sets = (pieces[:4], pieces[4:8], pieces[8:])
    wholes = (w_out, w_in, w_back)

    def waits(start):
        @pl.when(pl.program_id(0) == 0)
        def _():
            if start is None:
                for n in range(3):
                    load_whole(sets[n], layer, where_ref, wholes[n], sems.at[n])
            else:
                await_whole(sets[start], wholes[start], sems.at[start])

    waits(None)
    mixed = jnp.transpose(ct_ref[...])
    waits(0)
    first = x_ref[...].astype(F32) + dot(mixed, w_out[...]) + vec_ref[0, 2:3, :]
    n1, s1 = centre(first)
    n1_ref[...] = n1
    s1_ref[...] = jnp.broadcast_to(s1, s1_ref.shape)
    hidden = n1 * vec_ref[0, 3:4, :] + vec_ref[0, 4:5, :]
    low = hidden.astype(BF)
    hid_ref[...] = low
    total = hidden + vec_ref[0, 9:10, :]
    waits(1)
    chunk = 6 * TILE
    for c in range(w_in.shape[1] // chunk):
        cols = slice(c * chunk, (c + 1) * chunk)
        u = dot(low, w_in[:, cols]) + wide_ref[0, :, cols]
        phi = 0.5 + 0.5 * lax.erf(u * ROOT_HALF)
        tg = (u * phi).astype(BF)
        tg_ref[:, cols] = tg
        slope_ref[:, cols] = (phi + u * (jnp.exp(-0.5 * u * u) * INV_ROOT_TAU)).astype(BF)
        if c == 0:
            waits(2)
        total = total + dot(tg, w_back[cols, :])
    n2, s2 = centre(total)
    n2_ref[...] = n2
    s2_ref[...] = jnp.broadcast_to(s2, s2_ref.shape)
    y = n2 * vec_ref[0, 10:11, :] + vec_ref[0, 11:12, :]
    y_ref[...] = jnp.where(live_ref[:, :1] > 0.0, y, 0.0).astype(BF)


def feed(where, ct, x, live, vec, wide, sets, layer):
    rows, width = x.shape
    ff = sets[1][0].shape[1]
    block = 2 * TILE
    row = lambda cols: pl.BlockSpec((block, cols), lambda g: (g, 0))
    shapes = [
        ((rows, width), F32), ((rows, TILE), F32), ((rows, width), BF), ((rows, ff), BF), ((rows, ff), BF),
        ((rows, width), F32), ((rows, TILE), F32), ((rows, width), BF),
    ]
    return pl.pallas_call(
        functools.partial(feed_kernel, layer),
        grid=(rows // block,),
        in_specs=[
            SMEM_SPEC,
            pl.BlockSpec((width, block), lambda g: (0, g)),
            row(width),
            row(TILE),
            pl.BlockSpec((1, *vec.shape[1:]), lambda g: (layer, 0, 0)),
            pl.BlockSpec((1, 1, ff), lambda g: (layer, 0, 0)),
        ]
        + any_specs(12),
        out_specs=[row(shape[1]) for shape, _ in shapes],
        out_shape=[jax.ShapeDtypeStruct(*s) for s in shapes],
        scratch_shapes=[
            pltpu.VMEM((width, width), BF),
            pltpu.VMEM((width, ff), BF),
            pltpu.VMEM((ff, width), BF),
            pltpu.SemaphoreType.DMA((3, 2)),
        ],
        compiler_params=pltpu.CompilerParams(vmem_limit_bytes=VMEM),
        cost_estimate=FREE,
        name="feed",
    )(where, ct, x, live, vec, wide, *sets[0], *sets[1], *sets[2])


def feed_back_kernel(layer, where_ref, dy_ref, live_ref, vec_ref, n1_ref, s1_ref, n2_ref, s2_ref, slope_ref, inv_ref, *rest):
    pieces, rest = rest[:12], rest[12:]
    (df_ref, du_ref, dr_ref, da_ref, dct_ref, dc_ref, sum_ref, wsum_ref), rest = rest[:8], rest[8:]
    w_back, w_in, w_out, sems = rest
    sets = (pieces[:4], pieces[4:8], pieces[8:])
    wholes = (w_back, w_in, w_out)

    def waits(start):
        @pl.when(pl.program_id(0) == 0)
        def _():
            if start is None:
                for n in range(3):
                    load_whole(sets[n], layer, where_ref, wholes[n], sems.at[n])
                sum_ref[...] = jnp.zeros_like(sum_ref)
                wsum_ref[...] = jnp.zeros_like(wsum_ref)
            else:
                await_whole(sets[start], wholes[start], sems.at[start])

    def add(row, value):
        sum_ref[row : row + 1, :] += jnp.sum(value, axis=0, keepdims=True)

    waits(None)
    dy = jnp.where(live_ref[:, :1] > 0.0, dy_ref[...].astype(F32), 0.0)
    n2 = n2_ref[...]
    add(4, dy * n2)
    add(5, dy)
    dr2 = centre_back(dy * vec_ref[0, 10:11, :], n2, s2_ref[:, :1])
    df = dr2.astype(BF)
    df_ref[...] = df
    add(3, df.astype(F32))
    total = dr2
    waits(0)
    chunk = 6 * TILE
    for c in range(w_in.shape[1] // chunk):
        cols = slice(c * chunk, (c + 1) * chunk)
        du = (dot_nt(df, w_back[cols, :]) * slope_ref[:, cols].astype(F32)).astype(BF)
        du_ref[:, cols] = du
        wsum_ref[:, cols] += jnp.sum(du.astype(F32), axis=0, keepdims=True)
        if c == 0:
            waits(1)
        total = total + dot_nt(du, w_in[:, cols])
    n1 = n1_ref[...]
    add(1, total * n1)
    add(2, total)
    dr1 = centre_back(total * vec_ref[0, 3:4, :], n1, s1_ref[:, :1])
    dr_ref[...] = dr1
    da = dr1.astype(BF)
    da_ref[...] = da
    add(0, da.astype(F32))
    waits(2)
    grad = dot_nt(w_out[...], da)
    for head in range(grad.shape[0] // HEAD_DIM):
        mine = slice(head * HEAD_DIM, (head + 1) * HEAD_DIM)
        inv = inv_ref[head // 2, head % 2 : head % 2 + 1, :]
        dct_ref[mine, :] = (grad[mine, :] * inv).astype(BF)
    dc_ref[...] = jnp.transpose(dct_ref[...])


def feed_back(where, dy, live, vec, n1, s1, n2, s2, slope, inv, sets, layer):
    rows, width = dy.shape
    ff = slope.shape[1]
    block = 2 * TILE
    row = lambda cols: pl.BlockSpec((block, cols), lambda g: (g, 0))
    outs = [
        ((rows, width), BF, row(width)), ((rows, ff), BF, row(ff)), ((rows, width), F32, row(width)),
        ((rows, width), BF, row(width)), ((width, rows), BF, pl.BlockSpec((width, block), lambda g: (0, g))),
        ((rows, width), BF, row(width)),
        ((8, width), F32, pl.BlockSpec((8, width), lambda g: (0, 0))),
        ((1, ff), F32, pl.BlockSpec((1, ff), lambda g: (0, 0))),
    ]
    return pl.pallas_call(
        functools.partial(feed_back_kernel, layer),
        grid=(rows // block,),
        in_specs=[
            SMEM_SPEC,
            row(width),
            row(TILE),
            pl.BlockSpec((1, *vec.shape[1:]), lambda g: (layer, 0, 0)),
            row(width),
            row(TILE),
            row(width),
            row(TILE),
            row(ff),
            pl.BlockSpec((inv.shape[0], 8, block), lambda g: (0, 0, g)),
        ]
        + any_specs(12),
        out_specs=[o[2] for o in outs],
        out_shape=[jax.ShapeDtypeStruct(o[0], o[1]) for o in outs],
        scratch_shapes=[
            pltpu.VMEM((ff, width), BF),
            pltpu.VMEM((width, ff), BF),
            pltpu.VMEM((width, width), BF),
            pltpu.SemaphoreType.DMA((3, 2)),
        ],
        compiler_params=pltpu.CompilerParams(vmem_limit_bytes=VMEM),
        cost_estimate=FREE,
        name="feed_back",
    )(where, dy, live, vec, n1, s1, n2, s2, slope, inv, *sets[0], *sets[1], *sets[2])


def input_back_kernel(layer, where_ref, d_ref, dr_ref, m0, m1, m2, m3, o_ref, sum_ref, whole, sems):
    step = pl.program_id(0)

    @pl.when(step == 0)
    def fetch():
        load_whole((m0, m1, m2, m3), layer, where_ref, whole, sems)
        await_whole((m0, m1, m2, m3), whole, sems)
        sum_ref[...] = jnp.zeros_like(sum_ref)

    d = d_ref[...]
    sum_ref[...] += jnp.sum(d.astype(F32), axis=0, keepdims=True)
    o_ref[...] = (dr_ref[...] + dot_nt(d, whole[...])).astype(BF)


def input_back(where, dqkv, dr1, pieces, layer):
    rows, wide = dqkv.shape
    width = dr1.shape[1]
    block = 2 * TILE
    row = lambda cols: pl.BlockSpec((block, cols), lambda g: (g, 0))
    return pl.pallas_call(
        functools.partial(input_back_kernel, layer),
        grid=(rows // block,),
        in_specs=[SMEM_SPEC, row(wide), row(width)] + any_specs(4),
        out_specs=[row(width), pl.BlockSpec((1, wide), lambda g: (0, 0))],
        out_shape=[jax.ShapeDtypeStruct((rows, width), BF), jax.ShapeDtypeStruct((1, wide), F32)],
        scratch_shapes=[pltpu.VMEM((width, wide), BF), pltpu.SemaphoreType.DMA((2,))],
        compiler_params=pltpu.CompilerParams(vmem_limit_bytes=VMEM),
        cost_estimate=FREE,
        name="input_back",
    )(where, dqkv, dr1, *pieces)


def bucket_tree(delta, total, reach):
    half = total // 2
    exact = half // 2
    limits = bucket_limits(total, reach)
    dist = jnp.abs(delta)

    def count(low, high):
        if high - low == 1:
            return jnp.where(dist >= limits[low], 1, 0)
        middle = (low + high) // 2
        above = dist >= limits[middle]
        return jnp.where(above, middle - low + 1 + count(middle + 1, high), count(low, middle))

    bucket = jnp.where(dist < exact, dist, exact + count(0, len(limits)))
    return bucket + jnp.where(delta > 0, half, 0)


def prepare_kernel(where_ref, text_ref, patch_ref, x_ref, y_ref, across_ref, upward_ref, mask_ref, live_ref):
    rows = across_ref.shape[0]
    doc = where_ref[0]
    half = where_ref[1]
    text = text_ref[half, doc]
    patches = patch_ref[half, doc]
    lane = lax.broadcasted_iota(jnp.int32, (TILE, TILE), 1)
    for ref, out, base in ((x_ref, across_ref, 0), (y_ref, upward_ref, REL2)):
        line = ref[pl.ds(half * 2 + doc, 1), :]
        for r in range(rows // TILE):
            part = jnp.broadcast_to(line[:, r * TILE : (r + 1) * TILE], (TILE, TILE))
            column = jnp.transpose(part.astype(F32)).astype(jnp.int32)
            for c in range(rows // TILE):
                cols = slice(c * TILE, (c + 1) * TILE)
                out[r * TILE : (r + 1) * TILE, cols] = bucket_tree(column - line[:, cols], REL2, REACH2) + base
    index = lax.broadcasted_iota(jnp.int32, (rows, TILE), 0)
    live = (index < text) | ((index >= TEXT_MAX) & (index < TEXT_MAX + 1 + patches))
    first = lax.broadcasted_iota(jnp.int32, (rows, TILE), 1) == 0
    live_ref[...] = jnp.where(live, 1.0, 0.0)
    mask_ref[...] = jnp.where(first & jnp.logical_not(live), NEG * UNIT, 0.0).astype(BF)


def prepare(where, text_len, patches, box_x, box_y):
    rows = box_x.shape[2]
    flat = lambda a: a.reshape(-1, rows)
    vmem = pl.BlockSpec(memory_space=pltpu.VMEM)
    return pl.pallas_call(
        prepare_kernel,
        in_specs=[SMEM_SPEC] * 3 + [vmem] * 2,
        out_specs=[vmem] * 4,
        out_shape=[
            jax.ShapeDtypeStruct((rows, rows), jnp.int32),
            jax.ShapeDtypeStruct((rows, rows), jnp.int32),
            jax.ShapeDtypeStruct((rows, TILE), BF),
            jax.ShapeDtypeStruct((rows, TILE), F32),
        ],
        compiler_params=pltpu.CompilerParams(vmem_limit_bytes=VMEM),
        cost_estimate=FREE,
        name="prepare",
    )(where, text_len, patches, flat(box_x), flat(box_y))


def table_kernel(first_ref, second_ref, x_ref, y_ref, o_ref, scr):
    heads, block, rows = first_ref.shape
    parts = rows // TILE

    @pl.when(pl.program_id(0) == 0)
    def start():
        o_ref[...] = jnp.zeros_like(o_ref)
        scr[...] = jnp.zeros_like(scr)

    for layer, ref in enumerate((first_ref, second_ref)):
        for head in range(heads):
            wide = ref[head].astype(F32)
            at = (layer * heads + head) * block
            for c in range(parts):
                scr[c, at : at + block, :] = wide[:, c * TILE : (c + 1) * TILE]
    index = lax.broadcasted_iota(jnp.int32, (REL2, rows), 0)
    total = o_ref[...]
    for j in range(block):
        grads = jnp.concatenate(
            [scr[c, pl.ds(j, 32, stride=block), :] for c in range(parts)], axis=1
        ).astype(BF)
        row_x = jnp.broadcast_to(x_ref[j : j + 1, :], (REL2, rows))
        row_y = jnp.broadcast_to(y_ref[j : j + 1, :], (REL2, rows))
        hot = jnp.concatenate(
            [
                jnp.where(row_x == index, 1.0, 0.0).astype(BF),
                jnp.where(row_y == index + REL2, 1.0, 0.0).astype(BF),
            ],
            axis=0,
        )
        total = total + dot_nt(grads, hot)
    o_ref[...] = total


def table_sums(first, second, across, upward, part, parts):
    heads, rows, _ = first.shape
    block = 32
    count = rows // block // parts
    at = part * count
    return pl.pallas_call(
        table_kernel,
        grid=(count,),
        in_specs=[
            pl.BlockSpec((heads, block, rows), lambda g: (0, at + g, 0)),
            pl.BlockSpec((heads, block, rows), lambda g: (0, at + g, 0)),
            pl.BlockSpec((block, rows), lambda g: (at + g, 0)),
            pl.BlockSpec((block, rows), lambda g: (at + g, 0)),
        ],
        out_specs=pl.BlockSpec((32, 2 * REL2), lambda g: (0, 0)),
        out_shape=jax.ShapeDtypeStruct((32, 2 * REL2), F32),
        scratch_shapes=[pltpu.VMEM((rows // TILE, 32 * block, TILE), F32)],
        compiler_params=pltpu.CompilerParams(vmem_limit_bytes=VMEM),
        cost_estimate=FREE,
        name="table_sums",
    )(first, second, across, upward)


class Place:
    def __init__(self):
        index = lax.axis_index("section")
        self.peers = lax.axis_size("section")
        self.docs = lax.axis_size("dp")
        self.half = index % 2
        self.layer = index // 2
        where = lax.axis_index("dp")
        bits = range(self.docs.bit_length() - 1)
        self.orders = [list(bits), [1, 0] + list(bits)[2:]]
        self.sides = [
            jnp.where(self.half == 0, (where >> one) & 1, (where >> two) & 1)
            for one, two in zip(*self.orders)
        ]

    def across(self, value, mask):
        return lax.ppermute(value, "section", [(i, i ^ mask) for i in range(self.peers)])

    def to_layer(self, value, layer):
        other = 1 - layer
        pairs = [(2 * other + h, 2 * layer + h) for h in range(2)]
        return lax.ppermute(value, "section", pairs)

    def facing(self, value, step):
        pairs = []
        for s in range(self.peers):
            for d in range(self.docs):
                pairs.append((s * self.docs + d, s * self.docs + (d ^ (1 << self.orders[s % 2][step]))))
        return lax.ppermute(value, ("section", "dp"), pairs)

    def joined(self, mine, theirs, side):
        return jnp.where(
            side == 0, jnp.concatenate([mine, theirs], 0), jnp.concatenate([theirs, mine], 0)
        )

    def parted(self, value, side):
        rows = value.shape[0] // 2
        return (
            lax.dynamic_slice_in_dim(value, side * rows, rows, 0),
            lax.dynamic_slice_in_dim(value, (1 - side) * rows, rows, 0),
        )


    def over_core(self, value):
        return (value, lambda sent: self.across(sent, 1))

    def over_x(self, value):
        return (value, lambda sent: self.across(sent, 2))

    def over_dp(self, value, step):
        return (value, lambda sent: self.facing(sent, step))

    def weight_flow(self, mine, steps):
        part = mine.shape[0] >> steps
        spot = sum(side << step for step, side in enumerate(self.sides[:steps]))
        mate = self.across(mine, 1)
        got = yield self.over_x(lax.dynamic_slice_in_dim(mine, spot * part, part, 0))
        for step in range(steps):
            got = self.joined(got, (yield self.over_dp(got, step)), self.sides[step])
        return (mine, mate, got, (yield self.over_core(got)))

    def scatter_flow(self, full):
        size = full.shape[0]
        terms = [(full.astype(BF), 0)]

        def added(offset):
            parts = [lax.dynamic_slice_in_dim(array, at + offset, size, 0) for array, at in terms]
            if len(parts) == 1:
                return parts[0]
            return sum(part.astype(F32) for part in parts).astype(BF)

        moves = [self.over_core]
        moves += [functools.partial(self.over_dp, step=step) for step in range(len(self.sides))]
        for side, move in zip([self.half] + self.sides, moves):
            size //= 2
            arrived = yield move(added((1 - side) * size))
            terms = [(array, at + side * size) for array, at in terms] + [(arrived, 0)]
        return added(0)

    def gather_flow(self, second, first):
        mine = jnp.where(self.layer == 1, second, first)
        sent = yield self.over_x(jnp.where(self.layer == 1, first, second))
        total = (mine.astype(F32) + sent.astype(F32)).astype(BF)
        for step, side in reversed(list(enumerate(self.sides))):
            total = self.joined(total, (yield self.over_dp(total, step)), side)
        return total.astype(F32)

    def all_flow(self, value):
        for over in (self.over_core, self.over_x):
            value = value + (yield over(value))
        for step in range(len(self.sides)):
            value = value + (yield self.over_dp(value, step))
        return value


class Flow:
    def __init__(self, steps):
        self.steps = steps
        self.air = self.result = None
        self.ready, self.move = next(steps)

    def land(self, arrived):
        self.air = None
        try:
            self.ready, self.move = self.steps.send(arrived)
        except StopIteration as end:
            self.ready = self.move = None
            self.result = end.value

    @property
    def busy(self):
        return self.air is not None or self.ready is not None


def pace(value, *flows):
    flows = [flow for flow in flows if flow.busy]
    flying = [flow for flow in flows if flow.air is not None]
    value, air = lax.optimization_barrier((value, [flow.air for flow in flying]))
    for flow, arrived in zip(flying, air):
        flow.land(arrived)
    flows = [flow for flow in flows if flow.busy]
    value, ready = lax.optimization_barrier((value, [flow.ready for flow in flows]))
    for flow, sent in zip(flows, ready):
        flow.air, flow.ready = flow.move(sent), None
    return value


def finished(flow):
    while flow.busy:
        pace(0, flow)
    return flow.result


def score_tables(quarters):
    count, _, _, heads = quarters.shape
    cut = REL1 // 2
    box = quarters[:, :, cut:, :].astype(F32).reshape(count, 2, 2, REL2 // 2, heads)
    box = jnp.transpose(box, (0, 4, 2, 1, 3)).reshape(count, heads // 2, 2, 2 * REL2)
    fixed = jnp.round(box * UNIT).astype(jnp.int32)
    tabs = fixed[:, :, :1] * 65536 + fixed[:, :, 1:] + 16384
    chosen = np.concatenate([line_rows(), np.zeros((3, 2 * TILE), int)]).reshape(-1)
    hot = jnp.asarray(chosen[None, :] == np.arange(REL1)[:, None], BF)
    line = quarters[:, :, :cut, :].reshape(count, REL1, heads)
    lines = lax.dot_general(line, hot, (((1,), (0,)), ((), ())), preferred_element_type=F32)
    odd = (jnp.arange(heads) % 2).astype(F32)[:, None]
    lines = (lines * UNIT - odd * 32768.0).reshape(count, heads, 8, 2 * TILE)
    return (tabs, lines)


def packed(vectors, tables):
    wide = vectors[1].shape[-1]
    rows = [v.reshape(-1, wide) for v in vectors]
    rows.append(jnp.zeros((4, wide), rows[0].dtype))
    table = jnp.concatenate(tables, axis=0)
    rows.append(jnp.pad(table, ((0, 0), (0, wide - table.shape[1]))))
    return jnp.concatenate(rows, axis=0)


def unpacked(quarters, heads):
    wide = quarters.shape[-1]
    v = quarters[:, :, :16].astype(F32)
    rows = jnp.transpose(v, (0, 2, 1, 3)).reshape(2, 16, 2 * wide)
    b_in = v[:, :, 5:9].reshape(2, 1, 8 * wide)
    b_qv = v[:, :, :2].reshape(2, 2, 2 * wide)
    bias = jnp.concatenate([b_qv[:, :1], jnp.zeros_like(b_qv[:, :1]), b_qv[:, 1:]], axis=2)
    return (rows, b_in, bias), quarters[:, :, 16:, :heads]


def local(
    section_data,
    text_len,
    patches,
    box_x,
    box_y,
    w_qkv,
    b_qv,
    w_out,
    b_out,
    norm1_gain,
    norm1_bias,
    w_in,
    b_in,
    w_back,
    b_back,
    norm2_gain,
    norm2_bias,
    rel_line,
    rel_x,
    rel_y,
):
    place = Place()
    heads = rel_line.shape[2]
    rows, width = section_data.shape[2:]
    first = place.layer == 0
    where = jnp.stack([place.layer, place.half]).astype(jnp.int32)

    entries = section_data[0]
    wf_qkv = Flow(place.weight_flow(w_qkv[0], 2))
    boxes = pace((text_len, patches, box_x, box_y), wf_qkv)
    meta = prepare(where, *boxes)
    smalls = (b_qv, b_out, norm1_gain, norm1_bias, b_in, b_back, norm2_gain, norm2_bias)
    smalls += (rel_line, rel_x, rel_y)
    swapped = jnp.where(first, entries[1], entries[0])
    meta, smalls, swapped = pace((meta, smalls, swapped), wf_qkv)
    across, upward, mask, live = meta
    got = place.across(swapped, 2)
    smalls = packed([v[0] for v in smalls[:8]], [t[0] for t in smalls[8:]])
    w_rest = (w_out, w_in, w_back)
    smalls, theirs, w_rest = pace((smalls, place.across(smalls, 1), w_rest), wf_qkv)
    wf_out, wf_in, wf_back = [Flow(place.weight_flow(w[0], 1)) for w in w_rest]
    smalls = place.joined(smalls[None], theirs[None], place.half)
    smalls, theirs, got = pace((smalls, place.across(smalls, 2), got), wf_qkv, wf_out, wf_in)
    smalls = place.joined(smalls[None], theirs[None], place.layer)
    (vectors, b_in, b_qv), tables = unpacked(smalls, heads)
    scores = score_tables(tables)
    source = jnp.where(first, entries[0], got)
    cotangent = jnp.where(first, got, entries[1])
    source, cotangent, scores = pace((source, cotangent, scores), wf_qkv, wf_back)
    w_qkv = finished(wf_qkv)

    def forward(x, n, calls, paced):
        qkv, qkv_t = paced(project(where, x, b_qv, w_qkv, n), wf_out, wf_in)
        mixed = ()
        for part in range(calls):
            mixed = attend(
                qkv, qkv_t, mask, across, upward, scores[0][n], scores[1][n], calls, part, mixed
            )
            mixed = paced(mixed, wf_out, wf_in, wf_back)
        mixed = paced(mixed, wf_back)
        weights, ct, exact, inv = mixed
        sets = [finished(flow) for flow in (wf_out, wf_in, wf_back)]
        n1, s1, hidden, tg, slope, n2, s2, y = feed(where, ct, x, live, vectors, b_in, sets, n)
        return dict(
            x=x, qkv=qkv, qkv_t=qkv_t, weights=weights, ct=ct, exact=exact, inv=inv,
            n1=n1, s1=s1, hidden=hidden, tg=tg, slope=slope, n2=n2, s2=s2, y=y,
        )

    kept = [forward(source, 0, 2, pace)]
    kept.append(forward(kept[0]["y"], 1, 1, lambda value, *flows: value))
    w_out, w_in, w_back = [finished(flow) for flow in (wf_out, wf_in, wf_back)]

    def feed_grads(dy, n):
        k = kept[n]
        return feed_back(
            where, dy, live, vectors, k["n1"], k["s1"], k["n2"], k["s2"], k["slope"], k["inv"],
            (w_back, w_in, w_out), n,
        )

    def scores_back(dc, dct, n):
        k = kept[n]
        return attend_back(k["weights"], k["qkv"], k["qkv_t"], dc, dct, k["exact"])

    def back_grad(df, n):
        return Flow(place.scatter_flow(dot_tn(kept[n]["tg"], df)))

    def in_grad(du, n):
        return Flow(place.scatter_flow(dot_tn(kept[n]["hidden"], du)))

    def mixing_grad(dqkv, da, n):
        g_qkv = dot_tn(kept[n]["x"], dqkv)
        g_out = dot(kept[n]["ct"], da)
        return Flow(place.scatter_flow(jnp.concatenate([g_qkv, g_out], axis=1)))

    def vector_rows(sums, wide, qkv):
        return jnp.concatenate([sums, wide.reshape(-1, width), qkv.reshape(-1, width)], axis=0)

    df, du, dr, da, dct, dc, sums, wide = feed_grads(cotangent, 1)
    f_back = back_grad(df, 1)
    du = pace(du, f_back)
    f_in = in_grad(du, 1)
    dc, dct = pace((dc, dct), f_back, f_in)
    ds1, dqkv, line1 = pace(scores_back(dc, dct, 1), f_back, f_in)
    f_mix = mixing_grad(dqkv, da, 1)
    dqkv = pace(dqkv, f_back, f_in, f_mix)
    dx, s_qkv = input_back(where, dqkv, dr, w_qkv, 1)
    vectors1 = vector_rows(sums, wide, s_qkv)

    dx = pace(dx, f_in, f_mix)
    df, du, dr, da, dct, dc, sums, wide = pace(feed_grads(dx, 0), f_back, f_in, f_mix)
    e_back = back_grad(df, 0)
    du = pace(du, f_mix, e_back)
    e_in = in_grad(du, 0)
    dc, dct = pace((dc, dct), f_in, f_mix, e_back, e_in)
    ds0, dqkv, line0 = pace(scores_back(dc, dct, 0), f_mix, e_back, e_in)
    e_mix = mixing_grad(dqkv, da, 0)
    stores = (ds0, ds1)
    stores, dqkv = pace((stores, dqkv), e_back, e_mix)

    parts = 8
    table = 0.0

    def tabled(part, *flows):
        more = table_sums(*stores, across, upward, part, parts)
        return pace((table + more, stores), *flows)

    table, stores = tabled(0, e_in, e_mix)
    table, stores = tabled(1, e_back, e_in)
    s_back = Flow(place.gather_flow(finished(f_back), finished(e_back)))
    table, stores = pace((table, stores), s_back)
    table, stores = tabled(2, e_mix, s_back)
    table, stores = tabled(3, e_in, e_mix)
    s_in = Flow(place.gather_flow(finished(f_in), finished(e_in)))
    table, stores = pace((table, stores), s_in)
    table, stores = tabled(4, s_back, s_in)
    table, stores = tabled(5, e_mix, s_back)
    s_mix = Flow(place.gather_flow(finished(f_mix), finished(e_mix)))
    table, stores = pace((table, stores), s_mix)
    table, stores = tabled(6, s_mix, s_in)
    more = table_sums(*stores, across, upward, 7, parts)
    dqkv, table, more = pace((dqkv, table, more), s_back, s_in)
    table = table + more
    dx, s_qkv = input_back(where, dqkv, dr, w_qkv, 0)
    vectors0 = vector_rows(sums, wide, s_qkv)
    sent = place.across(jnp.where(first, kept[1]["y"], dx), 2)
    hot = jnp.asarray(line_tiles().reshape(-1)[:, None] == np.arange(REL1)[None, :], BF)
    lines = jnp.concatenate([line0, line1], axis=0).reshape(2 * heads, -1).astype(BF)
    lines = jnp.pad(dot(lines, hot), ((0, 32 - 2 * heads), (0, 0)))
    tables = jnp.concatenate([table, lines], axis=1)
    tables = jnp.pad(tables, ((0, 0), (0, width - tables.shape[1])))
    smalls = jnp.concatenate([vectors0, vectors1, tables], axis=0)
    a_small = Flow(place.all_flow(smalls))
    token = pace(dx, s_mix, a_small)
    token = pace(token, s_mix, s_in, a_small)
    flows = [s_back, s_in, s_mix, a_small]
    while any(flow.busy for flow in flows):
        token = pace(token, *flows)
    g_back, g_in, g_mix = s_back.result, s_in.result, s_mix.result
    g_qkv, g_out = g_mix[:, : 3 * width], g_mix[:, 3 * width :]

    count = vectors0.shape[0]
    v = lax.dynamic_slice_in_dim(a_small.result, place.layer * count, count, 0)
    half_width = width // 2
    v_half = lax.dynamic_slice_in_dim(v, place.half * half_width, half_width, 1)
    v_in = lax.dynamic_slice_in_dim(v, 8 + 2 * place.half, 2, 0).reshape(1, -1)
    v_qv = lax.dynamic_slice_in_dim(v, 12 + 2 * place.half, 1, 0)
    t = lax.dynamic_slice_in_dim(a_small.result, 2 * count + place.layer * heads, heads, 0).T

    def table_half(at, size):
        return lax.dynamic_slice_in_dim(t, at + place.half * size, size, 0)[None]

    t_x, t_y = table_half(0, REL2 // 2), table_half(REL2, REL2 // 2)
    t_line = table_half(2 * REL2, REL1 // 2)
    result = jnp.where(first, jnp.stack([dx, sent]), jnp.stack([sent, kept[1]["y"]]))[None]
    return (
        result, g_qkv[None], v_qv, g_out[None], v_half[0:1], v_half[1:2], v_half[2:3],
        g_in[None], v_in, g_back[None], v_half[3:4], v_half[4:5], v_half[5:6],
        t_line, t_x, t_y,
    )


def solution(mesh):
    matrix = P("section", None, None)
    vector = P("section", None)
    weights = (
        matrix, vector, matrix, vector, vector, vector, matrix, vector, matrix,
        vector, vector, vector, matrix, matrix, matrix,
    )
    data = P("section", "dp", None, None)
    return jax.shard_map(
        local,
        mesh=mesh,
        in_specs=(data, P(None, "dp"), P(None, "dp"), P(None, "dp", None), P(None, "dp", None))
        + weights,
        out_specs=(data,) + weights,
        check_vma=False,
    )
```

```python
import functools
import math

import jax
import jax.numpy as jnp
import numpy as np
from jax import lax
from jax.experimental import pallas as pl
from jax.experimental.pallas import tpu as pltpu
from jax.sharding import PartitionSpec as P

REL1 = 32
REL2 = 64
REACH1 = 128
REACH2 = 256
HEAD_DIM = 64
TEXT_MAX = 191
EPS = 1e-05
NEG = -1000000000.0
ROOT_HALF = 0.7071067811865476
INV_ROOT_TAU = 0.3989422804014327

UNIT = 4096.0
LOG2E = 1.4426950408889634
TILE = 128
VMEM = 60 * 2**20


def cost(us):
    return pl.CostEstimate(flops=int(us * 10**9), bytes_accessed=int(us * 10**6), transcendentals=0)


BF = jnp.bfloat16
F32 = jnp.float32
NT = (((1,), (1,)), ((), ()))
TN = (((0,), (0,)), ((), ()))


def dot(a, b):
    return jnp.dot(a, b, preferred_element_type=F32)


def dot_nt(a, b):
    return lax.dot_general(a, b, NT, preferred_element_type=F32)


def dot_tn(a, b):
    return lax.dot_general(a, b, TN, preferred_element_type=F32)


def bucket_limits(total, reach):
    half = total // 2
    exact = half // 2
    return [
        int(math.ceil(exact * (reach / exact) ** (step / (half - exact)) - 1e-09))
        for step in range(1, half - exact)
    ]


def line_bucket_np(delta):
    half = REL1 // 2
    exact = half // 2
    dist = np.abs(delta)
    far = np.full(dist.shape, exact)
    for limit in bucket_limits(REL1, REACH1):
        far = far + (dist >= limit)
    return np.where(delta > 0, half, 0) + np.where(dist < exact, dist, far)


def line_rows():
    k = np.arange(2 * TILE)
    shift = np.where(k < TILE, k, k - 2 * TILE)
    return line_bucket_np(np.stack([TILE * (s - 2) - shift for s in range(5)]))


def line_tiles():
    r = np.arange(TILE)
    return line_bucket_np(np.stack([TILE * (s - 2) + r[:, None] - r[None, :] for s in range(5)]))


def lane_pick(table, index):
    dims = lax.GatherDimensionNumbers(
        offset_dims=(),
        collapsed_slice_dims=(1,),
        start_index_map=(1,),
        operand_batching_dims=(0,),
        start_indices_batching_dims=(0,),
    )
    return lax.gather(
        table,
        index[..., None],
        dims,
        slice_sizes=(1, 1),
        mode=lax.GatherScatterMode.PROMISE_IN_BOUNDS,
    )


def attend_kernel(
    k_ref,
    qt_ref,
    vt_ref,
    mask_ref,
    x_ref,
    y_ref,
    tab_ref,
    line_ref,
    p_ref,
    c_ref,
    exact_ref,
    inv_ref,
    kaug,
    qaug,
    strip,
    scores,
):
    rows = k_ref.shape[0]
    chunk = 2 * TILE
    step = 32
    lane = lax.broadcasted_iota(jnp.int32, (rows, TILE), 1)
    keys = k_ref[...].astype(F32) * (UNIT / 8.0)
    kaug[0, :, :TILE] = jnp.where(lane < HEAD_DIM, keys, 0.0).astype(BF)
    kaug[1, :, :TILE] = jnp.where(lane < HEAD_DIM, 0.0, keys).astype(BF)
    kaug[0, :, TILE:] = mask_ref[...]
    kaug[1, :, TILE:] = mask_ref[...]
    qaug[:TILE, :] = qt_ref[...]
    qaug[TILE:, :] = jnp.ones((TILE, rows), BF)
    for head in range(2):
        for s in range(5):
            wide = jnp.broadcast_to(line_ref[head, s : s + 1, :], (TILE, 2 * TILE))
            if s in (1, 2, 3):
                wide = pltpu.roll(wide, 0, axis=1, stride=1, stride_axis=0)
            strip[head, s] = wide[:, :TILE]
    table = jnp.broadcast_to(tab_ref[0], (step, TILE))
    chunks = rows // chunk
    low = jnp.full((8, chunk), -3e38, F32)

    def score(t, n, peaks):
        cols = slice(t * chunk, (t + 1) * chunk)
        tile = pl.ds(pl.multiple_of(n * TILE, TILE), TILE)
        raw = [dot(kaug[head, tile, :], qaug[:, cols]) for head in range(2)]
        peaks = list(peaks)
        for m in range(TILE // step):
            at = pl.ds(pl.multiple_of(n * TILE + m * step, step), step)
            sub = slice(m * step, (m + 1) * step)
            parts = ([], [])
            for part in range(2):
                lanes = slice(part * TILE, (part + 1) * TILE)
                wide = slice(t * chunk + part * TILE, t * chunk + (part + 1) * TILE)
                both = lane_pick(table, x_ref[at, wide]) + lane_pick(table, y_ref[at, wide])
                off = jnp.clip(n - (2 * t + part), -2, 2) + 2
                for head, bits in ((0, both >> 16), (1, both & 0xFFFF)):
                    value = raw[head][sub, lanes] + strip[head, off, sub, :] + bits.astype(F32)
                    scores[t % 2, head, at, lanes] = value
                    parts[head].append(value)
            for head in range(2):
                wide = jnp.concatenate(parts[head], axis=1)
                for r in range(step // 8):
                    peaks[head] = jnp.maximum(peaks[head], wide[8 * r : 8 * r + 8, :])
        return tuple(peaks)

    def weigh(t, n, peaks):
        cols = slice(t * chunk, (t + 1) * chunk)
        for m in range(TILE // step):
            at = pl.ds(pl.multiple_of(n * TILE + m * step, step), step)
            for head in range(2):
                power = (scores[t % 2, head, at, :] - peaks[head]) * (LOG2E / UNIT)
                p_ref[head, at, cols] = jnp.exp2(power).astype(BF)

    ones = jnp.ones((16, rows), BF)

    def mix(t):
        cols = slice(t * chunk, (t + 1) * chunk)
        for head in range(2):
            mine = slice(head * HEAD_DIM, (head + 1) * HEAD_DIM)
            vals = jnp.concatenate([vt_ref[mine, :], ones], axis=0)
            mixed = dot(vals, p_ref[head, :, cols])
            inv = 1.0 / mixed[HEAD_DIM : HEAD_DIM + 1, :]
            exact = mixed[:HEAD_DIM, :] * inv
            exact_ref[mine, cols] = exact
            c_ref[mine, cols] = exact.astype(BF)
            inv_ref[0, head : head + 1, cols] = inv

    peaks = None
    for t in range(chunks + 1):
        old = peaks

        def both_steps(n, tops):
            if t < chunks:
                tops = score(t, n, tops)
            if t > 0:
                weigh(t - 1, n, old)
            return tops

        tops = lax.fori_loop(0, rows // TILE, both_steps, (low, low), unroll=6)
        peaks = [jnp.max(top, axis=0, keepdims=True) for top in tops]
        if t > 0:
            mix(t - 1)

def attend(qkv, qkv_t, mask, across, upward, tabs, lines, calls=1, part=0, before=()):
    rows = qkv.shape[0]
    width = qkv.shape[1] // 3
    pairs = width // TILE
    count = pairs // calls
    at = part * count
    whole = lambda p: (0, 0)
    kernel = attend_kernel
    if before:
        kernel = lambda *refs: attend_kernel(*refs[:8], *refs[12:])
    return pl.pallas_call(
        kernel,
        grid=(count,),
        in_specs=[
            pl.BlockSpec((rows, TILE), lambda p: (0, pairs + at + p)),
            pl.BlockSpec((TILE, rows), lambda p: (at + p, 0)),
            pl.BlockSpec((TILE, rows), lambda p: (2 * pairs + at + p, 0)),
            pl.BlockSpec((rows, TILE), whole),
            pl.BlockSpec((rows, rows), whole),
            pl.BlockSpec((rows, rows), whole),
            pl.BlockSpec((1, 1, TILE), lambda p: (at + p, 0, 0)),
            pl.BlockSpec((2, 8, 2 * TILE), lambda p: (at + p, 0, 0)),
        ]
        + [pl.BlockSpec(memory_space=pl.ANY) for _ in before],
        out_specs=[
            pl.BlockSpec((2, rows, rows), lambda p: (at + p, 0, 0)),
            pl.BlockSpec((TILE, rows), lambda p: (at + p, 0)),
            pl.BlockSpec((TILE, rows), lambda p: (at + p, 0)),
            pl.BlockSpec((1, 8, rows), lambda p: (at + p, 0, 0)),
        ],
        out_shape=[
            jax.ShapeDtypeStruct((2 * pairs, rows, rows), BF),
            jax.ShapeDtypeStruct((width, rows), BF),
            jax.ShapeDtypeStruct((width, rows), F32),
            jax.ShapeDtypeStruct((pairs, 8, rows), F32),
        ],
        scratch_shapes=[
            pltpu.VMEM((2, rows, 2 * TILE), BF),
            pltpu.VMEM((2 * TILE, rows), BF),
            pltpu.VMEM((2, 5, TILE, TILE), F32),
            pltpu.VMEM((2, 2, rows, 2 * TILE), F32),
        ],
        input_output_aliases={8 + n: n for n in range(len(before))},
        compiler_params=pltpu.CompilerParams(vmem_limit_bytes=VMEM),
        cost_estimate=cost(33 / calls),
        name="attend",
    )(qkv, qkv_t, qkv_t, mask, across, upward, tabs, lines, *before)


def attend_back_kernel(
    p_ref,
    q_ref,
    kt_ref,
    v_ref,
    dc_ref,
    dct_ref,
    ct_ref,
    ds_ref,
    d_ref,
    line_ref,
    dqt,
):
    rows = q_ref.shape[0]
    line_ref[...] = jnp.zeros_like(line_ref)
    product = dct_ref[...].astype(F32) * ct_ref[...]
    lane = lax.broadcasted_iota(jnp.int32, (rows, TILE), 1)
    vals = v_ref[...]
    out_k, out_v = [], []
    for head in range(2):
        mine = slice(head * HEAD_DIM, (head + 1) * HEAD_DIM)
        delta = jnp.sum(product[mine, :], axis=0, keepdims=True)
        own = (lane < HEAD_DIM) if head == 0 else (lane >= HEAD_DIM)
        picked = jnp.where(own, vals, jnp.zeros_like(vals))
        for n in range(rows // TILE):
            at = slice(n * TILE, (n + 1) * TILE)
            dp = dot(picked[at, :], dct_ref[...])
            sums = {}
            for part in range(rows // TILE):
                lanes = slice(part * TILE, (part + 1) * TILE)
                weights = p_ref[head, at, lanes].astype(F32)
                grad = weights * (dp[:, lanes] - delta[:, lanes])
                ds_ref[head, at, lanes] = grad.astype(BF)
                off = min(max(n - part, -2), 2) + 2
                sums[off] = grad if off not in sums else sums[off] + grad
            for off, value in sums.items():
                line_ref[head, off] += value
        out_k.append(dot(ds_ref[head], q_ref[...]))
        out_v.append(dot(p_ref[head], dc_ref[...]))
        dqt[mine, :] = dot(kt_ref[mine, :], ds_ref[head])
    width = d_ref.shape[1] // 3
    base = pl.multiple_of(pl.program_id(0) * TILE, TILE)
    d_ref[:, pl.ds(width + base, TILE)] = (
        jnp.where(lane < HEAD_DIM, out_k[0], out_k[1]) * 0.125
    ).astype(BF)
    d_ref[:, pl.ds(2 * width + base, TILE)] = jnp.where(lane < HEAD_DIM, out_v[0], out_v[1]).astype(BF)
    d_ref[:, pl.ds(base, TILE)] = (jnp.transpose(dqt[...]) * 0.125).astype(BF)


def attend_back(weights, qkv, qkv_t, dc, dct, ct):
    rows = qkv.shape[0]
    width = qkv.shape[1] // 3
    pairs = width // TILE
    return pl.pallas_call(
        attend_back_kernel,
        grid=(pairs,),
        in_specs=[
            pl.BlockSpec((2, rows, rows), lambda p: (p, 0, 0)),
            pl.BlockSpec((rows, TILE), lambda p: (0, p)),
            pl.BlockSpec((TILE, rows), lambda p: (pairs + p, 0)),
            pl.BlockSpec((rows, TILE), lambda p: (0, 2 * pairs + p)),
            pl.BlockSpec((rows, TILE), lambda p: (0, p)),
            pl.BlockSpec((TILE, rows), lambda p: (p, 0)),
            pl.BlockSpec((TILE, rows), lambda p: (p, 0)),
        ],
        out_specs=[
            pl.BlockSpec((2, rows, rows), lambda p: (p, 0, 0)),
            pl.BlockSpec((rows, 3 * width), lambda p: (0, 0)),
            pl.BlockSpec((2, 5, TILE, TILE), lambda p: (p, 0, 0, 0)),
        ],
        out_shape=[
            jax.ShapeDtypeStruct((2 * pairs, rows, rows), BF),
            jax.ShapeDtypeStruct((rows, 3 * width), BF),
            jax.ShapeDtypeStruct((2 * pairs, 5, TILE, TILE), F32),
        ],
        scratch_shapes=[
            pltpu.VMEM((TILE, rows), F32),
        ],
        compiler_params=pltpu.CompilerParams(vmem_limit_bytes=VMEM),
        cost_estimate=cost(20),
        name="attend_back",
    )(weights, qkv, qkv_t, qkv, dc, dct, ct)


def halves(pieces, whole, sems):
    rows = pieces[0].shape[0]
    return [(whole.at[pl.ds(half * rows, rows), :], sems.at[half]) for half in range(2)]


def load_whole(pieces, layer, where_ref, whole, sems):
    for half, (slot, sem) in enumerate(halves(pieces, whole, sems)):
        own_layer = where_ref[0] == layer
        own_half = where_ref[1] == half
        cases = (
            own_layer & own_half,
            own_layer & jnp.logical_not(own_half),
            jnp.logical_not(own_layer) & own_half,
            jnp.logical_not(own_layer) & jnp.logical_not(own_half),
        )
        for piece, case in zip(pieces, cases):

            @pl.when(case)
            def begin(piece=piece, slot=slot, sem=sem):
                pltpu.make_async_copy(piece, slot, sem).start()


def await_whole(pieces, whole, sems):
    for slot, sem in halves(pieces, whole, sems):
        pltpu.make_async_copy(pieces[0], slot, sem).wait()


def any_specs(count):
    return [pl.BlockSpec(memory_space=pl.ANY)] * count


SMEM_SPEC = pl.BlockSpec(memory_space=pltpu.SMEM)


def project_kernel(layer, where_ref, x_ref, bias_ref, m0, m1, m2, m3, o_ref, t_ref, whole, sems):
    step = pl.program_id(0)

    @pl.when(step == 0)
    def fetch():
        load_whole((m0, m1, m2, m3), layer, where_ref, whole, sems)
        await_whole((m0, m1, m2, m3), whole, sems)

    cols = o_ref.shape[1]
    at = pl.ds(pl.multiple_of(step * cols, cols), cols)
    value = (dot(x_ref[...], whole[:, at]) + bias_ref[0]).astype(BF)
    o_ref[...] = value
    t_ref[...] = jnp.transpose(value)


def project(where, x, bias, pieces, layer):
    rows = x.shape[0]
    half_rows, width = pieces[0].shape
    cols = 2 * TILE
    return pl.pallas_call(
        functools.partial(project_kernel, layer),
        grid=(width // cols,),
        in_specs=[
            SMEM_SPEC,
            pl.BlockSpec(x.shape, lambda g: (0, 0)),
            pl.BlockSpec((1, 1, cols), lambda g: (layer, 0, g)),
        ]
        + any_specs(4),
        out_specs=[
            pl.BlockSpec((rows, cols), lambda g: (0, g)),
            pl.BlockSpec((cols, rows), lambda g: (g, 0)),
        ],
        out_shape=[
            jax.ShapeDtypeStruct((rows, width), BF),
            jax.ShapeDtypeStruct((width, rows), BF),
        ],
        scratch_shapes=[pltpu.VMEM((2 * half_rows, width), BF), pltpu.SemaphoreType.DMA((2,))],
        compiler_params=pltpu.CompilerParams(vmem_limit_bytes=VMEM),
        cost_estimate=cost(10),
        name="project",
    )(where, x, bias, *pieces)


def centre(values):
    width = values.shape[1]
    centered = values - jnp.sum(values, axis=1, keepdims=True) * (1.0 / width)
    square = jnp.sum(centered * centered, axis=1, keepdims=True) * (1.0 / width)
    scale = lax.rsqrt(square + EPS)
    return (centered * scale, scale)


def centre_back(grad, normed, scale):
    width = grad.shape[1]
    mean = jnp.sum(grad, axis=1, keepdims=True) * (1.0 / width)
    along = jnp.sum(grad * normed, axis=1, keepdims=True) * (1.0 / width)
    return scale * (grad - mean - normed * along)


def feed_kernel(layer, where_ref, ct_ref, x_ref, live_ref, vec_ref, wide_ref, *rest):
    pieces, rest = rest[:12], rest[12:]
    (n1_ref, s1_ref, hid_ref, tg_ref, slope_ref, n2_ref, s2_ref, y_ref), rest = rest[:8], rest[8:]
    w_out, w_in, w_back, sems = rest
    sets = (pieces[:4], pieces[4:8], pieces[8:])
    wholes = (w_out, w_in, w_back)

    def waits(start):
        @pl.when(pl.program_id(0) == 0)
        def _():
            if start is None:
                for n in range(3):
                    load_whole(sets[n], layer, where_ref, wholes[n], sems.at[n])
            else:
                await_whole(sets[start], wholes[start], sems.at[start])

    waits(None)
    mixed = jnp.transpose(ct_ref[...])
    waits(0)
    first = x_ref[...].astype(F32) + dot(mixed, w_out[...]) + vec_ref[0, 2:3, :]
    n1, s1 = centre(first)
    n1_ref[...] = n1
    s1_ref[...] = jnp.broadcast_to(s1, s1_ref.shape)
    hidden = n1 * vec_ref[0, 3:4, :] + vec_ref[0, 4:5, :]
    low = hidden.astype(BF)
    hid_ref[...] = low
    total = hidden + vec_ref[0, 9:10, :]
    waits(1)
    chunk = 6 * TILE
    for c in range(w_in.shape[1] // chunk):
        cols = slice(c * chunk, (c + 1) * chunk)
        u = dot(low, w_in[:, cols]) + wide_ref[0, :, cols]
        phi = 0.5 + 0.5 * lax.erf(u * ROOT_HALF)
        tg = (u * phi).astype(BF)
        tg_ref[:, cols] = tg
        slope_ref[:, cols] = (phi + u * (jnp.exp(-0.5 * u * u) * INV_ROOT_TAU)).astype(BF)
        if c == 0:
            waits(2)
        total = total + dot(tg, w_back[cols, :])
    n2, s2 = centre(total)
    n2_ref[...] = n2
    s2_ref[...] = jnp.broadcast_to(s2, s2_ref.shape)
    y = n2 * vec_ref[0, 10:11, :] + vec_ref[0, 11:12, :]
    y_ref[...] = jnp.where(live_ref[:, :1] > 0.0, y, 0.0).astype(BF)


def feed(where, ct, x, live, vec, wide, sets, layer):
    rows, width = x.shape
    ff = sets[1][0].shape[1]
    block = 2 * TILE
    row = lambda cols: pl.BlockSpec((block, cols), lambda g: (g, 0))
    shapes = [
        ((rows, width), F32), ((rows, TILE), F32), ((rows, width), BF), ((rows, ff), BF), ((rows, ff), BF),
        ((rows, width), F32), ((rows, TILE), F32), ((rows, width), BF),
    ]
    return pl.pallas_call(
        functools.partial(feed_kernel, layer),
        grid=(rows // block,),
        in_specs=[
            SMEM_SPEC,
            pl.BlockSpec((width, block), lambda g: (0, g)),
            row(width),
            row(TILE),
            pl.BlockSpec((1, *vec.shape[1:]), lambda g: (layer, 0, 0)),
            pl.BlockSpec((1, 1, ff), lambda g: (layer, 0, 0)),
        ]
        + any_specs(12),
        out_specs=[row(shape[1]) for shape, _ in shapes],
        out_shape=[jax.ShapeDtypeStruct(*s) for s in shapes],
        scratch_shapes=[
            pltpu.VMEM((width, width), BF),
            pltpu.VMEM((width, ff), BF),
            pltpu.VMEM((ff, width), BF),
            pltpu.SemaphoreType.DMA((3, 2)),
        ],
        compiler_params=pltpu.CompilerParams(vmem_limit_bytes=VMEM),
        cost_estimate=cost(20),
        name="feed",
    )(where, ct, x, live, vec, wide, *sets[0], *sets[1], *sets[2])


def feed_back_kernel(layer, where_ref, dy_ref, live_ref, vec_ref, n1_ref, s1_ref, n2_ref, s2_ref, slope_ref, inv_ref, *rest):
    pieces, rest = rest[:12], rest[12:]
    (df_ref, du_ref, dr_ref, da_ref, dct_ref, dc_ref, sum_ref, wsum_ref), rest = rest[:8], rest[8:]
    w_back, w_in, w_out, sems = rest
    sets = (pieces[:4], pieces[4:8], pieces[8:])
    wholes = (w_back, w_in, w_out)

    def waits(start):
        @pl.when(pl.program_id(0) == 0)
        def _():
            if start is None:
                for n in range(3):
                    load_whole(sets[n], layer, where_ref, wholes[n], sems.at[n])
                sum_ref[...] = jnp.zeros_like(sum_ref)
                wsum_ref[...] = jnp.zeros_like(wsum_ref)
            else:
                await_whole(sets[start], wholes[start], sems.at[start])

    def add(row, value):
        sum_ref[row : row + 1, :] += jnp.sum(value, axis=0, keepdims=True)

    waits(None)
    dy = jnp.where(live_ref[:, :1] > 0.0, dy_ref[...].astype(F32), 0.0)
    n2 = n2_ref[...]
    add(4, dy * n2)
    add(5, dy)
    dr2 = centre_back(dy * vec_ref[0, 10:11, :], n2, s2_ref[:, :1])
    df = dr2.astype(BF)
    df_ref[...] = df
    add(3, df.astype(F32))
    total = dr2
    waits(0)
    chunk = 6 * TILE
    for c in range(w_in.shape[1] // chunk):
        cols = slice(c * chunk, (c + 1) * chunk)
        du = (dot_nt(df, w_back[cols, :]) * slope_ref[:, cols].astype(F32)).astype(BF)
        du_ref[:, cols] = du
        wsum_ref[:, cols] += jnp.sum(du.astype(F32), axis=0, keepdims=True)
        if c == 0:
            waits(1)
        total = total + dot_nt(du, w_in[:, cols])
    n1 = n1_ref[...]
    add(1, total * n1)
    add(2, total)
    dr1 = centre_back(total * vec_ref[0, 3:4, :], n1, s1_ref[:, :1])
    dr_ref[...] = dr1
    da = dr1.astype(BF)
    da_ref[...] = da
    add(0, da.astype(F32))
    waits(2)
    grad = dot_nt(w_out[...], da)
    for head in range(grad.shape[0] // HEAD_DIM):
        mine = slice(head * HEAD_DIM, (head + 1) * HEAD_DIM)
        inv = inv_ref[head // 2, head % 2 : head % 2 + 1, :]
        dct_ref[mine, :] = (grad[mine, :] * inv).astype(BF)
    dc_ref[...] = jnp.transpose(dct_ref[...])


def feed_back(where, dy, live, vec, n1, s1, n2, s2, slope, inv, sets, layer):
    rows, width = dy.shape
    ff = slope.shape[1]
    block = 2 * TILE
    row = lambda cols: pl.BlockSpec((block, cols), lambda g: (g, 0))
    outs = [
        ((rows, width), BF, row(width)), ((rows, ff), BF, row(ff)), ((rows, width), F32, row(width)),
        ((rows, width), BF, row(width)), ((width, rows), BF, pl.BlockSpec((width, block), lambda g: (0, g))),
        ((rows, width), BF, row(width)),
        ((8, width), F32, pl.BlockSpec((8, width), lambda g: (0, 0))),
        ((1, ff), F32, pl.BlockSpec((1, ff), lambda g: (0, 0))),
    ]
    return pl.pallas_call(
        functools.partial(feed_back_kernel, layer),
        grid=(rows // block,),
        in_specs=[
            SMEM_SPEC,
            row(width),
            row(TILE),
            pl.BlockSpec((1, *vec.shape[1:]), lambda g: (layer, 0, 0)),
            row(width),
            row(TILE),
            row(width),
            row(TILE),
            row(ff),
            pl.BlockSpec((inv.shape[0], 8, block), lambda g: (0, 0, g)),
        ]
        + any_specs(12),
        out_specs=[o[2] for o in outs],
        out_shape=[jax.ShapeDtypeStruct(o[0], o[1]) for o in outs],
        scratch_shapes=[
            pltpu.VMEM((ff, width), BF),
            pltpu.VMEM((width, ff), BF),
            pltpu.VMEM((width, width), BF),
            pltpu.SemaphoreType.DMA((3, 2)),
        ],
        compiler_params=pltpu.CompilerParams(vmem_limit_bytes=VMEM),
        cost_estimate=cost(20),
        name="feed_back",
    )(where, dy, live, vec, n1, s1, n2, s2, slope, inv, *sets[0], *sets[1], *sets[2])


def input_back_kernel(layer, where_ref, d_ref, dr_ref, m0, m1, m2, m3, o_ref, sum_ref, whole, sems):
    step = pl.program_id(0)

    @pl.when(step == 0)
    def fetch():
        load_whole((m0, m1, m2, m3), layer, where_ref, whole, sems)
        await_whole((m0, m1, m2, m3), whole, sems)
        sum_ref[...] = jnp.zeros_like(sum_ref)

    d = d_ref[...]
    sum_ref[...] += jnp.sum(d.astype(F32), axis=0, keepdims=True)
    o_ref[...] = (dr_ref[...] + dot_nt(d, whole[...])).astype(BF)


def input_back(where, dqkv, dr1, pieces, layer):
    rows, wide = dqkv.shape
    width = dr1.shape[1]
    block = 2 * TILE
    row = lambda cols: pl.BlockSpec((block, cols), lambda g: (g, 0))
    return pl.pallas_call(
        functools.partial(input_back_kernel, layer),
        grid=(rows // block,),
        in_specs=[SMEM_SPEC, row(wide), row(width)] + any_specs(4),
        out_specs=[row(width), pl.BlockSpec((1, wide), lambda g: (0, 0))],
        out_shape=[jax.ShapeDtypeStruct((rows, width), BF), jax.ShapeDtypeStruct((1, wide), F32)],
        scratch_shapes=[pltpu.VMEM((width, wide), BF), pltpu.SemaphoreType.DMA((2,))],
        compiler_params=pltpu.CompilerParams(vmem_limit_bytes=VMEM),
        cost_estimate=cost(8),
        name="input_back",
    )(where, dqkv, dr1, *pieces)


def bucket_tree(delta, total, reach):
    half = total // 2
    exact = half // 2
    limits = bucket_limits(total, reach)
    dist = jnp.abs(delta)

    def count(low, high):
        if high - low == 1:
            return jnp.where(dist >= limits[low], 1, 0)
        middle = (low + high) // 2
        above = dist >= limits[middle]
        return jnp.where(above, middle - low + 1 + count(middle + 1, high), count(low, middle))

    bucket = jnp.where(dist < exact, dist, exact + count(0, len(limits)))
    return bucket + jnp.where(delta > 0, half, 0)


def prepare_kernel(where_ref, text_ref, patch_ref, x_ref, y_ref, across_ref, upward_ref, mask_ref, live_ref):
    rows = across_ref.shape[0]
    doc = where_ref[0]
    half = where_ref[1]
    text = text_ref[half, doc]
    patches = patch_ref[half, doc]
    lane = lax.broadcasted_iota(jnp.int32, (TILE, TILE), 1)
    for ref, out, base in ((x_ref, across_ref, 0), (y_ref, upward_ref, REL2)):
        line = ref[pl.ds(half * 2 + doc, 1), :]
        for r in range(rows // TILE):
            part = jnp.broadcast_to(line[:, r * TILE : (r + 1) * TILE], (TILE, TILE))
            column = jnp.transpose(part.astype(F32)).astype(jnp.int32)
            for c in range(rows // TILE):
                cols = slice(c * TILE, (c + 1) * TILE)
                out[r * TILE : (r + 1) * TILE, cols] = bucket_tree(column - line[:, cols], REL2, REACH2) + base
    index = lax.broadcasted_iota(jnp.int32, (rows, TILE), 0)
    live = (index < text) | ((index >= TEXT_MAX) & (index < TEXT_MAX + 1 + patches))
    first = lax.broadcasted_iota(jnp.int32, (rows, TILE), 1) == 0
    live_ref[...] = jnp.where(live, 1.0, 0.0)
    mask_ref[...] = jnp.where(first & jnp.logical_not(live), NEG * UNIT, 0.0).astype(BF)


def prepare(where, text_len, patches, box_x, box_y):
    rows = box_x.shape[2]
    flat = lambda a: a.reshape(-1, rows)
    vmem = pl.BlockSpec(memory_space=pltpu.VMEM)
    return pl.pallas_call(
        prepare_kernel,
        in_specs=[SMEM_SPEC] * 3 + [vmem] * 2,
        out_specs=[vmem] * 4,
        out_shape=[
            jax.ShapeDtypeStruct((rows, rows), jnp.int32),
            jax.ShapeDtypeStruct((rows, rows), jnp.int32),
            jax.ShapeDtypeStruct((rows, TILE), BF),
            jax.ShapeDtypeStruct((rows, TILE), F32),
        ],
        compiler_params=pltpu.CompilerParams(vmem_limit_bytes=VMEM),
        cost_estimate=cost(10),
        name="prepare",
    )(where, text_len, patches, flat(box_x), flat(box_y))


def table_kernel(first_ref, second_ref, x_ref, y_ref, o_ref, scr):
    heads, block, rows = first_ref.shape
    parts = rows // TILE

    @pl.when(pl.program_id(0) == 0)
    def start():
        o_ref[...] = jnp.zeros_like(o_ref)
        scr[:, 2 * heads * block :, :] = jnp.zeros((parts, scr.shape[1] - 2 * heads * block, TILE), F32)

    for layer, ref in enumerate((first_ref, second_ref)):
        for head in range(heads):
            wide = ref[head].astype(F32)
            at = (layer * heads + head) * block
            for c in range(parts):
                scr[c, at : at + block, :] = wide[:, c * TILE : (c + 1) * TILE]
    index = lax.broadcasted_iota(jnp.int32, (REL2, rows), 0)
    total = o_ref[...]
    for j in range(block):
        grads = jnp.concatenate(
            [scr[c, pl.ds(j, 32, stride=block), :] for c in range(parts)], axis=1
        ).astype(BF)
        row_x = jnp.broadcast_to(x_ref[j : j + 1, :], (REL2, rows))
        row_y = jnp.broadcast_to(y_ref[j : j + 1, :], (REL2, rows))
        hot = jnp.concatenate(
            [
                jnp.where(row_x == index, 1.0, 0.0).astype(BF),
                jnp.where(row_y == index + REL2, 1.0, 0.0).astype(BF),
            ],
            axis=0,
        )
        total = total + dot_nt(grads, hot)
    o_ref[...] = total


def table_sums(first, second, across, upward, part, parts):
    heads, rows, _ = first.shape
    block = 32
    count = rows // block // parts
    at = part * count
    return pl.pallas_call(
        table_kernel,
        grid=(count,),
        in_specs=[
            pl.BlockSpec((heads, block, rows), lambda g: (0, at + g, 0)),
            pl.BlockSpec((heads, block, rows), lambda g: (0, at + g, 0)),
            pl.BlockSpec((block, rows), lambda g: (at + g, 0)),
            pl.BlockSpec((block, rows), lambda g: (at + g, 0)),
        ],
        out_specs=pl.BlockSpec((32, 2 * REL2), lambda g: (0, 0)),
        out_shape=jax.ShapeDtypeStruct((32, 2 * REL2), F32),
        scratch_shapes=[pltpu.VMEM((rows // TILE, 32 * block, TILE), F32)],
        compiler_params=pltpu.CompilerParams(vmem_limit_bytes=VMEM),
        cost_estimate=cost(60 / parts),
        name="table_sums",
    )(first, second, across, upward)


class Place:
    def __init__(self):
        index = lax.axis_index("section")
        self.peers = lax.axis_size("section")
        self.docs = lax.axis_size("dp")
        self.half = index % 2
        self.layer = index // 2
        where = lax.axis_index("dp")
        bits = range(self.docs.bit_length() - 1)
        self.orders = [list(bits), [1, 0] + list(bits)[2:]]
        self.sides = [
            jnp.where(self.half == 0, (where >> one) & 1, (where >> two) & 1)
            for one, two in zip(*self.orders)
        ]

    def across(self, value, mask):
        return lax.ppermute(value, "section", [(i, i ^ mask) for i in range(self.peers)])

    def to_layer(self, value, layer):
        other = 1 - layer
        pairs = [(2 * other + h, 2 * layer + h) for h in range(2)]
        return lax.ppermute(value, "section", pairs)

    def facing(self, value, step):
        pairs = []
        for s in range(self.peers):
            for d in range(self.docs):
                pairs.append((s * self.docs + d, s * self.docs + (d ^ (1 << self.orders[s % 2][step]))))
        return lax.ppermute(value, ("section", "dp"), pairs)

    def joined(self, mine, theirs, side, axis=0):
        return jnp.where(
            side == 0, jnp.concatenate([mine, theirs], axis), jnp.concatenate([theirs, mine], axis)
        )

    def parted(self, value, side):
        rows = value.shape[0] // 2
        return (
            lax.dynamic_slice_in_dim(value, side * rows, rows, 0),
            lax.dynamic_slice_in_dim(value, (1 - side) * rows, rows, 0),
        )


    def over_core(self, value):
        return (value, lambda sent: self.across(sent, 1))

    def over_x(self, value):
        return (value, lambda sent: self.across(sent, 2))

    def over_dp(self, value, step):
        return (value, lambda sent: self.facing(sent, step))

    def weight_flow(self, mine, steps):
        part = mine.shape[0] >> steps
        spot = sum(side << step for step, side in enumerate(self.sides[:steps]))
        mate = self.across(mine, 1)
        got = yield self.over_x(lax.dynamic_slice_in_dim(mine, spot * part, part, 0))
        for step in range(steps):
            got = self.joined(got, (yield self.over_dp(got, step)), self.sides[step])
        return (mine, mate, got, (yield self.over_core(got)))

    def half_flow(self, full):
        keep, send = self.parted(full.astype(BF), self.half)
        return (keep, (yield self.over_core(send)))

    def scatter_flow(self, full):
        size = full.shape[0]
        terms = [(full, 0)]

        def added(offset):
            parts = [lax.dynamic_slice_in_dim(array, at + offset, size, 0) for array, at in terms]
            if len(parts) == 1:
                return parts[0]
            return sum(part.astype(F32) for part in parts).astype(BF)

        for step, side in enumerate(self.sides[:-1]):
            size //= 2
            arrived = yield self.over_dp(added((1 - side) * size), step)
            terms = [(array, at + side * size) for array, at in terms] + [(arrived, 0)]
        return added(0)

    def gather_flow(self, second, first):
        mine = jnp.where(self.layer == 1, second, first)
        sent = yield self.over_x(jnp.where(self.layer == 1, first, second))
        total = (mine.astype(F32) + sent.astype(F32)).astype(BF)
        last = len(self.sides) - 1
        total = (total.astype(F32) + (yield self.over_dp(total, last)).astype(F32)).astype(BF)
        for step, side in reversed(list(enumerate(self.sides[:-1]))):
            total = self.joined(total, (yield self.over_dp(total, step)), side)
        return total.astype(F32)

    def all_flow(self, value):
        for over in (self.over_core, self.over_x):
            value = value + (yield over(value))
        for step in range(len(self.sides)):
            value = value + (yield self.over_dp(value, step))
        return value


class Flow:
    def __init__(self, steps):
        self.steps = steps
        self.air = self.result = None
        self.ready, self.move = next(steps)

    def land(self, arrived):
        self.air = None
        try:
            self.ready, self.move = self.steps.send(arrived)
        except StopIteration as end:
            self.ready = self.move = None
            self.result = end.value

    def go(self):
        self.air, self.ready = self.move(self.ready), None

    @property
    def busy(self):
        return self.air is not None or self.ready is not None


def pace(value, *flows):
    flows = [flow for flow in flows if flow.busy]
    flying = [flow for flow in flows if flow.air is not None]
    value, air = lax.optimization_barrier((value, [flow.air for flow in flying]))
    for flow, arrived in zip(flying, air):
        flow.land(arrived)
    flows = [flow for flow in flows if flow.busy]
    value, ready = lax.optimization_barrier((value, [flow.ready for flow in flows]))
    for flow, sent in zip(flows, ready):
        flow.air, flow.ready = flow.move(sent), None
    return value


def finished(flow):
    while flow.busy:
        pace(0, flow)
    return flow.result


def score_tables(quarters):
    count, _, _, heads = quarters.shape
    cut = REL1 // 2
    box = quarters[:, :, cut:, :].astype(F32).reshape(count, 2, 2, REL2 // 2, heads)
    box = jnp.transpose(box, (0, 4, 2, 1, 3)).reshape(count, heads // 2, 2, 2 * REL2)
    fixed = jnp.round(box * UNIT).astype(jnp.int32)
    tabs = fixed[:, :, :1] * 65536 + fixed[:, :, 1:] + 16384
    chosen = np.concatenate([line_rows(), np.zeros((3, 2 * TILE), int)]).reshape(-1)
    hot = jnp.asarray(chosen[None, :] == np.arange(REL1)[:, None], BF)
    line = quarters[:, :, :cut, :].reshape(count, REL1, heads)
    lines = lax.dot_general(line, hot, (((1,), (0,)), ((), ())), preferred_element_type=F32)
    odd = (jnp.arange(heads) % 2).astype(F32)[:, None]
    lines = (lines * UNIT - odd * 32768.0).reshape(count, heads, 8, 2 * TILE)
    return (tabs, lines)


def packed(vectors, tables):
    wide = vectors[1].shape[-1]
    rows = [v.reshape(-1, wide) for v in vectors]
    rows.append(jnp.zeros((4, wide), rows[0].dtype))
    table = jnp.concatenate(tables, axis=0)
    rows.append(jnp.pad(table, ((0, 0), (0, wide - table.shape[1]))))
    return jnp.concatenate(rows, axis=0)


def unpacked(quarters, heads):
    wide = quarters.shape[-1]
    v = quarters[:, :, :16].astype(F32)
    rows = jnp.transpose(v, (0, 2, 1, 3)).reshape(2, 16, 2 * wide)
    b_in = v[:, :, 5:9].reshape(2, 1, 8 * wide)
    b_qv = v[:, :, :2].reshape(2, 2, 2 * wide)
    bias = jnp.concatenate([b_qv[:, :1], jnp.zeros_like(b_qv[:, :1]), b_qv[:, 1:]], axis=2)
    return (rows, b_in, bias), quarters[:, :, 16:, :heads]


def local(
    section_data,
    text_len,
    patches,
    box_x,
    box_y,
    w_qkv,
    b_qv,
    w_out,
    b_out,
    norm1_gain,
    norm1_bias,
    w_in,
    b_in,
    w_back,
    b_back,
    norm2_gain,
    norm2_bias,
    rel_line,
    rel_x,
    rel_y,
):
    place = Place()
    heads = rel_line.shape[2]
    rows, width = section_data.shape[2:]
    first = place.layer == 0
    where = jnp.stack([place.layer, place.half]).astype(jnp.int32)

    entries = section_data[0]
    wf_qkv = Flow(place.weight_flow(w_qkv[0], 2))
    wf_qkv.go()
    smalls = [v[0] for v in (b_qv, b_out, norm1_gain, norm1_bias, b_in, b_back, norm2_gain, norm2_bias)]
    smalls = packed(smalls, [t[0] for t in (rel_line, rel_x, rel_y)])
    theirs = place.across(smalls, 2)
    meta = prepare(where, text_len, patches, box_x, box_y)
    swapped = jnp.where(first, entries[1], entries[0])
    meta, smalls, theirs, swapped = pace((meta, smalls, theirs, swapped), wf_qkv)
    across, upward, mask, live = meta
    got = place.across(swapped, 2)
    smalls = place.joined(smalls[None], theirs[None], place.layer)
    mates = place.across(smalls, 1)
    w_rest = (w_out, w_in, w_back)
    smalls, mates, w_rest = pace((smalls, mates, w_rest), wf_qkv)
    wf_out, wf_in, wf_back = [Flow(place.weight_flow(w[0], n)) for w, n in zip(w_rest, (1, 2, 2))]
    smalls = place.joined(smalls[:, None], mates[:, None], place.half, 1)
    (vectors, b_in, b_qv), tables = unpacked(smalls, heads)
    vectors, b_in, b_qv, tables, got = pace((vectors, b_in, b_qv, tables, got), wf_qkv, wf_out, wf_in)
    scores = score_tables(tables)
    source = jnp.where(first, entries[0], got)
    cotangent = jnp.where(first, got, entries[1])
    scores, source, cotangent = pace((scores, source, cotangent), wf_qkv, wf_back)
    w_qkv = finished(wf_qkv)

    def forward(x, n, calls, paced):
        qkv, qkv_t = paced(project(where, x, b_qv, w_qkv, n), wf_out, wf_in)
        mixed = ()
        for part in range(calls):
            mixed = attend(
                qkv, qkv_t, mask, across, upward, scores[0][n], scores[1][n], calls, part, mixed
            )
            mixed = paced(mixed, wf_out, wf_in, wf_back)
        weights, ct, exact, inv = mixed
        sets = [finished(flow) for flow in (wf_out, wf_in, wf_back)]
        n1, s1, hidden, tg, slope, n2, s2, y = feed(where, ct, x, live, vectors, b_in, sets, n)
        return dict(
            x=x, qkv=qkv, qkv_t=qkv_t, weights=weights, ct=ct, exact=exact, inv=inv,
            n1=n1, s1=s1, hidden=hidden, tg=tg, slope=slope, n2=n2, s2=s2, y=y,
        )

    kept = [forward(source, 0, 3, pace)]
    kept.append(forward(kept[0]["y"], 1, 1, lambda value, *flows: value))
    w_out, w_in, w_back = [finished(flow) for flow in (wf_out, wf_in, wf_back)]

    def feed_grads(dy, n):
        k = kept[n]
        return feed_back(
            where, dy, live, vectors, k["n1"], k["s1"], k["n2"], k["s2"], k["slope"], k["inv"],
            (w_back, w_in, w_out), n,
        )

    def scores_back(dc, dct, n):
        k = kept[n]
        return attend_back(k["weights"], k["qkv"], k["qkv_t"], dc, dct, k["exact"])

    def back_grad(df, n):
        return Flow(place.half_flow(dot_tn(kept[n]["tg"], df)))

    def in_grad(du, n):
        return Flow(place.half_flow(dot_tn(kept[n]["hidden"], du)))

    def mixing_grad(dqkv, da, n):
        g_qkv = dot_tn(kept[n]["x"], dqkv).astype(BF)
        g_out = dot(kept[n]["ct"], da).astype(BF)
        return Flow(place.half_flow(jnp.concatenate([g_qkv, g_out], axis=1)))

    def both_terms(flow):
        keep, arrived = finished(flow)
        return (keep.astype(F32) + arrived.astype(F32)).astype(BF)

    def feed_scatter(f_in, f_back):
        g_in, g_back = both_terms(f_in), both_terms(f_back)
        size = g_in.shape[0]
        blocks = [g_back[at : at + size] for at in range(0, g_back.shape[0], size)]
        return Flow(place.scatter_flow(jnp.concatenate([g_in] + blocks, axis=1)))

    def mix_scatter(flow):
        return Flow(place.scatter_flow(both_terms(flow)))

    def vector_rows(sums, wide, qkv):
        return jnp.concatenate([sums, wide.reshape(-1, width), qkv.reshape(-1, width)], axis=0)

    df, du, dr, da, dct, dc, sums, wide = feed_grads(cotangent, 1)
    f_back = back_grad(df, 1)
    du = pace(du, f_back)
    f_in = in_grad(du, 1)
    dc, dct = pace((dc, dct), f_back, f_in)
    dc, dct = pace((dc, dct), f_in)
    f_feed = feed_scatter(f_in, f_back)
    dc, dct = pace((dc, dct), f_feed)
    ds1, dqkv, line1 = scores_back(dc, dct, 1)
    f_mix = mixing_grad(dqkv, da, 1)
    dqkv = pace(dqkv, f_feed, f_mix)
    dx, s_qkv = input_back(where, dqkv, dr, w_qkv, 1)
    vectors1 = vector_rows(sums, wide, s_qkv)

    dx = pace(dx, f_mix)
    f_mix = mix_scatter(f_mix)
    dx = pace(dx, f_mix)
    df, du, dr, da, dct, dc, sums, wide = pace(feed_grads(dx, 0), f_feed, f_mix)
    e_back = back_grad(df, 0)
    du = pace(du, e_back)
    e_in = in_grad(du, 0)
    dc, dct = pace((dc, dct), f_mix, e_back, e_in)
    dc, dct = pace((dc, dct), e_in)
    e_feed = feed_scatter(e_in, e_back)
    dc, dct = pace((dc, dct), e_feed)
    ds0, dqkv, line0 = pace(scores_back(dc, dct, 0), e_feed)
    e_mix = mixing_grad(dqkv, da, 0)
    stores = (ds0, ds1)
    stores, dqkv = pace((stores, dqkv), e_feed, e_mix)
    s_feed = Flow(place.gather_flow(finished(f_feed), finished(e_feed)))
    stores, dqkv = pace((stores, dqkv), s_feed)

    parts = 4
    table = 0.0

    def tabled(part, *flows):
        more = table_sums(*stores, across, upward, part, parts)
        return pace((table + more, stores), *flows)

    table, stores = tabled(0, e_mix)
    e_mix = mix_scatter(e_mix)
    table, stores = pace((table, stores), e_mix)
    dx, s_qkv = input_back(where, dqkv, dr, w_qkv, 0)
    dx, s_qkv, stores = pace((dx, s_qkv, stores), s_feed)
    sent = place.across(jnp.where(first, kept[1]["y"], dx), 2)
    table, stores = tabled(1, e_mix)
    table, stores = tabled(2, e_mix)
    s_mix = Flow(place.gather_flow(finished(f_mix), finished(e_mix)))
    table, stores, sent = pace((table, stores, sent), s_mix)
    table, stores = tabled(3, s_mix)
    vectors0 = vector_rows(sums, wide, s_qkv)
    hot = jnp.asarray(line_tiles().reshape(-1)[:, None] == np.arange(REL1)[None, :], BF)
    lines = jnp.concatenate([line0, line1], axis=0).reshape(2 * heads, -1).astype(BF)
    lines = jnp.pad(dot(lines, hot), ((0, 32 - 2 * heads), (0, 0)))
    tables = jnp.concatenate([table, lines], axis=1)
    tables = jnp.pad(tables, ((0, 0), (0, width - tables.shape[1])))
    smalls = jnp.concatenate([vectors0, vectors1, tables], axis=0)
    a_small = Flow(place.all_flow(smalls))
    token = pace(dx, a_small)
    token = pace(token, a_small)
    token = pace(token, s_feed, a_small)
    token = pace(token, s_feed, s_mix)
    token = pace(token, s_mix, a_small)
    token = pace(token, a_small)
    flows = [s_feed, s_mix, a_small]
    while any(flow.busy for flow in flows):
        token = pace(token, *flows)
    g_feed, g_mix = s_feed.result, s_mix.result
    g_qkv, g_out = g_mix[:, : 3 * width], g_mix[:, 3 * width :]
    ff = du.shape[1]
    g_in = g_feed[:, :ff]
    g_back = jnp.concatenate(
        [g_feed[:, at : at + width] for at in range(ff, g_feed.shape[1], width)], axis=0
    )

    count = vectors0.shape[0]
    v = lax.dynamic_slice_in_dim(a_small.result, place.layer * count, count, 0)
    half_width = width // 2
    v_half = lax.dynamic_slice_in_dim(v, place.half * half_width, half_width, 1)
    v_in = lax.dynamic_slice_in_dim(v, 8 + 2 * place.half, 2, 0).reshape(1, -1)
    v_qv = lax.dynamic_slice_in_dim(v, 12 + 2 * place.half, 1, 0)
    t = lax.dynamic_slice_in_dim(a_small.result, 2 * count + place.layer * heads, heads, 0).T

    def table_half(at, size):
        return lax.dynamic_slice_in_dim(t, at + place.half * size, size, 0)[None]

    t_x, t_y = table_half(0, REL2 // 2), table_half(REL2, REL2 // 2)
    t_line = table_half(2 * REL2, REL1 // 2)
    result = jnp.where(first, jnp.stack([dx, sent]), jnp.stack([sent, kept[1]["y"]]))[None]
    return (
        result, g_qkv[None], v_qv, g_out[None], v_half[0:1], v_half[1:2], v_half[2:3],
        g_in[None], v_in, g_back[None], v_half[3:4], v_half[4:5], v_half[5:6],
        t_line, t_x, t_y,
    )


def solution(mesh):
    matrix = P("section", None, None)
    vector = P("section", None)
    weights = (
        matrix, vector, matrix, vector, vector, vector, matrix, vector, matrix,
        vector, vector, vector, matrix, matrix, matrix,
    )
    data = P("section", "dp", None, None)
    return jax.shard_map(
        local,
        mesh=mesh,
        in_specs=(data, P(None, "dp"), P(None, "dp"), P(None, "dp", None), P(None, "dp", None))
        + weights,
        out_specs=(data,) + weights,
        check_vma=False,
    )
```

```python
import functools
import math

import jax
import jax.numpy as jnp
import numpy as np
from jax import lax
from jax.experimental import pallas as pl
from jax.experimental.pallas import tpu as pltpu
from jax.sharding import PartitionSpec as P

REL1 = 32
REL2 = 64
REACH1 = 128
REACH2 = 256
HEAD_DIM = 64
TEXT_MAX = 191
EPS = 1e-05
NEG = -1000000000.0
ROOT_HALF = 0.7071067811865476
INV_ROOT_TAU = 0.3989422804014327

UNIT = 4096.0
LOG2E = 1.4426950408889634
TILE = 128
VMEM = 60 * 2**20
TABLE_BLOCK = 32


def cost(us):
    return pl.CostEstimate(flops=int(us * 10**9), bytes_accessed=int(us * 10**6), transcendentals=0)


BF = jnp.bfloat16
F32 = jnp.float32
NT = (((1,), (1,)), ((), ()))
TN = (((0,), (0,)), ((), ()))


def dot(a, b):
    return jnp.dot(a, b, preferred_element_type=F32)


def dot_nt(a, b):
    return lax.dot_general(a, b, NT, preferred_element_type=F32)


def dot_tn(a, b):
    return lax.dot_general(a, b, TN, preferred_element_type=F32)


def bucket_limits(total, reach):
    half = total // 2
    exact = half // 2
    return [
        int(math.ceil(exact * (reach / exact) ** (step / (half - exact)) - 1e-09))
        for step in range(1, half - exact)
    ]


def line_bucket_np(delta):
    half = REL1 // 2
    exact = half // 2
    dist = np.abs(delta)
    far = np.full(dist.shape, exact)
    for limit in bucket_limits(REL1, REACH1):
        far = far + (dist >= limit)
    return np.where(delta > 0, half, 0) + np.where(dist < exact, dist, far)


def line_rows():
    k = np.arange(2 * TILE)
    shift = np.where(k < TILE, k, k - 2 * TILE)
    return line_bucket_np(np.stack([TILE * (s - 2) - shift for s in range(5)]))


def line_tiles():
    r = np.arange(TILE)
    return line_bucket_np(np.stack([TILE * (s - 2) + r[:, None] - r[None, :] for s in range(5)]))


def lane_pick(table, index):
    dims = lax.GatherDimensionNumbers(
        offset_dims=(),
        collapsed_slice_dims=(1,),
        start_index_map=(1,),
        operand_batching_dims=(0,),
        start_indices_batching_dims=(0,),
    )
    return lax.gather(
        table,
        index[..., None],
        dims,
        slice_sizes=(1, 1),
        mode=lax.GatherScatterMode.PROMISE_IN_BOUNDS,
    )


def attend_kernel(
    k_ref,
    qt_ref,
    vt_ref,
    mask_ref,
    x_ref,
    y_ref,
    tab_ref,
    line_ref,
    p_ref,
    c_ref,
    exact_ref,
    inv_ref,
    kaug,
    qaug,
    strip,
    scores,
):
    rows = k_ref.shape[0]
    chunk = 2 * TILE
    step = 32
    lane = lax.broadcasted_iota(jnp.int32, (rows, TILE), 1)
    keys = k_ref[...].astype(F32) * (UNIT / 8.0)
    kaug[0, :, :TILE] = jnp.where(lane < HEAD_DIM, keys, 0.0).astype(BF)
    kaug[1, :, :TILE] = jnp.where(lane < HEAD_DIM, 0.0, keys).astype(BF)
    kaug[0, :, TILE:] = mask_ref[...]
    kaug[1, :, TILE:] = mask_ref[...]
    qaug[:TILE, :] = qt_ref[...]
    qaug[TILE:, :] = jnp.ones((TILE, rows), BF)
    for head in range(2):
        for s in range(5):
            wide = jnp.broadcast_to(line_ref[head, s : s + 1, :], (TILE, 2 * TILE))
            if s in (1, 2, 3):
                wide = pltpu.roll(wide, 0, axis=1, stride=1, stride_axis=0)
            strip[head, s] = wide[:, :TILE]
    table = jnp.broadcast_to(tab_ref[0], (step, TILE))
    chunks = rows // chunk
    low = jnp.full((8, chunk), -3e38, F32)

    def score(t, n, peaks):
        cols = slice(t * chunk, (t + 1) * chunk)
        tile = pl.ds(pl.multiple_of(n * TILE, TILE), TILE)
        raw = [dot(kaug[head, tile, :], qaug[:, cols]) for head in range(2)]
        peaks = list(peaks)
        for m in range(TILE // step):
            at = pl.ds(pl.multiple_of(n * TILE + m * step, step), step)
            sub = slice(m * step, (m + 1) * step)
            parts = ([], [])
            for part in range(2):
                lanes = slice(part * TILE, (part + 1) * TILE)
                wide = slice(t * chunk + part * TILE, t * chunk + (part + 1) * TILE)
                both = lane_pick(table, x_ref[at, wide]) + lane_pick(table, y_ref[at, wide])
                off = jnp.clip(n - (2 * t + part), -2, 2) + 2
                for head, bits in ((0, both >> 16), (1, both & 0xFFFF)):
                    value = raw[head][sub, lanes] + strip[head, off, sub, :] + bits.astype(F32)
                    scores[t % 2, head, at, lanes] = value
                    parts[head].append(value)
            for head in range(2):
                wide = jnp.concatenate(parts[head], axis=1)
                for r in range(step // 8):
                    peaks[head] = jnp.maximum(peaks[head], wide[8 * r : 8 * r + 8, :])
        return tuple(peaks)

    def weigh(t, n, peaks):
        cols = slice(t * chunk, (t + 1) * chunk)
        for m in range(TILE // step):
            at = pl.ds(pl.multiple_of(n * TILE + m * step, step), step)
            for head in range(2):
                power = (scores[t % 2, head, at, :] - peaks[head]) * (LOG2E / UNIT)
                p_ref[head, at, cols] = jnp.exp2(power).astype(BF)

    ones = jnp.ones((16, rows), BF)

    def mix(t):
        cols = slice(t * chunk, (t + 1) * chunk)
        for head in range(2):
            mine = slice(head * HEAD_DIM, (head + 1) * HEAD_DIM)
            vals = jnp.concatenate([vt_ref[mine, :], ones], axis=0)
            mixed = dot(vals, p_ref[head, :, cols])
            inv = 1.0 / mixed[HEAD_DIM : HEAD_DIM + 1, :]
            exact = mixed[:HEAD_DIM, :] * inv
            exact_ref[mine, cols] = exact
            c_ref[mine, cols] = exact.astype(BF)
            inv_ref[0, head : head + 1, cols] = inv

    peaks = None
    for t in range(chunks + 1):
        old = peaks

        def both_steps(n, tops):
            if t < chunks:
                tops = score(t, n, tops)
            if t > 0:
                weigh(t - 1, n, old)
            return tops

        tops = lax.fori_loop(0, rows // TILE, both_steps, (low, low), unroll=6)
        peaks = [jnp.max(top, axis=0, keepdims=True) for top in tops]
        if t > 0:
            mix(t - 1)

def attend(qkv, qkv_t, mask, across, upward, tabs, lines, calls=1, part=0, before=()):
    rows = qkv.shape[0]
    width = qkv.shape[1] // 3
    pairs = width // TILE
    count = pairs // calls
    at = part * count
    whole = lambda p: (0, 0)
    kernel = attend_kernel
    if before:
        kernel = lambda *refs: attend_kernel(*refs[:8], *refs[12:])
    return pl.pallas_call(
        kernel,
        grid=(count,),
        in_specs=[
            pl.BlockSpec((rows, TILE), lambda p: (0, pairs + at + p)),
            pl.BlockSpec((TILE, rows), lambda p: (at + p, 0)),
            pl.BlockSpec((TILE, rows), lambda p: (2 * pairs + at + p, 0)),
            pl.BlockSpec((rows, TILE), whole),
            pl.BlockSpec((rows, rows), whole),
            pl.BlockSpec((rows, rows), whole),
            pl.BlockSpec((1, 1, TILE), lambda p: (at + p, 0, 0)),
            pl.BlockSpec((2, 8, 2 * TILE), lambda p: (at + p, 0, 0)),
        ]
        + [pl.BlockSpec(memory_space=pl.ANY) for _ in before],
        out_specs=[
            pl.BlockSpec((2, rows, rows), lambda p: (at + p, 0, 0)),
            pl.BlockSpec((TILE, rows), lambda p: (at + p, 0)),
            pl.BlockSpec((TILE, rows), lambda p: (at + p, 0)),
            pl.BlockSpec((1, 8, rows), lambda p: (at + p, 0, 0)),
        ],
        out_shape=[
            jax.ShapeDtypeStruct((2 * pairs, rows, rows), BF),
            jax.ShapeDtypeStruct((width, rows), BF),
            jax.ShapeDtypeStruct((width, rows), F32),
            jax.ShapeDtypeStruct((pairs, 8, rows), F32),
        ],
        scratch_shapes=[
            pltpu.VMEM((2, rows, 2 * TILE), BF),
            pltpu.VMEM((2 * TILE, rows), BF),
            pltpu.VMEM((2, 5, TILE, TILE), F32),
            pltpu.VMEM((2, 2, rows, 2 * TILE), F32),
        ],
        input_output_aliases={8 + n: n for n in range(len(before))},
        compiler_params=pltpu.CompilerParams(vmem_limit_bytes=VMEM),
        cost_estimate=cost(33 / calls),
        name="attend",
    )(qkv, qkv_t, qkv_t, mask, across, upward, tabs, lines, *before)


def attend_back_kernel(
    p_ref,
    q_ref,
    kt_ref,
    v_ref,
    dc_ref,
    dct_ref,
    ct_ref,
    ds_ref,
    d_ref,
    line_ref,
    dqt,
):
    rows = q_ref.shape[0]
    line_ref[...] = jnp.zeros_like(line_ref)
    product = dct_ref[...].astype(F32) * ct_ref[...]
    lane = lax.broadcasted_iota(jnp.int32, (rows, TILE), 1)
    vals = v_ref[...]
    out_k, out_v = [], []
    for head in range(2):
        mine = slice(head * HEAD_DIM, (head + 1) * HEAD_DIM)
        delta = jnp.sum(product[mine, :], axis=0, keepdims=True)
        own = (lane < HEAD_DIM) if head == 0 else (lane >= HEAD_DIM)
        picked = jnp.where(own, vals, jnp.zeros_like(vals))
        for n in range(rows // TILE):
            at = slice(n * TILE, (n + 1) * TILE)
            dp = dot(picked[at, :], dct_ref[...])
            sums = {}
            for part in range(rows // TILE):
                lanes = slice(part * TILE, (part + 1) * TILE)
                weights = p_ref[head, at, lanes].astype(F32)
                grad = weights * (dp[:, lanes] - delta[:, lanes])
                ds_ref[head, at, lanes] = grad.astype(BF)
                off = min(max(n - part, -2), 2) + 2
                sums[off] = grad if off not in sums else sums[off] + grad
            for off, value in sums.items():
                line_ref[head, off] += value
        out_k.append(dot(ds_ref[head], q_ref[...]))
        out_v.append(dot(p_ref[head], dc_ref[...]))
        dqt[mine, :] = dot(kt_ref[mine, :], ds_ref[head])
    width = d_ref.shape[1] // 3
    base = pl.multiple_of(pl.program_id(0) * TILE, TILE)
    d_ref[:, pl.ds(width + base, TILE)] = (
        jnp.where(lane < HEAD_DIM, out_k[0], out_k[1]) * 0.125
    ).astype(BF)
    d_ref[:, pl.ds(2 * width + base, TILE)] = jnp.where(lane < HEAD_DIM, out_v[0], out_v[1]).astype(BF)
    d_ref[:, pl.ds(base, TILE)] = (jnp.transpose(dqt[...]) * 0.125).astype(BF)


def attend_back(weights, qkv, qkv_t, dc, dct, ct):
    rows = qkv.shape[0]
    width = qkv.shape[1] // 3
    pairs = width // TILE
    return pl.pallas_call(
        attend_back_kernel,
        grid=(pairs,),
        in_specs=[
            pl.BlockSpec((2, rows, rows), lambda p: (p, 0, 0)),
            pl.BlockSpec((rows, TILE), lambda p: (0, p)),
            pl.BlockSpec((TILE, rows), lambda p: (pairs + p, 0)),
            pl.BlockSpec((rows, TILE), lambda p: (0, 2 * pairs + p)),
            pl.BlockSpec((rows, TILE), lambda p: (0, p)),
            pl.BlockSpec((TILE, rows), lambda p: (p, 0)),
            pl.BlockSpec((TILE, rows), lambda p: (p, 0)),
        ],
        out_specs=[
            pl.BlockSpec((2, rows, rows), lambda p: (p, 0, 0)),
            pl.BlockSpec((rows, 3 * width), lambda p: (0, 0)),
            pl.BlockSpec((2, 5, TILE, TILE), lambda p: (p, 0, 0, 0)),
        ],
        out_shape=[
            jax.ShapeDtypeStruct((2 * pairs, rows, rows), BF),
            jax.ShapeDtypeStruct((rows, 3 * width), BF),
            jax.ShapeDtypeStruct((2 * pairs, 5, TILE, TILE), F32),
        ],
        scratch_shapes=[
            pltpu.VMEM((TILE, rows), F32),
        ],
        compiler_params=pltpu.CompilerParams(vmem_limit_bytes=VMEM),
        cost_estimate=cost(20),
        name="attend_back",
    )(weights, qkv, qkv_t, qkv, dc, dct, ct)


def halves(pieces, whole, sems):
    rows = pieces[0].shape[0]
    return [(whole.at[pl.ds(half * rows, rows), :], sems.at[half]) for half in range(2)]


def load_whole(pieces, layer, where_ref, whole, sems):
    for half, (slot, sem) in enumerate(halves(pieces, whole, sems)):
        own_layer = where_ref[0] == layer
        own_half = where_ref[1] == half
        cases = (
            own_layer & own_half,
            own_layer & jnp.logical_not(own_half),
            jnp.logical_not(own_layer) & own_half,
            jnp.logical_not(own_layer) & jnp.logical_not(own_half),
        )
        for piece, case in zip(pieces, cases):

            @pl.when(case)
            def begin(piece=piece, slot=slot, sem=sem):
                pltpu.make_async_copy(piece, slot, sem).start()


def await_whole(pieces, whole, sems):
    for slot, sem in halves(pieces, whole, sems):
        pltpu.make_async_copy(pieces[0], slot, sem).wait()


def any_specs(count):
    return [pl.BlockSpec(memory_space=pl.ANY)] * count


SMEM_SPEC = pl.BlockSpec(memory_space=pltpu.SMEM)


def project_kernel(layer, where_ref, x_ref, bias_ref, m0, m1, m2, m3, o_ref, t_ref, whole, sems):
    step = pl.program_id(0)

    @pl.when(step == 0)
    def fetch():
        load_whole((m0, m1, m2, m3), layer, where_ref, whole, sems)
        await_whole((m0, m1, m2, m3), whole, sems)

    cols = o_ref.shape[1]
    at = pl.ds(pl.multiple_of(step * cols, cols), cols)
    value = (dot(x_ref[...], whole[:, at]) + bias_ref[0]).astype(BF)
    o_ref[...] = value
    t_ref[...] = jnp.transpose(value)


def project(where, x, bias, pieces, layer):
    rows = x.shape[0]
    half_rows, width = pieces[0].shape
    cols = 2 * TILE
    return pl.pallas_call(
        functools.partial(project_kernel, layer),
        grid=(width // cols,),
        in_specs=[
            SMEM_SPEC,
            pl.BlockSpec(x.shape, lambda g: (0, 0)),
            pl.BlockSpec((1, 1, cols), lambda g: (layer, 0, g)),
        ]
        + any_specs(4),
        out_specs=[
            pl.BlockSpec((rows, cols), lambda g: (0, g)),
            pl.BlockSpec((cols, rows), lambda g: (g, 0)),
        ],
        out_shape=[
            jax.ShapeDtypeStruct((rows, width), BF),
            jax.ShapeDtypeStruct((width, rows), BF),
        ],
        scratch_shapes=[pltpu.VMEM((2 * half_rows, width), BF), pltpu.SemaphoreType.DMA((2,))],
        compiler_params=pltpu.CompilerParams(vmem_limit_bytes=VMEM),
        cost_estimate=cost(10),
        name="project",
    )(where, x, bias, *pieces)


def centre(values):
    width = values.shape[1]
    centered = values - jnp.sum(values, axis=1, keepdims=True) * (1.0 / width)
    square = jnp.sum(centered * centered, axis=1, keepdims=True) * (1.0 / width)
    scale = lax.rsqrt(square + EPS)
    return (centered * scale, scale)


def centre_back(grad, normed, scale):
    width = grad.shape[1]
    mean = jnp.sum(grad, axis=1, keepdims=True) * (1.0 / width)
    along = jnp.sum(grad * normed, axis=1, keepdims=True) * (1.0 / width)
    return scale * (grad - mean - normed * along)


def feed_kernel(layer, where_ref, ct_ref, x_ref, live_ref, vec_ref, wide_ref, *rest):
    pieces, rest = rest[:12], rest[12:]
    (n1_ref, s1_ref, hid_ref, tg_ref, slope_ref, n2_ref, s2_ref, y_ref), rest = rest[:8], rest[8:]
    w_out, w_in, w_back, sems = rest
    sets = (pieces[:4], pieces[4:8], pieces[8:])
    wholes = (w_out, w_in, w_back)

    def waits(start):
        @pl.when(pl.program_id(0) == 0)
        def _():
            if start is None:
                for n in range(3):
                    load_whole(sets[n], layer, where_ref, wholes[n], sems.at[n])
            else:
                await_whole(sets[start], wholes[start], sems.at[start])

    waits(None)
    mixed = jnp.transpose(ct_ref[...])
    waits(0)
    first = x_ref[...].astype(F32) + dot(mixed, w_out[...]) + vec_ref[0, 2:3, :]
    n1, s1 = centre(first)
    n1_ref[...] = n1
    s1_ref[...] = jnp.broadcast_to(s1, s1_ref.shape)
    hidden = n1 * vec_ref[0, 3:4, :] + vec_ref[0, 4:5, :]
    low = hidden.astype(BF)
    hid_ref[...] = low
    total = hidden + vec_ref[0, 9:10, :]
    waits(1)
    chunk = 6 * TILE
    for c in range(w_in.shape[1] // chunk):
        cols = slice(c * chunk, (c + 1) * chunk)
        u = dot(low, w_in[:, cols]) + wide_ref[0, :, cols]
        phi = 0.5 + 0.5 * lax.erf(u * ROOT_HALF)
        tg = (u * phi).astype(BF)
        tg_ref[:, cols] = tg
        slope_ref[:, cols] = (phi + u * (jnp.exp(-0.5 * u * u) * INV_ROOT_TAU)).astype(BF)
        if c == 0:
            waits(2)
        total = total + dot(tg, w_back[cols, :])
    n2, s2 = centre(total)
    n2_ref[...] = n2
    s2_ref[...] = jnp.broadcast_to(s2, s2_ref.shape)
    y = n2 * vec_ref[0, 10:11, :] + vec_ref[0, 11:12, :]
    y_ref[...] = jnp.where(live_ref[:, :1] > 0.0, y, 0.0).astype(BF)


def feed(where, ct, x, live, vec, wide, sets, layer):
    rows, width = x.shape
    ff = sets[1][0].shape[1]
    block = 2 * TILE
    row = lambda cols: pl.BlockSpec((block, cols), lambda g: (g, 0))
    shapes = [
        ((rows, width), F32), ((rows, TILE), F32), ((rows, width), BF), ((rows, ff), BF), ((rows, ff), BF),
        ((rows, width), F32), ((rows, TILE), F32), ((rows, width), BF),
    ]
    return pl.pallas_call(
        functools.partial(feed_kernel, layer),
        grid=(rows // block,),
        in_specs=[
            SMEM_SPEC,
            pl.BlockSpec((width, block), lambda g: (0, g)),
            row(width),
            row(TILE),
            pl.BlockSpec((1, *vec.shape[1:]), lambda g: (layer, 0, 0)),
            pl.BlockSpec((1, 1, ff), lambda g: (layer, 0, 0)),
        ]
        + any_specs(12),
        out_specs=[row(shape[1]) for shape, _ in shapes],
        out_shape=[jax.ShapeDtypeStruct(*s) for s in shapes],
        scratch_shapes=[
            pltpu.VMEM((width, width), BF),
            pltpu.VMEM((width, ff), BF),
            pltpu.VMEM((ff, width), BF),
            pltpu.SemaphoreType.DMA((3, 2)),
        ],
        compiler_params=pltpu.CompilerParams(vmem_limit_bytes=VMEM),
        cost_estimate=cost(20),
        name="feed",
    )(where, ct, x, live, vec, wide, *sets[0], *sets[1], *sets[2])


def feed_back_kernel(layer, where_ref, dy_ref, live_ref, vec_ref, n1_ref, s1_ref, n2_ref, s2_ref, slope_ref, inv_ref, *rest):
    pieces, rest = rest[:12], rest[12:]
    (df_ref, du_ref, dr_ref, da_ref, dct_ref, dc_ref, sum_ref, wsum_ref), rest = rest[:8], rest[8:]
    w_back, w_in, w_out, sems = rest
    sets = (pieces[:4], pieces[4:8], pieces[8:])
    wholes = (w_back, w_in, w_out)

    def waits(start):
        @pl.when(pl.program_id(0) == 0)
        def _():
            if start is None:
                for n in range(3):
                    load_whole(sets[n], layer, where_ref, wholes[n], sems.at[n])
                sum_ref[...] = jnp.zeros_like(sum_ref)
                wsum_ref[...] = jnp.zeros_like(wsum_ref)
            else:
                await_whole(sets[start], wholes[start], sems.at[start])

    def add(row, value):
        sum_ref[row : row + 1, :] += jnp.sum(value, axis=0, keepdims=True)

    waits(None)
    dy = jnp.where(live_ref[:, :1] > 0.0, dy_ref[...].astype(F32), 0.0)
    n2 = n2_ref[...]
    add(4, dy * n2)
    add(5, dy)
    dr2 = centre_back(dy * vec_ref[0, 10:11, :], n2, s2_ref[:, :1])
    df = dr2.astype(BF)
    df_ref[...] = df
    add(3, df.astype(F32))
    total = dr2
    waits(0)
    chunk = 6 * TILE
    for c in range(w_in.shape[1] // chunk):
        cols = slice(c * chunk, (c + 1) * chunk)
        du = (dot_nt(df, w_back[cols, :]) * slope_ref[:, cols].astype(F32)).astype(BF)
        du_ref[:, cols] = du
        wsum_ref[:, cols] += jnp.sum(du.astype(F32), axis=0, keepdims=True)
        if c == 0:
            waits(1)
        total = total + dot_nt(du, w_in[:, cols])
    n1 = n1_ref[...]
    add(1, total * n1)
    add(2, total)
    dr1 = centre_back(total * vec_ref[0, 3:4, :], n1, s1_ref[:, :1])
    dr_ref[...] = dr1
    da = dr1.astype(BF)
    da_ref[...] = da
    add(0, da.astype(F32))
    waits(2)
    grad = dot_nt(w_out[...], da)
    for head in range(grad.shape[0] // HEAD_DIM):
        mine = slice(head * HEAD_DIM, (head + 1) * HEAD_DIM)
        inv = inv_ref[head // 2, head % 2 : head % 2 + 1, :]
        dct_ref[mine, :] = (grad[mine, :] * inv).astype(BF)
    dc_ref[...] = jnp.transpose(dct_ref[...])


def feed_back(where, dy, live, vec, n1, s1, n2, s2, slope, inv, sets, layer):
    rows, width = dy.shape
    ff = slope.shape[1]
    block = 2 * TILE
    row = lambda cols: pl.BlockSpec((block, cols), lambda g: (g, 0))
    outs = [
        ((rows, width), BF, row(width)), ((rows, ff), BF, row(ff)), ((rows, width), F32, row(width)),
        ((rows, width), BF, row(width)), ((width, rows), BF, pl.BlockSpec((width, block), lambda g: (0, g))),
        ((rows, width), BF, row(width)),
        ((8, width), F32, pl.BlockSpec((8, width), lambda g: (0, 0))),
        ((1, ff), F32, pl.BlockSpec((1, ff), lambda g: (0, 0))),
    ]
    return pl.pallas_call(
        functools.partial(feed_back_kernel, layer),
        grid=(rows // block,),
        in_specs=[
            SMEM_SPEC,
            row(width),
            row(TILE),
            pl.BlockSpec((1, *vec.shape[1:]), lambda g: (layer, 0, 0)),
            row(width),
            row(TILE),
            row(width),
            row(TILE),
            row(ff),
            pl.BlockSpec((inv.shape[0], 8, block), lambda g: (0, 0, g)),
        ]
        + any_specs(12),
        out_specs=[o[2] for o in outs],
        out_shape=[jax.ShapeDtypeStruct(o[0], o[1]) for o in outs],
        scratch_shapes=[
            pltpu.VMEM((ff, width), BF),
            pltpu.VMEM((width, ff), BF),
            pltpu.VMEM((width, width), BF),
            pltpu.SemaphoreType.DMA((3, 2)),
        ],
        compiler_params=pltpu.CompilerParams(vmem_limit_bytes=VMEM),
        cost_estimate=cost(20),
        name="feed_back",
    )(where, dy, live, vec, n1, s1, n2, s2, slope, inv, *sets[0], *sets[1], *sets[2])


def input_back_kernel(layer, where_ref, d_ref, dr_ref, m0, m1, m2, m3, o_ref, sum_ref, whole, sems):
    step = pl.program_id(0)

    @pl.when(step == 0)
    def fetch():
        load_whole((m0, m1, m2, m3), layer, where_ref, whole, sems)
        await_whole((m0, m1, m2, m3), whole, sems)
        sum_ref[...] = jnp.zeros_like(sum_ref)

    d = d_ref[...]
    sum_ref[...] += jnp.sum(d.astype(F32), axis=0, keepdims=True)
    o_ref[...] = (dr_ref[...] + dot_nt(d, whole[...])).astype(BF)


def input_back(where, dqkv, dr1, pieces, layer):
    rows, wide = dqkv.shape
    width = dr1.shape[1]
    block = 2 * TILE
    row = lambda cols: pl.BlockSpec((block, cols), lambda g: (g, 0))
    return pl.pallas_call(
        functools.partial(input_back_kernel, layer),
        grid=(rows // block,),
        in_specs=[SMEM_SPEC, row(wide), row(width)] + any_specs(4),
        out_specs=[row(width), pl.BlockSpec((1, wide), lambda g: (0, 0))],
        out_shape=[jax.ShapeDtypeStruct((rows, width), BF), jax.ShapeDtypeStruct((1, wide), F32)],
        scratch_shapes=[pltpu.VMEM((width, wide), BF), pltpu.SemaphoreType.DMA((2,))],
        compiler_params=pltpu.CompilerParams(vmem_limit_bytes=VMEM),
        cost_estimate=cost(8),
        name="input_back",
    )(where, dqkv, dr1, *pieces)


def bucket_tree(delta, total, reach):
    half = total // 2
    exact = half // 2
    limits = bucket_limits(total, reach)
    dist = jnp.abs(delta)

    def count(low, high):
        if high - low == 1:
            return jnp.where(dist >= limits[low], 1, 0)
        middle = (low + high) // 2
        above = dist >= limits[middle]
        return jnp.where(above, middle - low + 1 + count(middle + 1, high), count(low, middle))

    bucket = jnp.where(dist < exact, dist, exact + count(0, len(limits)))
    return bucket + jnp.where(delta > 0, half, 0)


def prepare_kernel(where_ref, text_ref, patch_ref, x_ref, y_ref, across_ref, upward_ref, mask_ref, live_ref):
    rows = across_ref.shape[0]
    doc = where_ref[0]
    half = where_ref[1]
    text = text_ref[half, doc]
    patches = patch_ref[half, doc]
    lane = lax.broadcasted_iota(jnp.int32, (TILE, TILE), 1)
    for ref, out, base in ((x_ref, across_ref, 0), (y_ref, upward_ref, REL2)):
        line = ref[pl.ds(half * 2 + doc, 1), :]
        for r in range(rows // TILE):
            part = jnp.broadcast_to(line[:, r * TILE : (r + 1) * TILE], (TILE, TILE))
            column = jnp.transpose(part.astype(F32)).astype(jnp.int32)
            for c in range(rows // TILE):
                cols = slice(c * TILE, (c + 1) * TILE)
                out[r * TILE : (r + 1) * TILE, cols] = bucket_tree(column - line[:, cols], REL2, REACH2) + base
    index = lax.broadcasted_iota(jnp.int32, (rows, TILE), 0)
    live = (index < text) | ((index >= TEXT_MAX) & (index < TEXT_MAX + 1 + patches))
    first = lax.broadcasted_iota(jnp.int32, (rows, TILE), 1) == 0
    live_ref[...] = jnp.where(live, 1.0, 0.0)
    mask_ref[...] = jnp.where(first & jnp.logical_not(live), NEG * UNIT, 0.0).astype(BF)


def prepare(where, text_len, patches, box_x, box_y):
    rows = box_x.shape[2]
    flat = lambda a: a.reshape(-1, rows)
    vmem = pl.BlockSpec(memory_space=pltpu.VMEM)
    return pl.pallas_call(
        prepare_kernel,
        in_specs=[SMEM_SPEC] * 3 + [vmem] * 2,
        out_specs=[vmem] * 4,
        out_shape=[
            jax.ShapeDtypeStruct((rows, rows), jnp.int32),
            jax.ShapeDtypeStruct((rows, rows), jnp.int32),
            jax.ShapeDtypeStruct((rows, TILE), BF),
            jax.ShapeDtypeStruct((rows, TILE), F32),
        ],
        compiler_params=pltpu.CompilerParams(vmem_limit_bytes=VMEM),
        cost_estimate=cost(10),
        name="prepare",
    )(where, text_len, patches, flat(box_x), flat(box_y))


def table_kernel(first_ref, second_ref, x_ref, y_ref, o_ref, scr):
    heads, block, rows = first_ref.shape
    parts = rows // TILE

    @pl.when(pl.program_id(0) == 0)
    def start():
        o_ref[...] = jnp.zeros_like(o_ref)
        scr[:, 2 * heads * block :, :] = jnp.zeros((parts, scr.shape[1] - 2 * heads * block, TILE), F32)

    for layer, ref in enumerate((first_ref, second_ref)):
        for head in range(heads):
            wide = ref[head].astype(F32)
            at = (layer * heads + head) * block
            for c in range(parts):
                scr[c, at : at + block, :] = wide[:, c * TILE : (c + 1) * TILE]
    index = lax.broadcasted_iota(jnp.int32, (REL2, rows), 0)
    total = o_ref[...]
    for j in range(block):
        grads = jnp.concatenate(
            [scr[c, pl.ds(j, 32, stride=block), :] for c in range(parts)], axis=1
        ).astype(BF)
        row_x = jnp.broadcast_to(x_ref[j : j + 1, :], (REL2, rows))
        row_y = jnp.broadcast_to(y_ref[j : j + 1, :], (REL2, rows))
        hot = jnp.concatenate(
            [
                jnp.where(row_x == index, 1.0, 0.0).astype(BF),
                jnp.where(row_y == index + REL2, 1.0, 0.0).astype(BF),
            ],
            axis=0,
        )
        total = total + dot_nt(grads, hot)
    o_ref[...] = total


def table_sums(first, second, across, upward, at, count):
    heads, rows, _ = first.shape
    block = TABLE_BLOCK
    return pl.pallas_call(
        table_kernel,
        grid=(count,),
        in_specs=[
            pl.BlockSpec((heads, block, rows), lambda g: (0, at + g, 0)),
            pl.BlockSpec((heads, block, rows), lambda g: (0, at + g, 0)),
            pl.BlockSpec((block, rows), lambda g: (at + g, 0)),
            pl.BlockSpec((block, rows), lambda g: (at + g, 0)),
        ],
        out_specs=pl.BlockSpec((32, 2 * REL2), lambda g: (0, 0)),
        out_shape=jax.ShapeDtypeStruct((32, 2 * REL2), F32),
        scratch_shapes=[pltpu.VMEM((rows // TILE, 32 * block, TILE), F32)],
        compiler_params=pltpu.CompilerParams(vmem_limit_bytes=VMEM),
        cost_estimate=cost(2.5 * count),
        name="table_sums",
    )(first, second, across, upward)


class Place:
    def __init__(self):
        index = lax.axis_index("section")
        self.peers = lax.axis_size("section")
        self.docs = lax.axis_size("dp")
        self.half = index % 2
        self.layer = index // 2
        where = lax.axis_index("dp")
        bits = range(self.docs.bit_length() - 1)
        self.orders = [list(bits), [1, 0] + list(bits)[2:]]
        self.sides = [
            jnp.where(self.half == 0, (where >> one) & 1, (where >> two) & 1)
            for one, two in zip(*self.orders)
        ]

    def across(self, value, mask):
        return lax.ppermute(value, "section", [(i, i ^ mask) for i in range(self.peers)])

    def to_layer(self, value, layer):
        other = 1 - layer
        pairs = [(2 * other + h, 2 * layer + h) for h in range(2)]
        return lax.ppermute(value, "section", pairs)

    def facing(self, value, step):
        pairs = []
        for s in range(self.peers):
            for d in range(self.docs):
                pairs.append((s * self.docs + d, s * self.docs + (d ^ (1 << self.orders[s % 2][step]))))
        return lax.ppermute(value, ("section", "dp"), pairs)

    def joined(self, mine, theirs, side, axis=0):
        return jnp.where(
            side == 0, jnp.concatenate([mine, theirs], axis), jnp.concatenate([theirs, mine], axis)
        )

    def parted(self, value, side):
        rows = value.shape[0] // 2
        return (
            lax.dynamic_slice_in_dim(value, side * rows, rows, 0),
            lax.dynamic_slice_in_dim(value, (1 - side) * rows, rows, 0),
        )


    def over_core(self, value):
        return (value, lambda sent: self.across(sent, 1))

    def over_x(self, value):
        return (value, lambda sent: self.across(sent, 2))

    def over_dp(self, value, step):
        return (value, lambda sent: self.facing(sent, step))

    def weight_flow(self, mine, steps):
        part = mine.shape[0] >> steps
        spot = sum(side << step for step, side in enumerate(self.sides[:steps]))
        mate = self.across(mine, 1)
        got = yield self.over_x(lax.dynamic_slice_in_dim(mine, spot * part, part, 0))
        for step in range(steps):
            got = self.joined(got, (yield self.over_dp(got, step)), self.sides[step])
        return (mine, mate, got, (yield self.over_core(got)))

    def half_flow(self, full):
        keep, send = self.parted(full.astype(BF), self.half)
        return (keep, (yield self.over_core(send)))

    def scatter_flow(self, full):
        size = full.shape[0]
        terms = [(full, 0)]

        def added(offset):
            parts = [lax.dynamic_slice_in_dim(array, at + offset, size, 0) for array, at in terms]
            if len(parts) == 1:
                return parts[0]
            return sum(part.astype(F32) for part in parts).astype(BF)

        for step, side in enumerate(self.sides[:-1]):
            size //= 2
            arrived = yield self.over_dp(added((1 - side) * size), step)
            terms = [(array, at + side * size) for array, at in terms] + [(arrived, 0)]
        return added(0)

    def gather_flow(self, second, first):
        mine = jnp.where(self.layer == 1, second, first)
        sent = yield self.over_x(jnp.where(self.layer == 1, first, second))
        total = (mine.astype(F32) + sent.astype(F32)).astype(BF)
        last = len(self.sides) - 1
        total = (total.astype(F32) + (yield self.over_dp(total, last)).astype(F32)).astype(BF)
        for step, side in reversed(list(enumerate(self.sides[:-1]))):
            total = self.joined(total, (yield self.over_dp(total, step)), side)
        return total.astype(F32)

    def all_flow(self, value):
        value = value + (yield self.over_dp(value, 0))
        value = value + (yield self.over_x(value))
        for step in range(1, len(self.sides)):
            value = value + (yield self.over_dp(value, step))
        return value + (yield self.over_core(value))


class Flow:
    def __init__(self, steps):
        self.steps = steps
        self.air = self.result = None
        self.ready, self.move = next(steps)

    def land(self, arrived):
        self.air = None
        try:
            self.ready, self.move = self.steps.send(arrived)
        except StopIteration as end:
            self.ready = self.move = None
            self.result = end.value

    def go(self):
        self.air, self.ready = self.move(self.ready), None

    @property
    def busy(self):
        return self.air is not None or self.ready is not None


def pace(value, *flows):
    flows = [flow for flow in flows if flow.busy]
    flying = [flow for flow in flows if flow.air is not None]
    value, air = lax.optimization_barrier((value, [flow.air for flow in flying]))
    for flow, arrived in zip(flying, air):
        flow.land(arrived)
    flows = [flow for flow in flows if flow.busy]
    value, ready = lax.optimization_barrier((value, [flow.ready for flow in flows]))
    for flow, sent in zip(flows, ready):
        flow.air, flow.ready = flow.move(sent), None
    return value


def finished(flow):
    while flow.busy:
        pace(0, flow)
    return flow.result


def unpack_kernel(s_ref, hot_ref, vec_ref, wide_ref, bias_ref, tab_ref, line_ref):
    wide = s_ref.shape[3]
    cut = REL1 // 2
    for n in range(2):
        quarters = [s_ref[n, h].astype(F32) for h in range(2)]
        vec_ref[n] = jnp.concatenate([q[:16] for q in quarters], axis=1)
        bias_ref[n] = jnp.zeros(bias_ref.shape[1:], F32)
        for h, q in enumerate(quarters):
            for k in range(4):
                at = (4 * h + k) * wide
                wide_ref[n, :, at : at + wide] = q[5 + k : 6 + k]
            for k in range(2):
                at = (4 * h + k) * wide
                bias_ref[n, :, at : at + wide] = q[k : k + 1]
        rows = [q[16:, :TILE] for q in quarters]
        box = [r[at : at + REL2 // 2] for at in (cut, cut + REL2 // 2) for r in rows]
        fixed = jnp.floor(jnp.transpose(jnp.concatenate(box, axis=0)) * UNIT + 0.5).astype(jnp.int32)
        for p in range(tab_ref.shape[1]):
            tab_ref[n, p] = fixed[2 * p : 2 * p + 1] * 65536 + fixed[2 * p + 1 : 2 * p + 2] + 16384
        line = jnp.concatenate([r[:cut] for r in rows], axis=0).astype(BF)
        lines = dot_tn(line, hot_ref[...]) * UNIT
        for h in range(line_ref.shape[1]):
            for k in range(5):
                part = lines[h : h + 1, 2 * TILE * k : 2 * TILE * (k + 1)]
                line_ref[n, h, k : k + 1, :] = part - (h % 2) * 32768.0


def unpack(quarters, heads):
    wide = quarters.shape[-1]
    hot = jnp.asarray(line_rows().reshape(-1)[None, :] == np.arange(REL1)[:, None], BF)
    shapes = [
        ((2, 16, 2 * wide), F32), ((2, 1, 8 * wide), F32), ((2, 1, 6 * wide), F32),
        ((2, heads // 2, 1, 2 * REL2), jnp.int32), ((2, heads, 8, 2 * TILE), F32),
    ]
    vmem = pl.BlockSpec(memory_space=pltpu.VMEM)
    return pl.pallas_call(
        unpack_kernel,
        in_specs=[vmem, vmem],
        out_specs=[vmem] * len(shapes),
        out_shape=[jax.ShapeDtypeStruct(*s) for s in shapes],
        compiler_params=pltpu.CompilerParams(vmem_limit_bytes=VMEM),
        cost_estimate=cost(8),
        name="unpack",
    )(quarters, hot)


def packed(vectors, tables):
    wide = vectors[1].shape[-1]
    rows = [v.reshape(-1, wide) for v in vectors]
    rows.append(jnp.zeros((4, wide), rows[0].dtype))
    table = jnp.concatenate(tables, axis=0)
    rows.append(jnp.pad(table, ((0, 0), (0, wide - table.shape[1]))))
    return jnp.concatenate(rows, axis=0)


def local(
    section_data,
    text_len,
    patches,
    box_x,
    box_y,
    w_qkv,
    b_qv,
    w_out,
    b_out,
    norm1_gain,
    norm1_bias,
    w_in,
    b_in,
    w_back,
    b_back,
    norm2_gain,
    norm2_bias,
    rel_line,
    rel_x,
    rel_y,
):
    place = Place()
    heads = rel_line.shape[2]
    rows, width = section_data.shape[2:]
    first = place.layer == 0
    where = jnp.stack([place.layer, place.half]).astype(jnp.int32)

    entries = section_data[0]
    wf_qkv = Flow(place.weight_flow(w_qkv[0], 2))
    wf_qkv.go()
    smalls = [v[0] for v in (b_qv, b_out, norm1_gain, norm1_bias, b_in, b_back, norm2_gain, norm2_bias)]
    smalls = packed(smalls, [t[0] for t in (rel_line, rel_x, rel_y)])
    swapped = jnp.where(first, entries[1], entries[0])
    smalls, swapped = lax.optimization_barrier((smalls, swapped))
    theirs = place.across(smalls, 2)
    got = place.across(swapped, 2)
    meta = prepare(where, text_len, patches, box_x, box_y)
    meta, smalls, theirs = pace((meta, smalls, theirs), wf_qkv)
    across, upward, mask, live = meta
    smalls = place.joined(smalls[None], theirs[None], place.layer)
    mates = place.across(smalls, 1)
    w_rest = (w_out, w_in, w_back)
    wf_out, wf_in, wf_back = [Flow(place.weight_flow(w[0], 1)) for w in (w_out, w_in, w_back)]
    smalls, mates, got = pace((smalls, mates, got), wf_qkv, wf_out, wf_in, wf_back)
    smalls = place.joined(smalls[:, None], mates[:, None], place.half, 1)
    params = pace(unpack(smalls, heads), wf_qkv)
    vectors, b_in, b_qv, *scores = params
    source = jnp.where(first, entries[0], got)
    cotangent = jnp.where(first, got, entries[1])
    source, cotangent = pace((source, cotangent), wf_qkv)
    w_qkv = finished(wf_qkv)

    def forward(x, n, paced, *calls):
        qkv, qkv_t = paced(project(where, x, b_qv, w_qkv, n), wf_out)
        mixed = ()
        for part, flows in enumerate(calls):
            mixed = attend(
                qkv, qkv_t, mask, across, upward, scores[0][n], scores[1][n], len(calls), part, mixed
            )
            mixed = paced(mixed, *flows)
        weights, ct, exact, inv = mixed
        sets = [finished(flow) for flow in (wf_out, wf_in, wf_back)]
        n1, s1, hidden, tg, slope, n2, s2, y = feed(where, ct, x, live, vectors, b_in, sets, n)
        return dict(
            x=x, qkv=qkv, qkv_t=qkv_t, weights=weights, ct=ct, exact=exact, inv=inv,
            n1=n1, s1=s1, hidden=hidden, tg=tg, slope=slope, n2=n2, s2=s2, y=y,
        )

    kept = [forward(source, 0, pace, (wf_out, wf_in), (wf_out, wf_in, wf_back))]
    kept.append(forward(kept[0]["y"], 1, lambda value, *flows: value, ()))
    w_out, w_in, w_back = [finished(flow) for flow in (wf_out, wf_in, wf_back)]

    def feed_grads(dy, n):
        k = kept[n]
        return feed_back(
            where, dy, live, vectors, k["n1"], k["s1"], k["n2"], k["s2"], k["slope"], k["inv"],
            (w_back, w_in, w_out), n,
        )

    def scores_back(dc, dct, n):
        k = kept[n]
        return attend_back(k["weights"], k["qkv"], k["qkv_t"], dc, dct, k["exact"])

    def back_grad(df, n):
        return Flow(place.half_flow(dot_tn(kept[n]["tg"], df)))

    def in_grad(du, n):
        return Flow(place.half_flow(dot_tn(kept[n]["hidden"], du)))

    def mixing_grad(dqkv, da, n):
        g_qkv = dot_tn(kept[n]["x"], dqkv).astype(BF)
        g_out = dot(kept[n]["ct"], da).astype(BF)
        return Flow(place.half_flow(jnp.concatenate([g_qkv, g_out], axis=1)))

    def both_terms(flow):
        keep, arrived = finished(flow)
        return (keep.astype(F32) + arrived.astype(F32)).astype(BF)

    def feed_scatter(f_in, f_back):
        g_in, g_back = both_terms(f_in), both_terms(f_back)
        size = g_in.shape[0]
        blocks = [g_back[at : at + size] for at in range(0, g_back.shape[0], size)]
        return Flow(place.scatter_flow(jnp.concatenate([g_in] + blocks, axis=1)))

    def mix_scatter(flow):
        return Flow(place.scatter_flow(both_terms(flow)))

    def vector_rows(sums, wide, qkv):
        return jnp.concatenate([sums, wide.reshape(-1, width), qkv.reshape(-1, width)], axis=0)

    df, du, dr, da, dct, dc, sums, wide = feed_grads(cotangent, 1)
    f_back = back_grad(df, 1)
    du = pace(du, f_back)
    f_in = in_grad(du, 1)
    dc, dct = pace((dc, dct), f_back, f_in)
    dc, dct = pace((dc, dct), f_in)
    f_feed = feed_scatter(f_in, f_back)
    dc, dct = pace((dc, dct), f_feed)
    ds1, dqkv, line1 = scores_back(dc, dct, 1)
    f_mix = mixing_grad(dqkv, da, 1)
    dqkv = pace(dqkv, f_feed, f_mix)
    dx, s_qkv = input_back(where, dqkv, dr, w_qkv, 1)
    vectors1 = vector_rows(sums, wide, s_qkv)

    dx = pace(dx, f_mix)
    f_mix = mix_scatter(f_mix)
    dx = pace(dx, f_mix)
    df, du, dr, da, dct, dc, sums, wide = pace(feed_grads(dx, 0), f_feed, f_mix)
    e_back = back_grad(df, 0)
    du = pace(du, e_back)
    e_in = in_grad(du, 0)
    dc, dct = pace((dc, dct), f_mix, e_back, e_in)
    dc, dct = pace((dc, dct), e_in)
    e_feed = feed_scatter(e_in, e_back)
    dc, dct = pace((dc, dct), e_feed)
    ds0, dqkv, line0 = pace(scores_back(dc, dct, 0), e_feed)
    e_mix = mixing_grad(dqkv, da, 0)
    stores = (ds0, ds1)
    stores, dqkv = pace((stores, dqkv), e_feed, e_mix)
    s_feed = Flow(place.gather_flow(finished(f_feed), finished(e_feed)))
    stores, dqkv = pace((stores, dqkv), s_feed)
    dx, s_qkv = input_back(where, dqkv, dr, w_qkv, 0)
    dx, s_qkv, stores = pace((dx, s_qkv, stores), e_mix)
    e_mix = mix_scatter(e_mix)
    stores = pace(stores, e_mix)

    table = 0.0
    blocks = rows // TABLE_BLOCK

    def tabled(at, count, *flows):
        more = table_sums(*stores, across, upward, at, count)
        return pace((table + more, stores), *flows)

    table, stores = tabled(0, 3, s_feed, e_mix)
    table, stores = tabled(3, 3, e_mix)
    s_mix = Flow(place.gather_flow(finished(f_mix), finished(e_mix)))
    table, stores = pace((table, stores), s_mix)
    table, stores = tabled(6, 3)
    table, stores, dx = pace((table, stores, dx), s_mix)
    sent = place.across(jnp.where(first, kept[1]["y"], dx), 2)
    table, stores = tabled(9, blocks - 9)
    vectors0 = vector_rows(sums, wide, s_qkv)
    hot = jnp.asarray(line_tiles().reshape(-1)[:, None] == np.arange(REL1)[None, :], BF)
    lines = jnp.concatenate([line0, line1], axis=0).reshape(2 * heads, -1).astype(BF)
    lines = jnp.pad(dot(lines, hot), ((0, 32 - 2 * heads), (0, 0)))
    tables = jnp.concatenate([table, lines], axis=1)
    tables = jnp.pad(tables, ((0, 0), (0, width - tables.shape[1])))
    smalls = jnp.concatenate([vectors0, vectors1, tables], axis=0)
    a_small = Flow(place.all_flow(smalls))
    token, sent = pace((dx, sent), a_small)
    token = pace(token, s_feed, s_mix, a_small)
    token = pace(token, a_small)
    token = pace(token, s_feed, s_mix, a_small)
    token = pace(token, a_small)
    flows = [s_feed, s_mix, a_small]
    while any(flow.busy for flow in flows):
        token = pace(token, *flows)
    g_feed, g_mix = s_feed.result, s_mix.result
    g_qkv, g_out = g_mix[:, : 3 * width], g_mix[:, 3 * width :]
    ff = du.shape[1]
    g_in = g_feed[:, :ff]
    g_back = jnp.concatenate(
        [g_feed[:, at : at + width] for at in range(ff, g_feed.shape[1], width)], axis=0
    )

    count = vectors0.shape[0]
    v = lax.dynamic_slice_in_dim(a_small.result, place.layer * count, count, 0)
    half_width = width // 2
    v_half = lax.dynamic_slice_in_dim(v, place.half * half_width, half_width, 1)
    v_in = lax.dynamic_slice_in_dim(v, 8 + 2 * place.half, 2, 0).reshape(1, -1)
    v_qv = lax.dynamic_slice_in_dim(v, 12 + 2 * place.half, 1, 0)
    t = lax.dynamic_slice_in_dim(a_small.result, 2 * count + place.layer * heads, heads, 0).T

    def table_half(at, size):
        return lax.dynamic_slice_in_dim(t, at + place.half * size, size, 0)[None]

    t_x, t_y = table_half(0, REL2 // 2), table_half(REL2, REL2 // 2)
    t_line = table_half(2 * REL2, REL1 // 2)
    result = jnp.where(first, jnp.stack([dx, sent]), jnp.stack([sent, kept[1]["y"]]))[None]
    return (
        result, g_qkv[None], v_qv, g_out[None], v_half[0:1], v_half[1:2], v_half[2:3],
        g_in[None], v_in, g_back[None], v_half[3:4], v_half[4:5], v_half[5:6],
        t_line, t_x, t_y,
    )


def solution(mesh):
    matrix = P("section", None, None)
    vector = P("section", None)
    weights = (
        matrix, vector, matrix, vector, vector, vector, matrix, vector, matrix,
        vector, vector, vector, matrix, matrix, matrix,
    )
    data = P("section", "dp", None, None)
    return jax.shard_map(
        local,
        mesh=mesh,
        in_specs=(data, P(None, "dp"), P(None, "dp"), P(None, "dp", None), P(None, "dp", None))
        + weights,
        out_specs=(data,) + weights,
        check_vma=False,
    )
```

```python
import functools
import math

import jax
import jax.numpy as jnp
import numpy as np
from jax import lax
from jax.experimental import pallas as pl
from jax.experimental.pallas import tpu as pltpu
from jax.sharding import PartitionSpec as P

REL1 = 32
REL2 = 64
REACH1 = 128
REACH2 = 256
HEAD_DIM = 64
TEXT_MAX = 191
EPS = 1e-05
NEG = -1000000000.0
ROOT_HALF = 0.7071067811865476
INV_ROOT_TAU = 0.3989422804014327

UNIT = 4096.0
LOG2E = 1.4426950408889634
TILE = 128
VMEM = 60 * 2**20
TABLE_BLOCK = 32


def cost(us):
    return pl.CostEstimate(flops=int(us * 10**9), bytes_accessed=int(us * 10**6), transcendentals=0)


BF = jnp.bfloat16
F32 = jnp.float32
NT = (((1,), (1,)), ((), ()))
TN = (((0,), (0,)), ((), ()))


def dot(a, b):
    return jnp.dot(a, b, preferred_element_type=F32)


def dot_nt(a, b):
    return lax.dot_general(a, b, NT, preferred_element_type=F32)


def dot_tn(a, b):
    return lax.dot_general(a, b, TN, preferred_element_type=F32)


def bucket_limits(total, reach):
    half = total // 2
    exact = half // 2
    return [
        int(math.ceil(exact * (reach / exact) ** (step / (half - exact)) - 1e-09))
        for step in range(1, half - exact)
    ]


def line_bucket_np(delta):
    half = REL1 // 2
    exact = half // 2
    dist = np.abs(delta)
    far = np.full(dist.shape, exact)
    for limit in bucket_limits(REL1, REACH1):
        far = far + (dist >= limit)
    return np.where(delta > 0, half, 0) + np.where(dist < exact, dist, far)


def line_rows():
    k = np.arange(2 * TILE)
    shift = np.where(k < TILE, k, k - 2 * TILE)
    return line_bucket_np(np.stack([TILE * (s - 2) - shift for s in range(5)]))


def line_tiles():
    r = np.arange(TILE)
    return line_bucket_np(np.stack([TILE * (s - 2) + r[:, None] - r[None, :] for s in range(5)]))


def lane_pick(table, index):
    dims = lax.GatherDimensionNumbers(
        offset_dims=(),
        collapsed_slice_dims=(1,),
        start_index_map=(1,),
        operand_batching_dims=(0,),
        start_indices_batching_dims=(0,),
    )
    return lax.gather(
        table,
        index[..., None],
        dims,
        slice_sizes=(1, 1),
        mode=lax.GatherScatterMode.PROMISE_IN_BOUNDS,
    )


def attend_kernel(
    k_ref,
    qt_ref,
    vt_ref,
    mask_ref,
    x_ref,
    y_ref,
    tab_ref,
    line_ref,
    p_ref,
    c_ref,
    exact_ref,
    inv_ref,
    kaug,
    qaug,
    strip,
    scores,
):
    rows = k_ref.shape[0]
    chunk = 2 * TILE
    step = 32
    lane = lax.broadcasted_iota(jnp.int32, (rows, TILE), 1)
    keys = k_ref[...].astype(F32) * (UNIT / 8.0)
    kaug[0, :, :TILE] = jnp.where(lane < HEAD_DIM, keys, 0.0).astype(BF)
    kaug[1, :, :TILE] = jnp.where(lane < HEAD_DIM, 0.0, keys).astype(BF)
    kaug[0, :, TILE:] = mask_ref[...]
    kaug[1, :, TILE:] = mask_ref[...]
    qaug[:TILE, :] = qt_ref[...]
    qaug[TILE:, :] = jnp.ones((TILE, rows), BF)
    for head in range(2):
        for s in range(5):
            wide = jnp.broadcast_to(line_ref[head, s : s + 1, :], (TILE, 2 * TILE))
            if s in (1, 2, 3):
                wide = pltpu.roll(wide, 0, axis=1, stride=1, stride_axis=0)
            strip[head, s] = wide[:, :TILE]
    table = jnp.broadcast_to(tab_ref[0], (step, TILE))
    chunks = rows // chunk
    low = jnp.full((8, chunk), -3e38, F32)

    def score(t, n, peaks):
        cols = slice(t * chunk, (t + 1) * chunk)
        tile = pl.ds(pl.multiple_of(n * TILE, TILE), TILE)
        raw = [dot(kaug[head, tile, :], qaug[:, cols]) for head in range(2)]
        peaks = list(peaks)
        for m in range(TILE // step):
            at = pl.ds(pl.multiple_of(n * TILE + m * step, step), step)
            sub = slice(m * step, (m + 1) * step)
            parts = ([], [])
            for part in range(2):
                lanes = slice(part * TILE, (part + 1) * TILE)
                wide = slice(t * chunk + part * TILE, t * chunk + (part + 1) * TILE)
                both = lane_pick(table, x_ref[at, wide]) + lane_pick(table, y_ref[at, wide])
                off = jnp.clip(n - (2 * t + part), -2, 2) + 2
                for head, bits in ((0, both >> 16), (1, both & 0xFFFF)):
                    value = raw[head][sub, lanes] + strip[head, off, sub, :] + bits.astype(F32)
                    scores[t % 2, head, at, lanes] = value
                    parts[head].append(value)
            for head in range(2):
                wide = jnp.concatenate(parts[head], axis=1)
                for r in range(step // 8):
                    peaks[head] = jnp.maximum(peaks[head], wide[8 * r : 8 * r + 8, :])
        return tuple(peaks)

    def weigh(t, n, peaks):
        cols = slice(t * chunk, (t + 1) * chunk)
        for m in range(TILE // step):
            at = pl.ds(pl.multiple_of(n * TILE + m * step, step), step)
            for head in range(2):
                power = (scores[t % 2, head, at, :] - peaks[head]) * (LOG2E / UNIT)
                p_ref[head, at, cols] = jnp.exp2(power).astype(BF)

    ones = jnp.ones((16, rows), BF)

    def mix(t):
        cols = slice(t * chunk, (t + 1) * chunk)
        for head in range(2):
            mine = slice(head * HEAD_DIM, (head + 1) * HEAD_DIM)
            vals = jnp.concatenate([vt_ref[mine, :], ones], axis=0)
            mixed = dot(vals, p_ref[head, :, cols])
            inv = 1.0 / mixed[HEAD_DIM : HEAD_DIM + 1, :]
            exact = mixed[:HEAD_DIM, :] * inv
            exact_ref[mine, cols] = exact
            c_ref[mine, cols] = exact.astype(BF)
            inv_ref[0, head : head + 1, cols] = inv

    peaks = None
    for t in range(chunks + 1):
        old = peaks

        def both_steps(n, tops):
            if t < chunks:
                tops = score(t, n, tops)
            if t > 0:
                weigh(t - 1, n, old)
            return tops

        tops = lax.fori_loop(0, rows // TILE, both_steps, (low, low), unroll=6)
        peaks = [jnp.max(top, axis=0, keepdims=True) for top in tops]
        if t > 0:
            mix(t - 1)

def attend(qkv, qkv_t, mask, across, upward, tabs, lines, calls=1, part=0, before=()):
    rows = qkv.shape[0]
    width = qkv.shape[1] // 3
    pairs = width // TILE
    count = pairs // calls
    at = part * count
    whole = lambda p: (0, 0)
    kernel = attend_kernel
    if before:
        kernel = lambda *refs: attend_kernel(*refs[:8], *refs[12:])
    return pl.pallas_call(
        kernel,
        grid=(count,),
        in_specs=[
            pl.BlockSpec((rows, TILE), lambda p: (0, pairs + at + p)),
            pl.BlockSpec((TILE, rows), lambda p: (at + p, 0)),
            pl.BlockSpec((TILE, rows), lambda p: (2 * pairs + at + p, 0)),
            pl.BlockSpec((rows, TILE), whole),
            pl.BlockSpec((rows, rows), whole),
            pl.BlockSpec((rows, rows), whole),
            pl.BlockSpec((1, 1, TILE), lambda p: (at + p, 0, 0)),
            pl.BlockSpec((2, 8, 2 * TILE), lambda p: (at + p, 0, 0)),
        ]
        + [pl.BlockSpec(memory_space=pl.ANY) for _ in before],
        out_specs=[
            pl.BlockSpec((2, rows, rows), lambda p: (at + p, 0, 0)),
            pl.BlockSpec((TILE, rows), lambda p: (at + p, 0)),
            pl.BlockSpec((TILE, rows), lambda p: (at + p, 0)),
            pl.BlockSpec((1, 8, rows), lambda p: (at + p, 0, 0)),
        ],
        out_shape=[
            jax.ShapeDtypeStruct((2 * pairs, rows, rows), BF),
            jax.ShapeDtypeStruct((width, rows), BF),
            jax.ShapeDtypeStruct((width, rows), F32),
            jax.ShapeDtypeStruct((pairs, 8, rows), F32),
        ],
        scratch_shapes=[
            pltpu.VMEM((2, rows, 2 * TILE), BF),
            pltpu.VMEM((2 * TILE, rows), BF),
            pltpu.VMEM((2, 5, TILE, TILE), F32),
            pltpu.VMEM((2, 2, rows, 2 * TILE), F32),
        ],
        input_output_aliases={8 + n: n for n in range(len(before))},
        compiler_params=pltpu.CompilerParams(vmem_limit_bytes=VMEM),
        cost_estimate=cost(33 / calls),
        name="attend",
    )(qkv, qkv_t, qkv_t, mask, across, upward, tabs, lines, *before)


def attend_back_kernel(
    p_ref,
    q_ref,
    kt_ref,
    v_ref,
    dc_ref,
    dct_ref,
    ct_ref,
    ds_ref,
    d_ref,
    line_ref,
    dqt,
):
    rows = q_ref.shape[0]
    line_ref[...] = jnp.zeros_like(line_ref)
    product = dct_ref[...].astype(F32) * ct_ref[...]
    lane = lax.broadcasted_iota(jnp.int32, (rows, TILE), 1)
    vals = v_ref[...]
    out_k, out_v = [], []
    for head in range(2):
        mine = slice(head * HEAD_DIM, (head + 1) * HEAD_DIM)
        delta = jnp.sum(product[mine, :], axis=0, keepdims=True)
        own = (lane < HEAD_DIM) if head == 0 else (lane >= HEAD_DIM)
        picked = jnp.where(own, vals, jnp.zeros_like(vals))
        for n in range(rows // TILE):
            at = slice(n * TILE, (n + 1) * TILE)
            dp = dot(picked[at, :], dct_ref[...])
            sums = {}
            for part in range(rows // TILE):
                lanes = slice(part * TILE, (part + 1) * TILE)
                weights = p_ref[head, at, lanes].astype(F32)
                grad = weights * (dp[:, lanes] - delta[:, lanes])
                ds_ref[head, at, lanes] = grad.astype(BF)
                off = min(max(n - part, -2), 2) + 2
                sums[off] = grad if off not in sums else sums[off] + grad
            for off, value in sums.items():
                line_ref[head, off] += value
        out_k.append(dot(ds_ref[head], q_ref[...]))
        out_v.append(dot(p_ref[head], dc_ref[...]))
        dqt[mine, :] = dot(kt_ref[mine, :], ds_ref[head])
    width = d_ref.shape[1] // 3
    base = pl.multiple_of(pl.program_id(0) * TILE, TILE)
    d_ref[:, pl.ds(width + base, TILE)] = (
        jnp.where(lane < HEAD_DIM, out_k[0], out_k[1]) * 0.125
    ).astype(BF)
    d_ref[:, pl.ds(2 * width + base, TILE)] = jnp.where(lane < HEAD_DIM, out_v[0], out_v[1]).astype(BF)
    d_ref[:, pl.ds(base, TILE)] = (jnp.transpose(dqt[...]) * 0.125).astype(BF)


def attend_back(weights, qkv, qkv_t, dc, dct, ct):
    rows = qkv.shape[0]
    width = qkv.shape[1] // 3
    pairs = width // TILE
    return pl.pallas_call(
        attend_back_kernel,
        grid=(pairs,),
        in_specs=[
            pl.BlockSpec((2, rows, rows), lambda p: (p, 0, 0)),
            pl.BlockSpec((rows, TILE), lambda p: (0, p)),
            pl.BlockSpec((TILE, rows), lambda p: (pairs + p, 0)),
            pl.BlockSpec((rows, TILE), lambda p: (0, 2 * pairs + p)),
            pl.BlockSpec((rows, TILE), lambda p: (0, p)),
            pl.BlockSpec((TILE, rows), lambda p: (p, 0)),
            pl.BlockSpec((TILE, rows), lambda p: (p, 0)),
        ],
        out_specs=[
            pl.BlockSpec((2, rows, rows), lambda p: (p, 0, 0)),
            pl.BlockSpec((rows, 3 * width), lambda p: (0, 0)),
            pl.BlockSpec((2, 5, TILE, TILE), lambda p: (p, 0, 0, 0)),
        ],
        out_shape=[
            jax.ShapeDtypeStruct((2 * pairs, rows, rows), BF),
            jax.ShapeDtypeStruct((rows, 3 * width), BF),
            jax.ShapeDtypeStruct((2 * pairs, 5, TILE, TILE), F32),
        ],
        scratch_shapes=[
            pltpu.VMEM((TILE, rows), F32),
        ],
        compiler_params=pltpu.CompilerParams(vmem_limit_bytes=VMEM),
        cost_estimate=cost(20),
        name="attend_back",
    )(weights, qkv, qkv_t, qkv, dc, dct, ct)


def halves(pieces, whole, sems):
    rows = pieces[0].shape[0]
    return [(whole.at[pl.ds(half * rows, rows), :], sems.at[half]) for half in range(2)]


def load_whole(pieces, layer, where_ref, whole, sems):
    for half, (slot, sem) in enumerate(halves(pieces, whole, sems)):
        own_layer = where_ref[0] == layer
        own_half = where_ref[1] == half
        cases = (
            own_layer & own_half,
            own_layer & jnp.logical_not(own_half),
            jnp.logical_not(own_layer) & own_half,
            jnp.logical_not(own_layer) & jnp.logical_not(own_half),
        )
        for piece, case in zip(pieces, cases):

            @pl.when(case)
            def begin(piece=piece, slot=slot, sem=sem):
                pltpu.make_async_copy(piece, slot, sem).start()


def await_whole(pieces, whole, sems):
    for slot, sem in halves(pieces, whole, sems):
        pltpu.make_async_copy(pieces[0], slot, sem).wait()


def any_specs(count):
    return [pl.BlockSpec(memory_space=pl.ANY)] * count


SMEM_SPEC = pl.BlockSpec(memory_space=pltpu.SMEM)


def project_kernel(layer, where_ref, x_ref, bias_ref, m0, m1, m2, m3, o_ref, t_ref, whole, sems):
    step = pl.program_id(0)

    @pl.when(step == 0)
    def fetch():
        load_whole((m0, m1, m2, m3), layer, where_ref, whole, sems)
        await_whole((m0, m1, m2, m3), whole, sems)

    cols = o_ref.shape[1]
    at = pl.ds(pl.multiple_of(step * cols, cols), cols)
    value = (dot(x_ref[...], whole[:, at]) + bias_ref[0]).astype(BF)
    o_ref[...] = value
    t_ref[...] = jnp.transpose(value)


def project(where, x, bias, pieces, layer):
    rows = x.shape[0]
    half_rows, width = pieces[0].shape
    cols = 2 * TILE
    return pl.pallas_call(
        functools.partial(project_kernel, layer),
        grid=(width // cols,),
        in_specs=[
            SMEM_SPEC,
            pl.BlockSpec(x.shape, lambda g: (0, 0)),
            pl.BlockSpec((1, 1, cols), lambda g: (layer, 0, g)),
        ]
        + any_specs(4),
        out_specs=[
            pl.BlockSpec((rows, cols), lambda g: (0, g)),
            pl.BlockSpec((cols, rows), lambda g: (g, 0)),
        ],
        out_shape=[
            jax.ShapeDtypeStruct((rows, width), BF),
            jax.ShapeDtypeStruct((width, rows), BF),
        ],
        scratch_shapes=[pltpu.VMEM((2 * half_rows, width), BF), pltpu.SemaphoreType.DMA((2,))],
        compiler_params=pltpu.CompilerParams(vmem_limit_bytes=VMEM),
        cost_estimate=cost(10),
        name="project",
    )(where, x, bias, *pieces)


def centre(values):
    width = values.shape[1]
    centered = values - jnp.sum(values, axis=1, keepdims=True) * (1.0 / width)
    square = jnp.sum(centered * centered, axis=1, keepdims=True) * (1.0 / width)
    scale = lax.rsqrt(square + EPS)
    return (centered * scale, scale)


def centre_back(grad, normed, scale):
    width = grad.shape[1]
    mean = jnp.sum(grad, axis=1, keepdims=True) * (1.0 / width)
    along = jnp.sum(grad * normed, axis=1, keepdims=True) * (1.0 / width)
    return scale * (grad - mean - normed * along)


def feed_kernel(layer, where_ref, ct_ref, x_ref, live_ref, vec_ref, wide_ref, *rest):
    pieces, rest = rest[:12], rest[12:]
    (n1_ref, s1_ref, hid_ref, tg_ref, slope_ref, n2_ref, s2_ref, y_ref), rest = rest[:8], rest[8:]
    w_out, w_in, w_back, sems = rest
    sets = (pieces[:4], pieces[4:8], pieces[8:])
    wholes = (w_out, w_in, w_back)

    def waits(start):
        @pl.when(pl.program_id(0) == 0)
        def _():
            if start is None:
                for n in range(3):
                    load_whole(sets[n], layer, where_ref, wholes[n], sems.at[n])
            else:
                await_whole(sets[start], wholes[start], sems.at[start])

    waits(None)
    mixed = jnp.transpose(ct_ref[...])
    waits(0)
    first = x_ref[...].astype(F32) + dot(mixed, w_out[...]) + vec_ref[0, 2:3, :]
    n1, s1 = centre(first)
    n1_ref[...] = n1
    s1_ref[...] = jnp.broadcast_to(s1, s1_ref.shape)
    hidden = n1 * vec_ref[0, 3:4, :] + vec_ref[0, 4:5, :]
    low = hidden.astype(BF)
    hid_ref[...] = low
    total = hidden + vec_ref[0, 9:10, :]
    waits(1)
    chunk = 6 * TILE
    for c in range(w_in.shape[1] // chunk):
        cols = slice(c * chunk, (c + 1) * chunk)
        u = dot(low, w_in[:, cols]) + wide_ref[0, :, cols]
        phi = 0.5 + 0.5 * lax.erf(u * ROOT_HALF)
        tg = (u * phi).astype(BF)
        tg_ref[:, cols] = tg
        slope_ref[:, cols] = (phi + u * (jnp.exp(-0.5 * u * u) * INV_ROOT_TAU)).astype(BF)
        if c == 0:
            waits(2)
        total = total + dot(tg, w_back[cols, :])
    n2, s2 = centre(total)
    n2_ref[...] = n2
    s2_ref[...] = jnp.broadcast_to(s2, s2_ref.shape)
    y = n2 * vec_ref[0, 10:11, :] + vec_ref[0, 11:12, :]
    y_ref[...] = jnp.where(live_ref[:, :1] > 0.0, y, 0.0).astype(BF)


def feed(where, ct, x, live, vec, wide, sets, layer):
    rows, width = x.shape
    ff = sets[1][0].shape[1]
    block = 3 * TILE
    row = lambda cols: pl.BlockSpec((block, cols), lambda g: (g, 0))
    shapes = [
        ((rows, width), F32), ((rows, TILE), F32), ((rows, width), BF), ((rows, ff), BF), ((rows, ff), BF),
        ((rows, width), F32), ((rows, TILE), F32), ((rows, width), BF),
    ]
    return pl.pallas_call(
        functools.partial(feed_kernel, layer),
        grid=(rows // block,),
        in_specs=[
            SMEM_SPEC,
            pl.BlockSpec((width, block), lambda g: (0, g)),
            row(width),
            row(TILE),
            pl.BlockSpec((1, *vec.shape[1:]), lambda g: (layer, 0, 0)),
            pl.BlockSpec((1, 1, ff), lambda g: (layer, 0, 0)),
        ]
        + any_specs(12),
        out_specs=[row(shape[1]) for shape, _ in shapes],
        out_shape=[jax.ShapeDtypeStruct(*s) for s in shapes],
        scratch_shapes=[
            pltpu.VMEM((width, width), BF),
            pltpu.VMEM((width, ff), BF),
            pltpu.VMEM((ff, width), BF),
            pltpu.SemaphoreType.DMA((3, 2)),
        ],
        compiler_params=pltpu.CompilerParams(vmem_limit_bytes=VMEM),
        cost_estimate=cost(20),
        name="feed",
    )(where, ct, x, live, vec, wide, *sets[0], *sets[1], *sets[2])


def feed_back_kernel(layer, where_ref, dy_ref, live_ref, vec_ref, n1_ref, s1_ref, n2_ref, s2_ref, slope_ref, inv_ref, *rest):
    pieces, rest = rest[:12], rest[12:]
    (df_ref, du_ref, dr_ref, da_ref, dct_ref, dc_ref, sum_ref, wsum_ref), rest = rest[:8], rest[8:]
    w_back, w_in, w_out, sems = rest
    sets = (pieces[:4], pieces[4:8], pieces[8:])
    wholes = (w_back, w_in, w_out)

    def waits(start):
        @pl.when(pl.program_id(0) == 0)
        def _():
            if start is None:
                for n in range(3):
                    load_whole(sets[n], layer, where_ref, wholes[n], sems.at[n])
                sum_ref[...] = jnp.zeros_like(sum_ref)
                wsum_ref[...] = jnp.zeros_like(wsum_ref)
            else:
                await_whole(sets[start], wholes[start], sems.at[start])

    def add(row, value):
        sum_ref[row : row + 1, :] += jnp.sum(value, axis=0, keepdims=True)

    waits(None)
    dy = jnp.where(live_ref[:, :1] > 0.0, dy_ref[...].astype(F32), 0.0)
    n2 = n2_ref[...]
    add(4, dy * n2)
    add(5, dy)
    dr2 = centre_back(dy * vec_ref[0, 10:11, :], n2, s2_ref[:, :1])
    df = dr2.astype(BF)
    df_ref[...] = df
    add(3, df.astype(F32))
    total = dr2
    waits(0)
    chunk = 6 * TILE
    for c in range(w_in.shape[1] // chunk):
        cols = slice(c * chunk, (c + 1) * chunk)
        du = (dot_nt(df, w_back[cols, :]) * slope_ref[:, cols].astype(F32)).astype(BF)
        du_ref[:, cols] = du
        wsum_ref[:, cols] += jnp.sum(du.astype(F32), axis=0, keepdims=True)
        if c == 0:
            waits(1)
        total = total + dot_nt(du, w_in[:, cols])
    n1 = n1_ref[...]
    add(1, total * n1)
    add(2, total)
    dr1 = centre_back(total * vec_ref[0, 3:4, :], n1, s1_ref[:, :1])
    dr_ref[...] = dr1
    da = dr1.astype(BF)
    da_ref[...] = da
    add(0, da.astype(F32))
    waits(2)
    grad = dot_nt(w_out[...], da)
    for head in range(grad.shape[0] // HEAD_DIM):
        mine = slice(head * HEAD_DIM, (head + 1) * HEAD_DIM)
        inv = inv_ref[head // 2, head % 2 : head % 2 + 1, :]
        dct_ref[mine, :] = (grad[mine, :] * inv).astype(BF)
    dc_ref[...] = jnp.transpose(dct_ref[...])


def feed_back(where, dy, live, vec, n1, s1, n2, s2, slope, inv, sets, layer):
    rows, width = dy.shape
    ff = slope.shape[1]
    block = 2 * TILE
    row = lambda cols: pl.BlockSpec((block, cols), lambda g: (g, 0))
    outs = [
        ((rows, width), BF, row(width)), ((rows, ff), BF, row(ff)), ((rows, width), F32, row(width)),
        ((rows, width), BF, row(width)), ((width, rows), BF, pl.BlockSpec((width, block), lambda g: (0, g))),
        ((rows, width), BF, row(width)),
        ((8, width), F32, pl.BlockSpec((8, width), lambda g: (0, 0))),
        ((1, ff), F32, pl.BlockSpec((1, ff), lambda g: (0, 0))),
    ]
    return pl.pallas_call(
        functools.partial(feed_back_kernel, layer),
        grid=(rows // block,),
        in_specs=[
            SMEM_SPEC,
            row(width),
            row(TILE),
            pl.BlockSpec((1, *vec.shape[1:]), lambda g: (layer, 0, 0)),
            row(width),
            row(TILE),
            row(width),
            row(TILE),
            row(ff),
            pl.BlockSpec((inv.shape[0], 8, block), lambda g: (0, 0, g)),
        ]
        + any_specs(12),
        out_specs=[o[2] for o in outs],
        out_shape=[jax.ShapeDtypeStruct(o[0], o[1]) for o in outs],
        scratch_shapes=[
            pltpu.VMEM((ff, width), BF),
            pltpu.VMEM((width, ff), BF),
            pltpu.VMEM((width, width), BF),
            pltpu.SemaphoreType.DMA((3, 2)),
        ],
        compiler_params=pltpu.CompilerParams(vmem_limit_bytes=VMEM),
        cost_estimate=cost(20),
        name="feed_back",
    )(where, dy, live, vec, n1, s1, n2, s2, slope, inv, *sets[0], *sets[1], *sets[2])


def input_back_kernel(layer, where_ref, d_ref, dr_ref, m0, m1, m2, m3, o_ref, sum_ref, whole, sems):
    step = pl.program_id(0)

    @pl.when(step == 0)
    def fetch():
        load_whole((m0, m1, m2, m3), layer, where_ref, whole, sems)
        await_whole((m0, m1, m2, m3), whole, sems)
        sum_ref[...] = jnp.zeros_like(sum_ref)

    d = d_ref[...]
    sum_ref[...] += jnp.sum(d.astype(F32), axis=0, keepdims=True)
    o_ref[...] = (dr_ref[...] + dot_nt(d, whole[...])).astype(BF)


def input_back(where, dqkv, dr1, pieces, layer):
    rows, wide = dqkv.shape
    width = dr1.shape[1]
    block = 3 * TILE
    row = lambda cols: pl.BlockSpec((block, cols), lambda g: (g, 0))
    return pl.pallas_call(
        functools.partial(input_back_kernel, layer),
        grid=(rows // block,),
        in_specs=[SMEM_SPEC, row(wide), row(width)] + any_specs(4),
        out_specs=[row(width), pl.BlockSpec((1, wide), lambda g: (0, 0))],
        out_shape=[jax.ShapeDtypeStruct((rows, width), BF), jax.ShapeDtypeStruct((1, wide), F32)],
        scratch_shapes=[pltpu.VMEM((width, wide), BF), pltpu.SemaphoreType.DMA((2,))],
        compiler_params=pltpu.CompilerParams(vmem_limit_bytes=VMEM),
        cost_estimate=cost(8),
        name="input_back",
    )(where, dqkv, dr1, *pieces)


def bucket_tree(delta, total, reach):
    half = total // 2
    exact = half // 2
    limits = bucket_limits(total, reach)
    dist = jnp.abs(delta)

    def count(low, high):
        if high - low == 1:
            return jnp.where(dist >= limits[low], 1, 0)
        middle = (low + high) // 2
        above = dist >= limits[middle]
        return jnp.where(above, middle - low + 1 + count(middle + 1, high), count(low, middle))

    bucket = jnp.where(dist < exact, dist, exact + count(0, len(limits)))
    return bucket + jnp.where(delta > 0, half, 0)


def prepare_kernel(where_ref, text_ref, patch_ref, x_ref, y_ref, across_ref, upward_ref, mask_ref, live_ref):
    rows = across_ref.shape[0]
    doc = where_ref[0]
    half = where_ref[1]
    text = text_ref[half, doc]
    patches = patch_ref[half, doc]
    lane = lax.broadcasted_iota(jnp.int32, (TILE, TILE), 1)
    for ref, out, base in ((x_ref, across_ref, 0), (y_ref, upward_ref, REL2)):
        line = ref[pl.ds(half * 2 + doc, 1), :]
        for r in range(rows // TILE):
            part = jnp.broadcast_to(line[:, r * TILE : (r + 1) * TILE], (TILE, TILE))
            column = jnp.transpose(part.astype(F32)).astype(jnp.int32)
            for c in range(rows // TILE):
                cols = slice(c * TILE, (c + 1) * TILE)
                out[r * TILE : (r + 1) * TILE, cols] = bucket_tree(column - line[:, cols], REL2, REACH2) + base
    index = lax.broadcasted_iota(jnp.int32, (rows, TILE), 0)
    live = (index < text) | ((index >= TEXT_MAX) & (index < TEXT_MAX + 1 + patches))
    first = lax.broadcasted_iota(jnp.int32, (rows, TILE), 1) == 0
    live_ref[...] = jnp.where(live, 1.0, 0.0)
    mask_ref[...] = jnp.where(first & jnp.logical_not(live), NEG * UNIT, 0.0).astype(BF)


def prepare(where, text_len, patches, box_x, box_y):
    rows = box_x.shape[2]
    flat = lambda a: a.reshape(-1, rows)
    vmem = pl.BlockSpec(memory_space=pltpu.VMEM)
    return pl.pallas_call(
        prepare_kernel,
        in_specs=[SMEM_SPEC] * 3 + [vmem] * 2,
        out_specs=[vmem] * 4,
        out_shape=[
            jax.ShapeDtypeStruct((rows, rows), jnp.int32),
            jax.ShapeDtypeStruct((rows, rows), jnp.int32),
            jax.ShapeDtypeStruct((rows, TILE), BF),
            jax.ShapeDtypeStruct((rows, TILE), F32),
        ],
        compiler_params=pltpu.CompilerParams(vmem_limit_bytes=VMEM),
        cost_estimate=cost(10),
        name="prepare",
    )(where, text_len, patches, flat(box_x), flat(box_y))


def table_kernel(first_ref, second_ref, x_ref, y_ref, o_ref, scr):
    heads, block, rows = first_ref.shape
    parts = rows // TILE

    @pl.when(pl.program_id(0) == 0)
    def start():
        o_ref[...] = jnp.zeros_like(o_ref)
        scr[:, 2 * heads * block :, :] = jnp.zeros((parts, scr.shape[1] - 2 * heads * block, TILE), F32)

    for layer, ref in enumerate((first_ref, second_ref)):
        for head in range(heads):
            wide = ref[head].astype(F32)
            at = (layer * heads + head) * block
            for c in range(parts):
                scr[c, at : at + block, :] = wide[:, c * TILE : (c + 1) * TILE]
    index = lax.broadcasted_iota(jnp.int32, (REL2, rows), 0)
    total = o_ref[...]
    for j in range(block):
        grads = jnp.concatenate(
            [scr[c, pl.ds(j, 32, stride=block), :] for c in range(parts)], axis=1
        ).astype(BF)
        row_x = jnp.broadcast_to(x_ref[j : j + 1, :], (REL2, rows))
        row_y = jnp.broadcast_to(y_ref[j : j + 1, :], (REL2, rows))
        hot = jnp.concatenate(
            [
                jnp.where(row_x == index, 1.0, 0.0).astype(BF),
                jnp.where(row_y == index + REL2, 1.0, 0.0).astype(BF),
            ],
            axis=0,
        )
        total = total + dot_nt(grads, hot)
    o_ref[...] = total


def table_sums(first, second, across, upward, at, count):
    heads, rows, _ = first.shape
    block = TABLE_BLOCK
    return pl.pallas_call(
        table_kernel,
        grid=(count,),
        in_specs=[
            pl.BlockSpec((heads, block, rows), lambda g: (0, at + g, 0)),
            pl.BlockSpec((heads, block, rows), lambda g: (0, at + g, 0)),
            pl.BlockSpec((block, rows), lambda g: (at + g, 0)),
            pl.BlockSpec((block, rows), lambda g: (at + g, 0)),
        ],
        out_specs=pl.BlockSpec((32, 2 * REL2), lambda g: (0, 0)),
        out_shape=jax.ShapeDtypeStruct((32, 2 * REL2), F32),
        scratch_shapes=[pltpu.VMEM((rows // TILE, 32 * block, TILE), F32)],
        compiler_params=pltpu.CompilerParams(vmem_limit_bytes=VMEM),
        cost_estimate=cost(2.5 * count),
        name="table_sums",
    )(first, second, across, upward)


class Place:
    def __init__(self):
        index = lax.axis_index("section")
        self.peers = lax.axis_size("section")
        self.docs = lax.axis_size("dp")
        self.half = index % 2
        self.layer = index // 2
        where = lax.axis_index("dp")
        bits = range(self.docs.bit_length() - 1)
        self.orders = [list(bits), [1, 0] + list(bits)[2:]]
        self.sides = [
            jnp.where(self.half == 0, (where >> one) & 1, (where >> two) & 1)
            for one, two in zip(*self.orders)
        ]

    def across(self, value, mask):
        return lax.ppermute(value, "section", [(i, i ^ mask) for i in range(self.peers)])

    def to_layer(self, value, layer):
        other = 1 - layer
        pairs = [(2 * other + h, 2 * layer + h) for h in range(2)]
        return lax.ppermute(value, "section", pairs)

    def facing(self, value, step):
        pairs = []
        for s in range(self.peers):
            for d in range(self.docs):
                pairs.append((s * self.docs + d, s * self.docs + (d ^ (1 << self.orders[s % 2][step]))))
        return lax.ppermute(value, ("section", "dp"), pairs)

    def joined(self, mine, theirs, side, axis=0):
        return jnp.where(
            side == 0, jnp.concatenate([mine, theirs], axis), jnp.concatenate([theirs, mine], axis)
        )

    def parted(self, value, side):
        rows = value.shape[0] // 2
        return (
            lax.dynamic_slice_in_dim(value, side * rows, rows, 0),
            lax.dynamic_slice_in_dim(value, (1 - side) * rows, rows, 0),
        )


    def over_core(self, value):
        return (value, lambda sent: self.across(sent, 1))

    def over_x(self, value):
        return (value, lambda sent: self.across(sent, 2))

    def over_dp(self, value, step):
        return (value, lambda sent: self.facing(sent, step))

    def weight_flow(self, mine, steps):
        part = mine.shape[0] >> steps
        spot = sum(side << step for step, side in enumerate(self.sides[:steps]))
        mate = self.across(mine, 1)
        got = yield self.over_x(lax.dynamic_slice_in_dim(mine, spot * part, part, 0))
        for step in range(steps):
            got = self.joined(got, (yield self.over_dp(got, step)), self.sides[step])
        return (mine, mate, got, (yield self.over_core(got)))

    def half_flow(self, full):
        keep, send = self.parted(full.astype(BF), self.half)
        return (keep, (yield self.over_core(send)))

    def scatter_flow(self, full):
        size = full.shape[0]
        terms = [(full, 0)]

        def added(offset):
            parts = [lax.dynamic_slice_in_dim(array, at + offset, size, 0) for array, at in terms]
            if len(parts) == 1:
                return parts[0]
            return sum(part.astype(F32) for part in parts).astype(BF)

        for step, side in enumerate(self.sides[:-1]):
            size //= 2
            arrived = yield self.over_dp(added((1 - side) * size), step)
            terms = [(array, at + side * size) for array, at in terms] + [(arrived, 0)]
        return added(0)

    def gather_flow(self, second, first):
        mine = jnp.where(self.layer == 1, second, first)
        sent = yield self.over_x(jnp.where(self.layer == 1, first, second))
        total = (mine.astype(F32) + sent.astype(F32)).astype(BF)
        last = len(self.sides) - 1
        total = (total.astype(F32) + (yield self.over_dp(total, last)).astype(F32)).astype(BF)
        for step, side in reversed(list(enumerate(self.sides[:-1]))):
            total = self.joined(total, (yield self.over_dp(total, step)), side)
        return total.astype(F32)

    def all_flow(self, value):
        value = value + (yield self.over_dp(value, 0))
        value = value + (yield self.over_x(value))
        for step in range(1, len(self.sides)):
            value = value + (yield self.over_dp(value, step))
        return value + (yield self.over_core(value))


class Flow:
    def __init__(self, steps):
        self.steps = steps
        self.air = self.result = None
        self.ready, self.move = next(steps)

    def land(self, arrived):
        self.air = None
        try:
            self.ready, self.move = self.steps.send(arrived)
        except StopIteration as end:
            self.ready = self.move = None
            self.result = end.value

    def go(self):
        self.air, self.ready = self.move(self.ready), None

    @property
    def busy(self):
        return self.air is not None or self.ready is not None


def pace(value, *flows):
    flows = [flow for flow in flows if flow.busy]
    flying = [flow for flow in flows if flow.air is not None]
    value, air = lax.optimization_barrier((value, [flow.air for flow in flying]))
    for flow, arrived in zip(flying, air):
        flow.land(arrived)
    flows = [flow for flow in flows if flow.busy]
    value, ready = lax.optimization_barrier((value, [flow.ready for flow in flows]))
    for flow, sent in zip(flows, ready):
        flow.air, flow.ready = flow.move(sent), None
    return value


def finished(flow):
    while flow.busy:
        pace(0, flow)
    return flow.result


def unpack_kernel(s_ref, hot_ref, vec_ref, wide_ref, bias_ref, tab_ref, line_ref):
    wide = s_ref.shape[3]
    cut = REL1 // 2
    for n in range(2):
        quarters = [s_ref[n, h].astype(F32) for h in range(2)]
        vec_ref[n] = jnp.concatenate([q[:16] for q in quarters], axis=1)
        bias_ref[n] = jnp.zeros(bias_ref.shape[1:], F32)
        for h, q in enumerate(quarters):
            for k in range(4):
                at = (4 * h + k) * wide
                wide_ref[n, :, at : at + wide] = q[5 + k : 6 + k]
            for k in range(2):
                at = (4 * h + k) * wide
                bias_ref[n, :, at : at + wide] = q[k : k + 1]
        rows = [q[16:, :TILE] for q in quarters]
        box = [r[at : at + REL2 // 2] for at in (cut, cut + REL2 // 2) for r in rows]
        fixed = jnp.floor(jnp.transpose(jnp.concatenate(box, axis=0)) * UNIT + 0.5).astype(jnp.int32)
        for p in range(tab_ref.shape[1]):
            tab_ref[n, p] = fixed[2 * p : 2 * p + 1] * 65536 + fixed[2 * p + 1 : 2 * p + 2] + 16384
        line = jnp.concatenate([r[:cut] for r in rows], axis=0).astype(BF)
        lines = dot_tn(line, hot_ref[...]) * UNIT
        for h in range(line_ref.shape[1]):
            for k in range(5):
                part = lines[h : h + 1, 2 * TILE * k : 2 * TILE * (k + 1)]
                line_ref[n, h, k : k + 1, :] = part - (h % 2) * 32768.0


def unpack(quarters, heads):
    wide = quarters.shape[-1]
    hot = jnp.asarray(line_rows().reshape(-1)[None, :] == np.arange(REL1)[:, None], BF)
    shapes = [
        ((2, 16, 2 * wide), F32), ((2, 1, 8 * wide), F32), ((2, 1, 6 * wide), F32),
        ((2, heads // 2, 1, 2 * REL2), jnp.int32), ((2, heads, 8, 2 * TILE), F32),
    ]
    vmem = pl.BlockSpec(memory_space=pltpu.VMEM)
    return pl.pallas_call(
        unpack_kernel,
        in_specs=[vmem, vmem],
        out_specs=[vmem] * len(shapes),
        out_shape=[jax.ShapeDtypeStruct(*s) for s in shapes],
        compiler_params=pltpu.CompilerParams(vmem_limit_bytes=VMEM),
        cost_estimate=cost(8),
        name="unpack",
    )(quarters, hot)


def packed(vectors, tables):
    wide = vectors[1].shape[-1]
    rows = [v.reshape(-1, wide) for v in vectors]
    rows.append(jnp.zeros((4, wide), rows[0].dtype))
    table = jnp.concatenate(tables, axis=0)
    rows.append(jnp.pad(table, ((0, 0), (0, wide - table.shape[1]))))
    return jnp.concatenate(rows, axis=0)


def local(
    section_data,
    text_len,
    patches,
    box_x,
    box_y,
    w_qkv,
    b_qv,
    w_out,
    b_out,
    norm1_gain,
    norm1_bias,
    w_in,
    b_in,
    w_back,
    b_back,
    norm2_gain,
    norm2_bias,
    rel_line,
    rel_x,
    rel_y,
):
    place = Place()
    heads = rel_line.shape[2]
    rows, width = section_data.shape[2:]
    first = place.layer == 0
    where = jnp.stack([place.layer, place.half]).astype(jnp.int32)

    entries = section_data[0]
    wf_qkv = Flow(place.weight_flow(w_qkv[0], 2))
    wf_qkv.go()
    smalls = [v[0] for v in (b_qv, b_out, norm1_gain, norm1_bias, b_in, b_back, norm2_gain, norm2_bias)]
    smalls = packed(smalls, [t[0] for t in (rel_line, rel_x, rel_y)])
    swapped = jnp.where(first, entries[1], entries[0])
    smalls, swapped = lax.optimization_barrier((smalls, swapped))
    theirs = place.across(smalls, 2)
    got = place.across(swapped, 2)
    meta = prepare(where, text_len, patches, box_x, box_y)
    meta, smalls, theirs = pace((meta, smalls, theirs), wf_qkv)
    across, upward, mask, live = meta
    smalls = place.joined(smalls[None], theirs[None], place.layer)
    mates = place.across(smalls, 1)
    w_rest = (w_out, w_in, w_back)
    wf_out, wf_in, wf_back = [Flow(place.weight_flow(w[0], 1)) for w in (w_out, w_in, w_back)]
    smalls, mates, got = pace((smalls, mates, got), wf_qkv, wf_out, wf_in, wf_back)
    smalls = place.joined(smalls[:, None], mates[:, None], place.half, 1)
    params = pace(unpack(smalls, heads), wf_qkv)
    vectors, b_in, b_qv, *scores = params
    source = jnp.where(first, entries[0], got)
    cotangent = jnp.where(first, got, entries[1])
    source, cotangent = pace((source, cotangent), wf_qkv)
    w_qkv = finished(wf_qkv)

    def forward(x, n, paced, *calls):
        qkv, qkv_t = paced(project(where, x, b_qv, w_qkv, n), wf_out)
        mixed = ()
        for part, flows in enumerate(calls):
            mixed = attend(
                qkv, qkv_t, mask, across, upward, scores[0][n], scores[1][n], len(calls), part, mixed
            )
            mixed = paced(mixed, *flows)
        weights, ct, exact, inv = mixed
        sets = [finished(flow) for flow in (wf_out, wf_in, wf_back)]
        n1, s1, hidden, tg, slope, n2, s2, y = feed(where, ct, x, live, vectors, b_in, sets, n)
        return dict(
            x=x, qkv=qkv, qkv_t=qkv_t, weights=weights, ct=ct, exact=exact, inv=inv,
            n1=n1, s1=s1, hidden=hidden, tg=tg, slope=slope, n2=n2, s2=s2, y=y,
        )

    kept = [forward(source, 0, pace, (wf_out, wf_in), (wf_out, wf_in, wf_back))]
    kept.append(forward(kept[0]["y"], 1, lambda value, *flows: value, ()))
    w_out, w_in, w_back = [finished(flow) for flow in (wf_out, wf_in, wf_back)]

    def feed_grads(dy, n):
        k = kept[n]
        return feed_back(
            where, dy, live, vectors, k["n1"], k["s1"], k["n2"], k["s2"], k["slope"], k["inv"],
            (w_back, w_in, w_out), n,
        )

    def scores_back(dc, dct, n):
        k = kept[n]
        return attend_back(k["weights"], k["qkv"], k["qkv_t"], dc, dct, k["exact"])

    def back_grad(df, n):
        return Flow(place.half_flow(dot_tn(kept[n]["tg"], df)))

    def in_grad(du, n):
        return Flow(place.half_flow(dot_tn(kept[n]["hidden"], du)))

    def mixing_grad(dqkv, da, n):
        g_qkv = dot_tn(kept[n]["x"], dqkv).astype(BF)
        g_out = dot(kept[n]["ct"], da).astype(BF)
        return Flow(place.half_flow(jnp.concatenate([g_qkv, g_out], axis=1)))

    def both_terms(flow):
        keep, arrived = finished(flow)
        return (keep.astype(F32) + arrived.astype(F32)).astype(BF)

    def feed_scatter(f_in, f_back):
        g_in, g_back = both_terms(f_in), both_terms(f_back)
        size = g_in.shape[0]
        blocks = [g_back[at : at + size] for at in range(0, g_back.shape[0], size)]
        return Flow(place.scatter_flow(jnp.concatenate([g_in] + blocks, axis=1)))

    def mix_scatter(flow):
        return Flow(place.scatter_flow(both_terms(flow)))

    def vector_rows(sums, wide, qkv):
        return jnp.concatenate([sums, wide.reshape(-1, width), qkv.reshape(-1, width)], axis=0)

    df, du, dr, da, dct, dc, sums, wide = feed_grads(cotangent, 1)
    f_back = back_grad(df, 1)
    du = pace(du, f_back)
    f_in = in_grad(du, 1)
    dc, dct = pace((dc, dct), f_back, f_in)
    dc, dct = pace((dc, dct), f_in)
    f_feed = feed_scatter(f_in, f_back)
    dc, dct = pace((dc, dct), f_feed)
    ds1, dqkv, line1 = scores_back(dc, dct, 1)
    f_mix = mixing_grad(dqkv, da, 1)
    dqkv = pace(dqkv, f_feed, f_mix)
    dx, s_qkv = input_back(where, dqkv, dr, w_qkv, 1)
    vectors1 = vector_rows(sums, wide, s_qkv)

    dx = pace(dx, f_mix)
    f_mix = mix_scatter(f_mix)
    dx = pace(dx, f_mix)
    df, du, dr, da, dct, dc, sums, wide = pace(feed_grads(dx, 0), f_feed, f_mix)
    e_back = back_grad(df, 0)
    du = pace(du, e_back)
    e_in = in_grad(du, 0)
    dc, dct = pace((dc, dct), f_mix, e_back, e_in)
    dc, dct = pace((dc, dct), e_in)
    e_feed = feed_scatter(e_in, e_back)
    dc, dct = pace((dc, dct), e_feed)
    ds0, dqkv, line0 = pace(scores_back(dc, dct, 0), e_feed)
    e_mix = mixing_grad(dqkv, da, 0)
    stores = (ds0, ds1)
    stores, dqkv = pace((stores, dqkv), e_feed, e_mix)
    s_feed = Flow(place.gather_flow(finished(f_feed), finished(e_feed)))
    stores, dqkv = pace((stores, dqkv), s_feed)
    dx, s_qkv = input_back(where, dqkv, dr, w_qkv, 0)
    dx, s_qkv, stores = pace((dx, s_qkv, stores), e_mix)
    e_mix = mix_scatter(e_mix)
    stores = pace(stores, e_mix)

    table = 0.0
    blocks = rows // TABLE_BLOCK

    def tabled(at, count, *flows):
        more = table_sums(*stores, across, upward, at, count)
        return pace((table + more, stores), *flows)

    table, stores = tabled(0, 3, s_feed, e_mix)
    table, stores = tabled(3, 3, e_mix)
    s_mix = Flow(place.gather_flow(finished(f_mix), finished(e_mix)))
    table, stores = pace((table, stores), s_mix)
    table, stores = tabled(6, 3)
    table, stores, dx = pace((table, stores, dx), s_mix)
    sent = place.across(jnp.where(first, kept[1]["y"], dx), 2)
    table, stores = tabled(9, blocks - 9)
    vectors0 = vector_rows(sums, wide, s_qkv)
    hot = jnp.asarray(line_tiles().reshape(-1)[:, None] == np.arange(REL1)[None, :], BF)
    lines = jnp.concatenate([line0, line1], axis=0).reshape(2 * heads, -1).astype(BF)
    lines = jnp.pad(dot(lines, hot), ((0, 32 - 2 * heads), (0, 0)))
    tables = jnp.concatenate([table, lines], axis=1)
    tables = jnp.pad(tables, ((0, 0), (0, width - tables.shape[1])))
    smalls = jnp.concatenate([vectors0, vectors1, tables], axis=0)
    a_small = Flow(place.all_flow(smalls))
    token, sent = pace((dx, sent), a_small)
    token = pace(token, s_feed, s_mix, a_small)
    token = pace(token, a_small)
    token = pace(token, s_feed, s_mix, a_small)
    token = pace(token, a_small)
    token = pace(token, s_mix)
    flows = [s_feed, s_mix, a_small]
    while any(flow.busy for flow in flows):
        token = pace(token, *flows)
    g_feed, g_mix = s_feed.result, s_mix.result
    g_qkv, g_out = g_mix[:, : 3 * width], g_mix[:, 3 * width :]
    ff = du.shape[1]
    g_in = g_feed[:, :ff]
    g_back = jnp.concatenate(
        [g_feed[:, at : at + width] for at in range(ff, g_feed.shape[1], width)], axis=0
    )

    count = vectors0.shape[0]
    v = lax.dynamic_slice_in_dim(a_small.result, place.layer * count, count, 0)
    half_width = width // 2
    v_half = lax.dynamic_slice_in_dim(v, place.half * half_width, half_width, 1)
    v_in = lax.dynamic_slice_in_dim(v, 8 + 2 * place.half, 2, 0).reshape(1, -1)
    v_qv = lax.dynamic_slice_in_dim(v, 12 + 2 * place.half, 1, 0)
    t = lax.dynamic_slice_in_dim(a_small.result, 2 * count + place.layer * heads, heads, 0).T

    def table_half(at, size):
        return lax.dynamic_slice_in_dim(t, at + place.half * size, size, 0)[None]

    t_x, t_y = table_half(0, REL2 // 2), table_half(REL2, REL2 // 2)
    t_line = table_half(2 * REL2, REL1 // 2)
    result = jnp.where(first, jnp.stack([dx, sent]), jnp.stack([sent, kept[1]["y"]]))[None]
    return (
        result, g_qkv[None], v_qv, g_out[None], v_half[0:1], v_half[1:2], v_half[2:3],
        g_in[None], v_in, g_back[None], v_half[3:4], v_half[4:5], v_half[5:6],
        t_line, t_x, t_y,
    )


def solution(mesh):
    matrix = P("section", None, None)
    vector = P("section", None)
    weights = (
        matrix, vector, matrix, vector, vector, vector, matrix, vector, matrix,
        vector, vector, vector, matrix, matrix, matrix,
    )
    data = P("section", "dp", None, None)
    return jax.shard_map(
        local,
        mesh=mesh,
        in_specs=(data, P(None, "dp"), P(None, "dp"), P(None, "dp", None), P(None, "dp", None))
        + weights,
        out_specs=(data,) + weights,
        check_vma=False,
    )
```

```python
import functools
import math

import jax
import jax.numpy as jnp
import numpy as np
from jax import lax
from jax.experimental import pallas as pl
from jax.experimental.pallas import tpu as pltpu
from jax.sharding import PartitionSpec as P

REL1 = 32
REL2 = 64
REACH1 = 128
REACH2 = 256
HEAD_DIM = 64
TEXT_MAX = 191
EPS = 1e-05
NEG = -1000000000.0
ROOT_HALF = 0.7071067811865476
INV_ROOT_TAU = 0.3989422804014327

UNIT = 4096.0
LOG2E = 1.4426950408889634
TILE = 128
VMEM = 60 * 2**20
TABLE_BLOCK = 32


def cost(us):
    return pl.CostEstimate(flops=int(us * 10**9), bytes_accessed=int(us * 10**6), transcendentals=0)


BF = jnp.bfloat16
F32 = jnp.float32
NT = (((1,), (1,)), ((), ()))
TN = (((0,), (0,)), ((), ()))


def dot(a, b):
    return jnp.dot(a, b, preferred_element_type=F32)


def dot_nt(a, b):
    return lax.dot_general(a, b, NT, preferred_element_type=F32)


def dot_tn(a, b):
    return lax.dot_general(a, b, TN, preferred_element_type=F32)


def bucket_limits(total, reach):
    half = total // 2
    exact = half // 2
    return [
        int(math.ceil(exact * (reach / exact) ** (step / (half - exact)) - 1e-09))
        for step in range(1, half - exact)
    ]


def line_bucket_np(delta):
    half = REL1 // 2
    exact = half // 2
    dist = np.abs(delta)
    far = np.full(dist.shape, exact)
    for limit in bucket_limits(REL1, REACH1):
        far = far + (dist >= limit)
    return np.where(delta > 0, half, 0) + np.where(dist < exact, dist, far)


def line_rows():
    k = np.arange(2 * TILE)
    shift = np.where(k < TILE, k, k - 2 * TILE)
    return line_bucket_np(np.stack([TILE * (s - 2) - shift for s in range(5)]))


def line_tiles():
    r = np.arange(TILE)
    return line_bucket_np(np.stack([TILE * (s - 2) + r[:, None] - r[None, :] for s in range(5)]))


def lane_pick(table, index):
    dims = lax.GatherDimensionNumbers(
        offset_dims=(),
        collapsed_slice_dims=(1,),
        start_index_map=(1,),
        operand_batching_dims=(0,),
        start_indices_batching_dims=(0,),
    )
    return lax.gather(
        table,
        index[..., None],
        dims,
        slice_sizes=(1, 1),
        mode=lax.GatherScatterMode.PROMISE_IN_BOUNDS,
    )


def attend_kernel(
    k_ref,
    qt_ref,
    vt_ref,
    mask_ref,
    x_ref,
    y_ref,
    tab_ref,
    line_ref,
    p_ref,
    c_ref,
    exact_ref,
    inv_ref,
    kaug,
    qaug,
    strip,
    scores,
):
    rows = k_ref.shape[0]
    chunk = 2 * TILE
    step = 32
    lane = lax.broadcasted_iota(jnp.int32, (rows, TILE), 1)
    keys = k_ref[...].astype(F32) * (UNIT / 8.0)
    kaug[0, :, :TILE] = jnp.where(lane < HEAD_DIM, keys, 0.0).astype(BF)
    kaug[1, :, :TILE] = jnp.where(lane < HEAD_DIM, 0.0, keys).astype(BF)
    kaug[0, :, TILE:] = mask_ref[...]
    kaug[1, :, TILE:] = mask_ref[...]
    qaug[:TILE, :] = qt_ref[...]
    qaug[TILE:, :] = jnp.ones((TILE, rows), BF)
    for head in range(2):
        for s in range(5):
            wide = jnp.broadcast_to(line_ref[head, s : s + 1, :], (TILE, 2 * TILE))
            if s in (1, 2, 3):
                wide = pltpu.roll(wide, 0, axis=1, stride=1, stride_axis=0)
            strip[head, s] = wide[:, :TILE]
    table = jnp.broadcast_to(tab_ref[0], (step, TILE))
    chunks = rows // chunk
    low = jnp.full((8, chunk), -3e38, F32)

    def score(t, n, peaks):
        cols = slice(t * chunk, (t + 1) * chunk)
        tile = pl.ds(pl.multiple_of(n * TILE, TILE), TILE)
        raw = [dot(kaug[head, tile, :], qaug[:, cols]) for head in range(2)]
        peaks = list(peaks)
        for m in range(TILE // step):
            at = pl.ds(pl.multiple_of(n * TILE + m * step, step), step)
            sub = slice(m * step, (m + 1) * step)
            parts = ([], [])
            for part in range(2):
                lanes = slice(part * TILE, (part + 1) * TILE)
                wide = slice(t * chunk + part * TILE, t * chunk + (part + 1) * TILE)
                both = lane_pick(table, x_ref[at, wide]) + lane_pick(table, y_ref[at, wide])
                off = jnp.clip(n - (2 * t + part), -2, 2) + 2
                for head, bits in ((0, both >> 16), (1, both & 0xFFFF)):
                    value = raw[head][sub, lanes] + strip[head, off, sub, :] + bits.astype(F32)
                    scores[t % 2, head, at, lanes] = value
                    parts[head].append(value)
            for head in range(2):
                wide = jnp.concatenate(parts[head], axis=1)
                for r in range(step // 8):
                    peaks[head] = jnp.maximum(peaks[head], wide[8 * r : 8 * r + 8, :])
        return tuple(peaks)

    def weigh(t, n, peaks):
        cols = slice(t * chunk, (t + 1) * chunk)
        for m in range(TILE // step):
            at = pl.ds(pl.multiple_of(n * TILE + m * step, step), step)
            for head in range(2):
                power = (scores[t % 2, head, at, :] - peaks[head]) * (LOG2E / UNIT)
                p_ref[head, at, cols] = jnp.exp2(power).astype(BF)

    ones = jnp.ones((16, rows), BF)

    def mix(t):
        cols = slice(t * chunk, (t + 1) * chunk)
        for head in range(2):
            mine = slice(head * HEAD_DIM, (head + 1) * HEAD_DIM)
            vals = jnp.concatenate([vt_ref[mine, :], ones], axis=0)
            mixed = dot(vals, p_ref[head, :, cols])
            inv = 1.0 / mixed[HEAD_DIM : HEAD_DIM + 1, :]
            exact = mixed[:HEAD_DIM, :] * inv
            exact_ref[mine, cols] = exact
            c_ref[mine, cols] = exact.astype(BF)
            inv_ref[0, head : head + 1, cols] = inv

    peaks = None
    for t in range(chunks + 1):
        old = peaks

        def both_steps(n, tops):
            if t < chunks:
                tops = score(t, n, tops)
            if t > 0:
                weigh(t - 1, n, old)
            return tops

        tops = lax.fori_loop(0, rows // TILE, both_steps, (low, low), unroll=6)
        peaks = [jnp.max(top, axis=0, keepdims=True) for top in tops]
        if t > 0:
            mix(t - 1)

def attend(qkv, qkv_t, mask, across, upward, tabs, lines, calls=1, part=0, before=()):
    rows = qkv.shape[0]
    width = qkv.shape[1] // 3
    pairs = width // TILE
    count = pairs // calls
    at = part * count
    whole = lambda p: (0, 0)
    kernel = attend_kernel
    if before:
        kernel = lambda *refs: attend_kernel(*refs[:8], *refs[12:])
    return pl.pallas_call(
        kernel,
        grid=(count,),
        in_specs=[
            pl.BlockSpec((rows, TILE), lambda p: (0, pairs + at + p)),
            pl.BlockSpec((TILE, rows), lambda p: (at + p, 0)),
            pl.BlockSpec((TILE, rows), lambda p: (2 * pairs + at + p, 0)),
            pl.BlockSpec((rows, TILE), whole),
            pl.BlockSpec((rows, rows), whole),
            pl.BlockSpec((rows, rows), whole),
            pl.BlockSpec((1, 1, TILE), lambda p: (at + p, 0, 0)),
            pl.BlockSpec((2, 8, 2 * TILE), lambda p: (at + p, 0, 0)),
        ]
        + [pl.BlockSpec(memory_space=pl.ANY) for _ in before],
        out_specs=[
            pl.BlockSpec((2, rows, rows), lambda p: (at + p, 0, 0)),
            pl.BlockSpec((TILE, rows), lambda p: (at + p, 0)),
            pl.BlockSpec((TILE, rows), lambda p: (at + p, 0)),
            pl.BlockSpec((1, 8, rows), lambda p: (at + p, 0, 0)),
        ],
        out_shape=[
            jax.ShapeDtypeStruct((2 * pairs, rows, rows), BF),
            jax.ShapeDtypeStruct((width, rows), BF),
            jax.ShapeDtypeStruct((width, rows), F32),
            jax.ShapeDtypeStruct((pairs, 8, rows), F32),
        ],
        scratch_shapes=[
            pltpu.VMEM((2, rows, 2 * TILE), BF),
            pltpu.VMEM((2 * TILE, rows), BF),
            pltpu.VMEM((2, 5, TILE, TILE), F32),
            pltpu.VMEM((2, 2, rows, 2 * TILE), F32),
        ],
        input_output_aliases={8 + n: n for n in range(len(before))},
        compiler_params=pltpu.CompilerParams(vmem_limit_bytes=VMEM),
        cost_estimate=cost(33 / calls),
        name="attend",
    )(qkv, qkv_t, qkv_t, mask, across, upward, tabs, lines, *before)


def attend_back_kernel(
    p_ref,
    q_ref,
    kt_ref,
    v_ref,
    dc_ref,
    dct_ref,
    ct_ref,
    ds_ref,
    d_ref,
    line_ref,
    dqt,
):
    rows = q_ref.shape[0]
    line_ref[...] = jnp.zeros_like(line_ref)
    product = dct_ref[...].astype(F32) * ct_ref[...]
    lane = lax.broadcasted_iota(jnp.int32, (rows, TILE), 1)
    vals = v_ref[...]
    out_k, out_v = [], []
    for head in range(2):
        mine = slice(head * HEAD_DIM, (head + 1) * HEAD_DIM)
        delta = jnp.sum(product[mine, :], axis=0, keepdims=True)
        own = (lane < HEAD_DIM) if head == 0 else (lane >= HEAD_DIM)
        picked = jnp.where(own, vals, jnp.zeros_like(vals))
        for n in range(rows // TILE):
            at = slice(n * TILE, (n + 1) * TILE)
            dp = dot(picked[at, :], dct_ref[...])
            sums = {}
            for part in range(rows // TILE):
                lanes = slice(part * TILE, (part + 1) * TILE)
                weights = p_ref[head, at, lanes].astype(F32)
                grad = weights * (dp[:, lanes] - delta[:, lanes])
                ds_ref[head, at, lanes] = grad.astype(BF)
                off = min(max(n - part, -2), 2) + 2
                sums[off] = grad if off not in sums else sums[off] + grad
            for off, value in sums.items():
                line_ref[head, off] += value
        out_k.append(dot(ds_ref[head], q_ref[...]))
        out_v.append(dot(p_ref[head], dc_ref[...]))
        dqt[mine, :] = dot(kt_ref[mine, :], ds_ref[head])
    width = d_ref.shape[1] // 3
    base = pl.multiple_of(pl.program_id(0) * TILE, TILE)
    d_ref[:, pl.ds(width + base, TILE)] = (
        jnp.where(lane < HEAD_DIM, out_k[0], out_k[1]) * 0.125
    ).astype(BF)
    d_ref[:, pl.ds(2 * width + base, TILE)] = jnp.where(lane < HEAD_DIM, out_v[0], out_v[1]).astype(BF)
    d_ref[:, pl.ds(base, TILE)] = (jnp.transpose(dqt[...]) * 0.125).astype(BF)


def attend_back(weights, qkv, qkv_t, dc, dct, ct):
    rows = qkv.shape[0]
    width = qkv.shape[1] // 3
    pairs = width // TILE
    return pl.pallas_call(
        attend_back_kernel,
        grid=(pairs,),
        in_specs=[
            pl.BlockSpec((2, rows, rows), lambda p: (p, 0, 0)),
            pl.BlockSpec((rows, TILE), lambda p: (0, p)),
            pl.BlockSpec((TILE, rows), lambda p: (pairs + p, 0)),
            pl.BlockSpec((rows, TILE), lambda p: (0, 2 * pairs + p)),
            pl.BlockSpec((rows, TILE), lambda p: (0, p)),
            pl.BlockSpec((TILE, rows), lambda p: (p, 0)),
            pl.BlockSpec((TILE, rows), lambda p: (p, 0)),
        ],
        out_specs=[
            pl.BlockSpec((2, rows, rows), lambda p: (p, 0, 0)),
            pl.BlockSpec((rows, 3 * width), lambda p: (0, 0)),
            pl.BlockSpec((2, 5, TILE, TILE), lambda p: (p, 0, 0, 0)),
        ],
        out_shape=[
            jax.ShapeDtypeStruct((2 * pairs, rows, rows), BF),
            jax.ShapeDtypeStruct((rows, 3 * width), BF),
            jax.ShapeDtypeStruct((2 * pairs, 5, TILE, TILE), F32),
        ],
        scratch_shapes=[
            pltpu.VMEM((TILE, rows), F32),
        ],
        compiler_params=pltpu.CompilerParams(vmem_limit_bytes=VMEM),
        cost_estimate=cost(20),
        name="attend_back",
    )(weights, qkv, qkv_t, qkv, dc, dct, ct)


def halves(pieces, whole, sems):
    rows = pieces[0].shape[0]
    return [(whole.at[pl.ds(half * rows, rows), :], sems.at[half]) for half in range(2)]


def load_whole(pieces, layer, where_ref, whole, sems):
    for half, (slot, sem) in enumerate(halves(pieces, whole, sems)):
        own_layer = where_ref[0] == layer
        own_half = where_ref[1] == half
        cases = (
            own_layer & own_half,
            own_layer & jnp.logical_not(own_half),
            jnp.logical_not(own_layer) & own_half,
            jnp.logical_not(own_layer) & jnp.logical_not(own_half),
        )
        for piece, case in zip(pieces, cases):

            @pl.when(case)
            def begin(piece=piece, slot=slot, sem=sem):
                pltpu.make_async_copy(piece, slot, sem).start()


def await_whole(pieces, whole, sems):
    for slot, sem in halves(pieces, whole, sems):
        pltpu.make_async_copy(pieces[0], slot, sem).wait()


def any_specs(count):
    return [pl.BlockSpec(memory_space=pl.ANY)] * count


SMEM_SPEC = pl.BlockSpec(memory_space=pltpu.SMEM)


def project_kernel(layer, where_ref, x_ref, bias_ref, m0, m1, m2, m3, o_ref, t_ref, whole, sems):
    step = pl.program_id(0)

    @pl.when(step == 0)
    def fetch():
        load_whole((m0, m1, m2, m3), layer, where_ref, whole, sems)
        await_whole((m0, m1, m2, m3), whole, sems)

    cols = o_ref.shape[1]
    at = pl.ds(pl.multiple_of(step * cols, cols), cols)
    value = (dot(x_ref[...], whole[:, at]) + bias_ref[0]).astype(BF)
    o_ref[...] = value
    t_ref[...] = jnp.transpose(value)


def project(where, x, bias, pieces, layer):
    rows = x.shape[0]
    half_rows, width = pieces[0].shape
    cols = 3 * TILE
    return pl.pallas_call(
        functools.partial(project_kernel, layer),
        grid=(width // cols,),
        in_specs=[
            SMEM_SPEC,
            pl.BlockSpec(x.shape, lambda g: (0, 0)),
            pl.BlockSpec((1, 1, cols), lambda g: (layer, 0, g)),
        ]
        + any_specs(4),
        out_specs=[
            pl.BlockSpec((rows, cols), lambda g: (0, g)),
            pl.BlockSpec((cols, rows), lambda g: (g, 0)),
        ],
        out_shape=[
            jax.ShapeDtypeStruct((rows, width), BF),
            jax.ShapeDtypeStruct((width, rows), BF),
        ],
        scratch_shapes=[pltpu.VMEM((2 * half_rows, width), BF), pltpu.SemaphoreType.DMA((2,))],
        compiler_params=pltpu.CompilerParams(vmem_limit_bytes=VMEM),
        cost_estimate=cost(10),
        name="project",
    )(where, x, bias, *pieces)


def centre(values):
    width = values.shape[1]
    centered = values - jnp.sum(values, axis=1, keepdims=True) * (1.0 / width)
    square = jnp.sum(centered * centered, axis=1, keepdims=True) * (1.0 / width)
    scale = lax.rsqrt(square + EPS)
    return (centered * scale, scale)


def centre_back(grad, normed, scale):
    width = grad.shape[1]
    mean = jnp.sum(grad, axis=1, keepdims=True) * (1.0 / width)
    along = jnp.sum(grad * normed, axis=1, keepdims=True) * (1.0 / width)
    return scale * (grad - mean - normed * along)


def feed_kernel(layer, where_ref, ct_ref, x_ref, live_ref, vec_ref, wide_ref, *rest):
    pieces, rest = rest[:12], rest[12:]
    (n1_ref, s1_ref, hid_ref, tg_ref, slope_ref, n2_ref, s2_ref, y_ref), rest = rest[:8], rest[8:]
    w_out, w_in, w_back, sems = rest
    sets = (pieces[:4], pieces[4:8], pieces[8:])
    wholes = (w_out, w_in, w_back)

    def waits(start):
        @pl.when(pl.program_id(0) == 0)
        def _():
            if start is None:
                for n in range(3):
                    load_whole(sets[n], layer, where_ref, wholes[n], sems.at[n])
            else:
                await_whole(sets[start], wholes[start], sems.at[start])

    waits(None)
    mixed = jnp.transpose(ct_ref[...])
    waits(0)
    first = x_ref[...].astype(F32) + dot(mixed, w_out[...]) + vec_ref[0, 2:3, :]
    n1, s1 = centre(first)
    n1_ref[...] = n1
    s1_ref[...] = jnp.broadcast_to(s1, s1_ref.shape)
    hidden = n1 * vec_ref[0, 3:4, :] + vec_ref[0, 4:5, :]
    low = hidden.astype(BF)
    hid_ref[...] = low
    total = hidden + vec_ref[0, 9:10, :]
    waits(1)
    chunk = 6 * TILE
    for c in range(w_in.shape[1] // chunk):
        cols = slice(c * chunk, (c + 1) * chunk)
        u = dot(low, w_in[:, cols]) + wide_ref[0, :, cols]
        phi = 0.5 + 0.5 * lax.erf(u * ROOT_HALF)
        tg = (u * phi).astype(BF)
        tg_ref[:, cols] = tg
        slope_ref[:, cols] = (phi + u * (jnp.exp(-0.5 * u * u) * INV_ROOT_TAU)).astype(BF)
        if c == 0:
            waits(2)
        total = total + dot(tg, w_back[cols, :])
    n2, s2 = centre(total)
    n2_ref[...] = n2
    s2_ref[...] = jnp.broadcast_to(s2, s2_ref.shape)
    y = n2 * vec_ref[0, 10:11, :] + vec_ref[0, 11:12, :]
    y_ref[...] = jnp.where(live_ref[:, :1] > 0.0, y, 0.0).astype(BF)


def feed(where, ct, x, live, vec, wide, sets, layer):
    rows, width = x.shape
    ff = sets[1][0].shape[1]
    block = 3 * TILE
    row = lambda cols: pl.BlockSpec((block, cols), lambda g: (g, 0))
    shapes = [
        ((rows, width), F32), ((rows, TILE), F32), ((rows, width), BF), ((rows, ff), BF), ((rows, ff), BF),
        ((rows, width), F32), ((rows, TILE), F32), ((rows, width), BF),
    ]
    return pl.pallas_call(
        functools.partial(feed_kernel, layer),
        grid=(rows // block,),
        in_specs=[
            SMEM_SPEC,
            pl.BlockSpec((width, block), lambda g: (0, g)),
            row(width),
            row(TILE),
            pl.BlockSpec((1, *vec.shape[1:]), lambda g: (layer, 0, 0)),
            pl.BlockSpec((1, 1, ff), lambda g: (layer, 0, 0)),
        ]
        + any_specs(12),
        out_specs=[row(shape[1]) for shape, _ in shapes],
        out_shape=[jax.ShapeDtypeStruct(*s) for s in shapes],
        scratch_shapes=[
            pltpu.VMEM((width, width), BF),
            pltpu.VMEM((width, ff), BF),
            pltpu.VMEM((ff, width), BF),
            pltpu.SemaphoreType.DMA((3, 2)),
        ],
        compiler_params=pltpu.CompilerParams(vmem_limit_bytes=VMEM),
        cost_estimate=cost(20),
        name="feed",
    )(where, ct, x, live, vec, wide, *sets[0], *sets[1], *sets[2])


def feed_back_kernel(layer, where_ref, dy_ref, live_ref, vec_ref, n1_ref, s1_ref, n2_ref, s2_ref, slope_ref, inv_ref, *rest):
    pieces, rest = rest[:12], rest[12:]
    (df_ref, du_ref, dr_ref, da_ref, dct_ref, dc_ref, sum_ref, wsum_ref), rest = rest[:8], rest[8:]
    w_back, w_in, w_out, sems = rest
    sets = (pieces[:4], pieces[4:8], pieces[8:])
    wholes = (w_back, w_in, w_out)

    def waits(start):
        @pl.when(pl.program_id(0) == 0)
        def _():
            if start is None:
                for n in range(3):
                    load_whole(sets[n], layer, where_ref, wholes[n], sems.at[n])
                sum_ref[...] = jnp.zeros_like(sum_ref)
                wsum_ref[...] = jnp.zeros_like(wsum_ref)
            else:
                await_whole(sets[start], wholes[start], sems.at[start])

    def add(row, value):
        sum_ref[row : row + 1, :] += jnp.sum(value, axis=0, keepdims=True)

    waits(None)
    dy = jnp.where(live_ref[:, :1] > 0.0, dy_ref[...].astype(F32), 0.0)
    n2 = n2_ref[...]
    add(4, dy * n2)
    add(5, dy)
    dr2 = centre_back(dy * vec_ref[0, 10:11, :], n2, s2_ref[:, :1])
    df = dr2.astype(BF)
    df_ref[...] = df
    add(3, df.astype(F32))
    total = dr2
    waits(0)
    chunk = 6 * TILE
    for c in range(w_in.shape[1] // chunk):
        cols = slice(c * chunk, (c + 1) * chunk)
        du = (dot_nt(df, w_back[cols, :]) * slope_ref[:, cols].astype(F32)).astype(BF)
        du_ref[:, cols] = du
        wsum_ref[:, cols] += jnp.sum(du.astype(F32), axis=0, keepdims=True)
        if c == 0:
            waits(1)
        total = total + dot_nt(du, w_in[:, cols])
    n1 = n1_ref[...]
    add(1, total * n1)
    add(2, total)
    dr1 = centre_back(total * vec_ref[0, 3:4, :], n1, s1_ref[:, :1])
    dr_ref[...] = dr1
    da = dr1.astype(BF)
    da_ref[...] = da
    add(0, da.astype(F32))
    waits(2)
    grad = dot_nt(w_out[...], da)
    for head in range(grad.shape[0] // HEAD_DIM):
        mine = slice(head * HEAD_DIM, (head + 1) * HEAD_DIM)
        inv = inv_ref[head // 2, head % 2 : head % 2 + 1, :]
        dct_ref[mine, :] = (grad[mine, :] * inv).astype(BF)
    dc_ref[...] = jnp.transpose(dct_ref[...])


def feed_back(where, dy, live, vec, n1, s1, n2, s2, slope, inv, sets, layer):
    rows, width = dy.shape
    ff = slope.shape[1]
    block = 2 * TILE
    row = lambda cols: pl.BlockSpec((block, cols), lambda g: (g, 0))
    outs = [
        ((rows, width), BF, row(width)), ((rows, ff), BF, row(ff)), ((rows, width), F32, row(width)),
        ((rows, width), BF, row(width)), ((width, rows), BF, pl.BlockSpec((width, block), lambda g: (0, g))),
        ((rows, width), BF, row(width)),
        ((8, width), F32, pl.BlockSpec((8, width), lambda g: (0, 0))),
        ((1, ff), F32, pl.BlockSpec((1, ff), lambda g: (0, 0))),
    ]
    return pl.pallas_call(
        functools.partial(feed_back_kernel, layer),
        grid=(rows // block,),
        in_specs=[
            SMEM_SPEC,
            row(width),
            row(TILE),
            pl.BlockSpec((1, *vec.shape[1:]), lambda g: (layer, 0, 0)),
            row(width),
            row(TILE),
            row(width),
            row(TILE),
            row(ff),
            pl.BlockSpec((inv.shape[0], 8, block), lambda g: (0, 0, g)),
        ]
        + any_specs(12),
        out_specs=[o[2] for o in outs],
        out_shape=[jax.ShapeDtypeStruct(o[0], o[1]) for o in outs],
        scratch_shapes=[
            pltpu.VMEM((ff, width), BF),
            pltpu.VMEM((width, ff), BF),
            pltpu.VMEM((width, width), BF),
            pltpu.SemaphoreType.DMA((3, 2)),
        ],
        compiler_params=pltpu.CompilerParams(vmem_limit_bytes=VMEM),
        cost_estimate=cost(20),
        name="feed_back",
    )(where, dy, live, vec, n1, s1, n2, s2, slope, inv, *sets[0], *sets[1], *sets[2])


def input_back_kernel(layer, where_ref, d_ref, dr_ref, m0, m1, m2, m3, o_ref, sum_ref, whole, sems):
    step = pl.program_id(0)

    @pl.when(step == 0)
    def fetch():
        load_whole((m0, m1, m2, m3), layer, where_ref, whole, sems)
        await_whole((m0, m1, m2, m3), whole, sems)
        sum_ref[...] = jnp.zeros_like(sum_ref)

    d = d_ref[...]
    sum_ref[...] += jnp.sum(d.astype(F32), axis=0, keepdims=True)
    o_ref[...] = (dr_ref[...] + dot_nt(d, whole[...])).astype(BF)


def input_back(where, dqkv, dr1, pieces, layer):
    rows, wide = dqkv.shape
    width = dr1.shape[1]
    block = 3 * TILE
    row = lambda cols: pl.BlockSpec((block, cols), lambda g: (g, 0))
    return pl.pallas_call(
        functools.partial(input_back_kernel, layer),
        grid=(rows // block,),
        in_specs=[SMEM_SPEC, row(wide), row(width)] + any_specs(4),
        out_specs=[row(width), pl.BlockSpec((1, wide), lambda g: (0, 0))],
        out_shape=[jax.ShapeDtypeStruct((rows, width), BF), jax.ShapeDtypeStruct((1, wide), F32)],
        scratch_shapes=[pltpu.VMEM((width, wide), BF), pltpu.SemaphoreType.DMA((2,))],
        compiler_params=pltpu.CompilerParams(vmem_limit_bytes=VMEM),
        cost_estimate=cost(8),
        name="input_back",
    )(where, dqkv, dr1, *pieces)


def bucket_tree(delta, total, reach):
    half = total // 2
    exact = half // 2
    limits = bucket_limits(total, reach)
    dist = jnp.abs(delta)

    def count(low, high):
        if high - low == 1:
            return jnp.where(dist >= limits[low], 1, 0)
        middle = (low + high) // 2
        above = dist >= limits[middle]
        return jnp.where(above, middle - low + 1 + count(middle + 1, high), count(low, middle))

    bucket = jnp.where(dist < exact, dist, exact + count(0, len(limits)))
    return bucket + jnp.where(delta > 0, half, 0)


def prepare_kernel(where_ref, text_ref, patch_ref, x_ref, y_ref, across_ref, upward_ref, mask_ref, live_ref):
    rows = across_ref.shape[0]
    doc = where_ref[0]
    half = where_ref[1]
    text = text_ref[half, doc]
    patches = patch_ref[half, doc]
    lane = lax.broadcasted_iota(jnp.int32, (TILE, TILE), 1)
    for ref, out, base in ((x_ref, across_ref, 0), (y_ref, upward_ref, REL2)):
        line = ref[pl.ds(half * 2 + doc, 1), :]
        for r in range(rows // TILE):
            part = jnp.broadcast_to(line[:, r * TILE : (r + 1) * TILE], (TILE, TILE))
            column = jnp.transpose(part.astype(F32)).astype(jnp.int32)
            for c in range(rows // TILE):
                cols = slice(c * TILE, (c + 1) * TILE)
                out[r * TILE : (r + 1) * TILE, cols] = bucket_tree(column - line[:, cols], REL2, REACH2) + base
    index = lax.broadcasted_iota(jnp.int32, (rows, TILE), 0)
    live = (index < text) | ((index >= TEXT_MAX) & (index < TEXT_MAX + 1 + patches))
    first = lax.broadcasted_iota(jnp.int32, (rows, TILE), 1) == 0
    live_ref[...] = jnp.where(live, 1.0, 0.0)
    mask_ref[...] = jnp.where(first & jnp.logical_not(live), NEG * UNIT, 0.0).astype(BF)


def prepare(where, text_len, patches, box_x, box_y):
    rows = box_x.shape[2]
    flat = lambda a: a.reshape(-1, rows)
    vmem = pl.BlockSpec(memory_space=pltpu.VMEM)
    return pl.pallas_call(
        prepare_kernel,
        in_specs=[SMEM_SPEC] * 3 + [vmem] * 2,
        out_specs=[vmem] * 4,
        out_shape=[
            jax.ShapeDtypeStruct((rows, rows), jnp.int32),
            jax.ShapeDtypeStruct((rows, rows), jnp.int32),
            jax.ShapeDtypeStruct((rows, TILE), BF),
            jax.ShapeDtypeStruct((rows, TILE), F32),
        ],
        compiler_params=pltpu.CompilerParams(vmem_limit_bytes=VMEM),
        cost_estimate=cost(10),
        name="prepare",
    )(where, text_len, patches, flat(box_x), flat(box_y))


def table_kernel(first_ref, second_ref, x_ref, y_ref, o_ref, scr):
    heads, block, rows = first_ref.shape
    parts = rows // TILE

    @pl.when(pl.program_id(0) == 0)
    def start():
        o_ref[...] = jnp.zeros_like(o_ref)
        scr[:, 2 * heads * block :, :] = jnp.zeros((parts, scr.shape[1] - 2 * heads * block, TILE), F32)

    for layer, ref in enumerate((first_ref, second_ref)):
        for head in range(heads):
            wide = ref[head].astype(F32)
            at = (layer * heads + head) * block
            for c in range(parts):
                scr[c, at : at + block, :] = wide[:, c * TILE : (c + 1) * TILE]
    index = lax.broadcasted_iota(jnp.int32, (REL2, rows), 0)
    total = o_ref[...]
    for j in range(block):
        grads = jnp.concatenate(
            [scr[c, pl.ds(j, 32, stride=block), :] for c in range(parts)], axis=1
        ).astype(BF)
        row_x = jnp.broadcast_to(x_ref[j : j + 1, :], (REL2, rows))
        row_y = jnp.broadcast_to(y_ref[j : j + 1, :], (REL2, rows))
        hot = jnp.concatenate(
            [
                jnp.where(row_x == index, 1.0, 0.0).astype(BF),
                jnp.where(row_y == index + REL2, 1.0, 0.0).astype(BF),
            ],
            axis=0,
        )
        total = total + dot_nt(grads, hot)
    o_ref[...] = total


def table_sums(first, second, across, upward, at, count):
    heads, rows, _ = first.shape
    block = TABLE_BLOCK
    return pl.pallas_call(
        table_kernel,
        grid=(count,),
        in_specs=[
            pl.BlockSpec((heads, block, rows), lambda g: (0, at + g, 0)),
            pl.BlockSpec((heads, block, rows), lambda g: (0, at + g, 0)),
            pl.BlockSpec((block, rows), lambda g: (at + g, 0)),
            pl.BlockSpec((block, rows), lambda g: (at + g, 0)),
        ],
        out_specs=pl.BlockSpec((32, 2 * REL2), lambda g: (0, 0)),
        out_shape=jax.ShapeDtypeStruct((32, 2 * REL2), F32),
        scratch_shapes=[pltpu.VMEM((rows // TILE, 32 * block, TILE), F32)],
        compiler_params=pltpu.CompilerParams(vmem_limit_bytes=VMEM),
        cost_estimate=cost(2.5 * count),
        name="table_sums",
    )(first, second, across, upward)


class Place:
    def __init__(self):
        index = lax.axis_index("section")
        self.peers = lax.axis_size("section")
        self.docs = lax.axis_size("dp")
        self.half = index % 2
        self.layer = index // 2
        where = lax.axis_index("dp")
        bits = range(self.docs.bit_length() - 1)
        self.orders = [list(bits), [1, 0] + list(bits)[2:]]
        self.sides = [
            jnp.where(self.half == 0, (where >> one) & 1, (where >> two) & 1)
            for one, two in zip(*self.orders)
        ]

    def across(self, value, mask):
        return lax.ppermute(value, "section", [(i, i ^ mask) for i in range(self.peers)])

    def to_layer(self, value, layer):
        other = 1 - layer
        pairs = [(2 * other + h, 2 * layer + h) for h in range(2)]
        return lax.ppermute(value, "section", pairs)

    def facing(self, value, step):
        pairs = []
        for s in range(self.peers):
            for d in range(self.docs):
                pairs.append((s * self.docs + d, s * self.docs + (d ^ (1 << self.orders[s % 2][step]))))
        return lax.ppermute(value, ("section", "dp"), pairs)

    def joined(self, mine, theirs, side, axis=0):
        return jnp.where(
            side == 0, jnp.concatenate([mine, theirs], axis), jnp.concatenate([theirs, mine], axis)
        )

    def parted(self, value, side):
        rows = value.shape[0] // 2
        return (
            lax.dynamic_slice_in_dim(value, side * rows, rows, 0),
            lax.dynamic_slice_in_dim(value, (1 - side) * rows, rows, 0),
        )


    def over_core(self, value):
        return (value, lambda sent: self.across(sent, 1))

    def over_x(self, value):
        return (value, lambda sent: self.across(sent, 2))

    def over_dp(self, value, step):
        return (value, lambda sent: self.facing(sent, step))

    def weight_flow(self, mine, steps):
        part = mine.shape[0] >> steps
        spot = sum(side << step for step, side in enumerate(self.sides[:steps]))
        mate = self.across(mine, 1)
        got = yield self.over_x(lax.dynamic_slice_in_dim(mine, spot * part, part, 0))
        for step in range(steps):
            got = self.joined(got, (yield self.over_dp(got, step)), self.sides[step])
        return (mine, mate, got, (yield self.over_core(got)))

    def half_flow(self, full):
        keep, send = self.parted(full.astype(BF), self.half)
        return (keep, (yield self.over_core(send)))

    def scatter_flow(self, full):
        size = full.shape[0]
        terms = [(full, 0)]

        def added(offset):
            parts = [lax.dynamic_slice_in_dim(array, at + offset, size, 0) for array, at in terms]
            if len(parts) == 1:
                return parts[0]
            return sum(part.astype(F32) for part in parts).astype(BF)

        for step, side in enumerate(self.sides[:-1]):
            size //= 2
            arrived = yield self.over_dp(added((1 - side) * size), step)
            terms = [(array, at + side * size) for array, at in terms] + [(arrived, 0)]
        return added(0)

    def gather_flow(self, second, first):
        mine = jnp.where(self.layer == 1, second, first)
        sent = yield self.over_x(jnp.where(self.layer == 1, first, second))
        total = (mine.astype(F32) + sent.astype(F32)).astype(BF)
        last = len(self.sides) - 1
        total = (total.astype(F32) + (yield self.over_dp(total, last)).astype(F32)).astype(BF)
        for step, side in reversed(list(enumerate(self.sides[:-1]))):
            total = self.joined(total, (yield self.over_dp(total, step)), side)
        return total.astype(F32)

    def all_flow(self, value):
        value = value + (yield self.over_dp(value, 0))
        value = value + (yield self.over_x(value))
        for step in range(1, len(self.sides)):
            value = value + (yield self.over_dp(value, step))
        return value + (yield self.over_core(value))


class Flow:
    def __init__(self, steps):
        self.steps = steps
        self.air = self.result = None
        self.ready, self.move = next(steps)

    def land(self, arrived):
        self.air = None
        try:
            self.ready, self.move = self.steps.send(arrived)
        except StopIteration as end:
            self.ready = self.move = None
            self.result = end.value

    def go(self):
        self.air, self.ready = self.move(self.ready), None

    @property
    def busy(self):
        return self.air is not None or self.ready is not None


def pace(value, *flows):
    flows = [flow for flow in flows if flow.busy]
    flying = [flow for flow in flows if flow.air is not None]
    value, air = lax.optimization_barrier((value, [flow.air for flow in flying]))
    for flow, arrived in zip(flying, air):
        flow.land(arrived)
    flows = [flow for flow in flows if flow.busy]
    value, ready = lax.optimization_barrier((value, [flow.ready for flow in flows]))
    for flow, sent in zip(flows, ready):
        flow.air, flow.ready = flow.move(sent), None
    return value


def finished(flow):
    while flow.busy:
        pace(0, flow)
    return flow.result


def unpack_kernel(s_ref, hot_ref, vec_ref, wide_ref, bias_ref, tab_ref, line_ref):
    wide = s_ref.shape[3]
    cut = REL1 // 2
    for n in range(2):
        quarters = [s_ref[n, h].astype(F32) for h in range(2)]
        vec_ref[n] = jnp.concatenate([q[:16] for q in quarters], axis=1)
        bias_ref[n] = jnp.zeros(bias_ref.shape[1:], F32)
        for h, q in enumerate(quarters):
            for k in range(4):
                at = (4 * h + k) * wide
                wide_ref[n, :, at : at + wide] = q[5 + k : 6 + k]
            for k in range(2):
                at = (4 * h + k) * wide
                bias_ref[n, :, at : at + wide] = q[k : k + 1]
        rows = [q[16:, :TILE] for q in quarters]
        box = [r[at : at + REL2 // 2] for at in (cut, cut + REL2 // 2) for r in rows]
        fixed = jnp.floor(jnp.transpose(jnp.concatenate(box, axis=0)) * UNIT + 0.5).astype(jnp.int32)
        for p in range(tab_ref.shape[1]):
            tab_ref[n, p] = fixed[2 * p : 2 * p + 1] * 65536 + fixed[2 * p + 1 : 2 * p + 2] + 16384
        line = jnp.concatenate([r[:cut] for r in rows], axis=0).astype(BF)
        lines = dot_tn(line, hot_ref[...]) * UNIT
        for h in range(line_ref.shape[1]):
            for k in range(5):
                part = lines[h : h + 1, 2 * TILE * k : 2 * TILE * (k + 1)]
                line_ref[n, h, k : k + 1, :] = part - (h % 2) * 32768.0


def unpack(quarters, heads):
    wide = quarters.shape[-1]
    hot = jnp.asarray(line_rows().reshape(-1)[None, :] == np.arange(REL1)[:, None], BF)
    shapes = [
        ((2, 16, 2 * wide), F32), ((2, 1, 8 * wide), F32), ((2, 1, 6 * wide), F32),
        ((2, heads // 2, 1, 2 * REL2), jnp.int32), ((2, heads, 8, 2 * TILE), F32),
    ]
    vmem = pl.BlockSpec(memory_space=pltpu.VMEM)
    return pl.pallas_call(
        unpack_kernel,
        in_specs=[vmem, vmem],
        out_specs=[vmem] * len(shapes),
        out_shape=[jax.ShapeDtypeStruct(*s) for s in shapes],
        compiler_params=pltpu.CompilerParams(vmem_limit_bytes=VMEM),
        cost_estimate=cost(8),
        name="unpack",
    )(quarters, hot)


def packed(vectors, tables):
    wide = vectors[1].shape[-1]
    rows = [v.reshape(-1, wide) for v in vectors]
    rows.append(jnp.zeros((4, wide), rows[0].dtype))
    table = jnp.concatenate(tables, axis=0)
    rows.append(jnp.pad(table, ((0, 0), (0, wide - table.shape[1]))))
    return jnp.concatenate(rows, axis=0)


def local(
    section_data,
    text_len,
    patches,
    box_x,
    box_y,
    w_qkv,
    b_qv,
    w_out,
    b_out,
    norm1_gain,
    norm1_bias,
    w_in,
    b_in,
    w_back,
    b_back,
    norm2_gain,
    norm2_bias,
    rel_line,
    rel_x,
    rel_y,
):
    place = Place()
    heads = rel_line.shape[2]
    rows, width = section_data.shape[2:]
    first = place.layer == 0
    where = jnp.stack([place.layer, place.half]).astype(jnp.int32)

    entries = section_data[0]
    wf_qkv = Flow(place.weight_flow(w_qkv[0], 2))
    wf_qkv.go()
    smalls = [v[0] for v in (b_qv, b_out, norm1_gain, norm1_bias, b_in, b_back, norm2_gain, norm2_bias)]
    smalls = packed(smalls, [t[0] for t in (rel_line, rel_x, rel_y)])
    swapped = jnp.where(first, entries[1], entries[0])
    smalls, swapped = lax.optimization_barrier((smalls, swapped))
    theirs = place.across(smalls, 2)
    got = place.across(swapped, 2)
    meta = prepare(where, text_len, patches, box_x, box_y)
    meta, smalls, theirs = pace((meta, smalls, theirs), wf_qkv)
    across, upward, mask, live = meta
    smalls = place.joined(smalls[None], theirs[None], place.layer)
    mates = place.across(smalls, 1)
    w_rest = (w_out, w_in, w_back)
    wf_out, wf_in, wf_back = [Flow(place.weight_flow(w[0], 1)) for w in (w_out, w_in, w_back)]
    smalls, mates, got = pace((smalls, mates, got), wf_qkv, wf_out, wf_in, wf_back)
    smalls = place.joined(smalls[:, None], mates[:, None], place.half, 1)
    params = pace(unpack(smalls, heads), wf_qkv)
    vectors, b_in, b_qv, *scores = params
    source = jnp.where(first, entries[0], got)
    cotangent = jnp.where(first, got, entries[1])
    source, cotangent = pace((source, cotangent), wf_qkv)
    w_qkv = finished(wf_qkv)

    def forward(x, n, paced, *calls):
        qkv, qkv_t = paced(project(where, x, b_qv, w_qkv, n), wf_out)
        mixed = ()
        for part, flows in enumerate(calls):
            mixed = attend(
                qkv, qkv_t, mask, across, upward, scores[0][n], scores[1][n], len(calls), part, mixed
            )
            mixed = paced(mixed, *flows)
        weights, ct, exact, inv = mixed
        sets = [finished(flow) for flow in (wf_out, wf_in, wf_back)]
        n1, s1, hidden, tg, slope, n2, s2, y = feed(where, ct, x, live, vectors, b_in, sets, n)
        return dict(
            x=x, qkv=qkv, qkv_t=qkv_t, weights=weights, ct=ct, exact=exact, inv=inv,
            n1=n1, s1=s1, hidden=hidden, tg=tg, slope=slope, n2=n2, s2=s2, y=y,
        )

    kept = [forward(source, 0, pace, (wf_out, wf_in), (wf_out, wf_in, wf_back))]
    kept.append(forward(kept[0]["y"], 1, lambda value, *flows: value, ()))
    w_out, w_in, w_back = [finished(flow) for flow in (wf_out, wf_in, wf_back)]

    def feed_grads(dy, n):
        k = kept[n]
        return feed_back(
            where, dy, live, vectors, k["n1"], k["s1"], k["n2"], k["s2"], k["slope"], k["inv"],
            (w_back, w_in, w_out), n,
        )

    def scores_back(dc, dct, n):
        k = kept[n]
        return attend_back(k["weights"], k["qkv"], k["qkv_t"], dc, dct, k["exact"])

    def back_grad(df, n):
        return Flow(place.half_flow(dot_tn(kept[n]["tg"], df)))

    def in_grad(du, n):
        return Flow(place.half_flow(dot_tn(kept[n]["hidden"], du)))

    def mixing_grad(dqkv, da, n):
        g_qkv = dot_tn(kept[n]["x"], dqkv).astype(BF)
        g_out = dot(kept[n]["ct"], da).astype(BF)
        return Flow(place.half_flow(jnp.concatenate([g_qkv, g_out], axis=1)))

    def both_terms(flow):
        keep, arrived = finished(flow)
        return (keep.astype(F32) + arrived.astype(F32)).astype(BF)

    def feed_scatter(f_in, f_back):
        g_in, g_back = both_terms(f_in), both_terms(f_back)
        size = g_in.shape[0]
        blocks = [g_back[at : at + size] for at in range(0, g_back.shape[0], size)]
        return Flow(place.scatter_flow(jnp.concatenate([g_in] + blocks, axis=1)))

    def mix_scatter(flow):
        return Flow(place.scatter_flow(both_terms(flow)))

    def vector_rows(sums, wide, qkv):
        return jnp.concatenate([sums, wide.reshape(-1, width), qkv.reshape(-1, width)], axis=0)

    df, du, dr, da, dct, dc, sums, wide = feed_grads(cotangent, 1)
    f_back = back_grad(df, 1)
    du = pace(du, f_back)
    f_in = in_grad(du, 1)
    dc, dct = pace((dc, dct), f_back, f_in)
    dc, dct = pace((dc, dct), f_in)
    f_feed = feed_scatter(f_in, f_back)
    dc, dct = pace((dc, dct), f_feed)
    ds1, dqkv, line1 = scores_back(dc, dct, 1)
    f_mix = mixing_grad(dqkv, da, 1)
    dqkv = pace(dqkv, f_feed, f_mix)
    dx, s_qkv = input_back(where, dqkv, dr, w_qkv, 1)
    vectors1 = vector_rows(sums, wide, s_qkv)

    dx = pace(dx, f_mix)
    f_mix = mix_scatter(f_mix)
    dx = pace(dx, f_mix)
    df, du, dr, da, dct, dc, sums, wide = pace(feed_grads(dx, 0), f_feed, f_mix)
    e_back = back_grad(df, 0)
    du = pace(du, e_back)
    e_in = in_grad(du, 0)
    dc, dct = pace((dc, dct), f_mix, e_back, e_in)
    dc, dct = pace((dc, dct), e_in)
    e_feed = feed_scatter(e_in, e_back)
    dc, dct = pace((dc, dct), e_feed)
    ds0, dqkv, line0 = pace(scores_back(dc, dct, 0), e_feed)
    e_mix = mixing_grad(dqkv, da, 0)
    stores = (ds0, ds1)
    stores, dqkv = pace((stores, dqkv), e_feed, e_mix)
    s_feed = Flow(place.gather_flow(finished(f_feed), finished(e_feed)))
    stores, dqkv = pace((stores, dqkv), s_feed)
    dx, s_qkv = input_back(where, dqkv, dr, w_qkv, 0)
    dx, s_qkv, stores = pace((dx, s_qkv, stores), e_mix)
    e_mix = mix_scatter(e_mix)
    stores = pace(stores, e_mix)

    table = 0.0
    blocks = rows // TABLE_BLOCK

    def tabled(at, count, *flows):
        more = table_sums(*stores, across, upward, at, count)
        return pace((table + more, stores), *flows)

    table, stores = tabled(0, 3, s_feed, e_mix)
    table, stores = tabled(3, 3, e_mix)
    s_mix = Flow(place.gather_flow(finished(f_mix), finished(e_mix)))
    table, stores = pace((table, stores), s_mix)
    table, stores = tabled(6, 3)
    table, stores, dx = pace((table, stores, dx), s_mix)
    sent = place.across(jnp.where(first, kept[1]["y"], dx), 2)
    table, stores = tabled(9, blocks - 9)
    vectors0 = vector_rows(sums, wide, s_qkv)
    hot = jnp.asarray(line_tiles().reshape(-1)[:, None] == np.arange(REL1)[None, :], BF)
    lines = jnp.concatenate([line0, line1], axis=0).reshape(2 * heads, -1).astype(BF)
    lines = jnp.pad(dot(lines, hot), ((0, 32 - 2 * heads), (0, 0)))
    tables = jnp.concatenate([table, lines], axis=1)
    tables = jnp.pad(tables, ((0, 0), (0, width - tables.shape[1])))
    smalls = jnp.concatenate([vectors0, vectors1, tables], axis=0)
    a_small = Flow(place.all_flow(smalls))
    token, sent = pace((dx, sent), a_small)
    token = pace(token, s_feed, s_mix, a_small)
    token = pace(token, a_small)
    token = pace(token, s_feed, s_mix, a_small)
    token = pace(token, a_small)
    token = pace(token, s_mix)
    flows = [s_feed, s_mix, a_small]
    while any(flow.busy for flow in flows):
        token = pace(token, *flows)
    g_feed, g_mix = s_feed.result, s_mix.result
    g_qkv, g_out = g_mix[:, : 3 * width], g_mix[:, 3 * width :]
    ff = du.shape[1]
    g_in = g_feed[:, :ff]
    g_back = jnp.concatenate(
        [g_feed[:, at : at + width] for at in range(ff, g_feed.shape[1], width)], axis=0
    )

    count = vectors0.shape[0]
    v = lax.dynamic_slice_in_dim(a_small.result, place.layer * count, count, 0)
    half_width = width // 2
    v_half = lax.dynamic_slice_in_dim(v, place.half * half_width, half_width, 1)
    v_in = lax.dynamic_slice_in_dim(v, 8 + 2 * place.half, 2, 0).reshape(1, -1)
    v_qv = lax.dynamic_slice_in_dim(v, 12 + 2 * place.half, 1, 0)
    t = lax.dynamic_slice_in_dim(a_small.result, 2 * count + place.layer * heads, heads, 0).T

    def table_half(at, size):
        return lax.dynamic_slice_in_dim(t, at + place.half * size, size, 0)[None]

    t_x, t_y = table_half(0, REL2 // 2), table_half(REL2, REL2 // 2)
    t_line = table_half(2 * REL2, REL1 // 2)
    result = jnp.where(first, jnp.stack([dx, sent]), jnp.stack([sent, kept[1]["y"]]))[None]
    return (
        result, g_qkv[None], v_qv, g_out[None], v_half[0:1], v_half[1:2], v_half[2:3],
        g_in[None], v_in, g_back[None], v_half[3:4], v_half[4:5], v_half[5:6],
        t_line, t_x, t_y,
    )


def solution(mesh):
    matrix = P("section", None, None)
    vector = P("section", None)
    weights = (
        matrix, vector, matrix, vector, vector, vector, matrix, vector, matrix,
        vector, vector, vector, matrix, matrix, matrix,
    )
    data = P("section", "dp", None, None)
    return jax.shard_map(
        local,
        mesh=mesh,
        in_specs=(data, P(None, "dp"), P(None, "dp"), P(None, "dp", None), P(None, "dp", None))
        + weights,
        out_specs=(data,) + weights,
        check_vma=False,
    )
```
